128 devices in a mesh: member: 2 (over core), lat: 8 (over y, x_hi), lon: 8 (over z, x_lo).
Axes of the slice: x: 4 (x_hi: 2, x_lo: 2; x = x_hi * 2 + x_lo), y: 4, z: 4, core: 2. Of those that a mesh axis runs over, the one named last changes fastest.
Arguments:
- features: bfloat16 [4, 192, 128, 1024], P('member', 'lat', None, 'lon'), may hold values from -6 to 6
- cotangent: bfloat16 [4, 192, 128, 1024], P('member', 'lat', None, 'lon'), may hold values from -6 to 6
- basis_table: bfloat16 [192, 4, 3, 33], replicated, may hold values from -1.25 to 1.25
- halo_depth: int32 [192], replicated, may hold values from 1 to 16, as said below
- mix_weight: bfloat16 [128, 4, 128], replicated, may hold values from -0.25 to 0.25
- mix_bias: float32 [128], replicated, may hold values from -3 to 3
- norm_gain: float32 [128], replicated, may hold values from 0.1 to 1.9
- hidden_weight: bfloat16 [256, 128], replicated, may hold values from -0.5 to 0.5
- hidden_bias: float32 [256], replicated, may hold values from -3 to 3
- output_weight: bfloat16 [128, 256], replicated, may hold values from -0.375 to 0.375
Outputs:
- feature_grad: float32 [4, 192, 128, 1024], P('member', 'lat', None, 'lon')
- mix_weight_grad: float32 [128, 4, 128], replicated
- mix_bias_grad: float32 [128], replicated
- norm_gain_grad: float32 [128], replicated
- hidden_weight_grad: float32 [256, 128], replicated
- hidden_bias_grad: float32 [256], replicated
- output_weight_grad: float32 [128, 256], replicated
The draws below stay inside these ranges and needn't reach their ends.
Inputs may be any that keep to these rules, and one draw needn't show every extreme that they name: `halo_depth`: rows 0 and 191 have reach 16; every row with index from 12 to 179 has reach at most 4, and row 12 has exactly 4.
All inputs are finite; a program needn't handle non-finite values.
Results may differ from the reference program's by a relative error of at most 0.0067.
Values may be sent and summed in bfloat16 or wider, within the bound.
No kernel may reach another device: no remote copies, remote signals or barrier semaphores. Data moves between devices by JAX's collectives and lax.ppermute only.
A program may use at most 128 MiB of HBM per device.

```python
import math
import jax
import jax.numpy as jnp
from jax import lax

C = 128
F = 256
K = 4
S = 16
NARROW = 4
POLE = 12
M = 4
H = 192
W = 1024


def draw_halo_depth(key, part):
    key = jax.random.fold_in(key, 7)
    polar_key, inner_key = jax.random.split(key)
    rows = jnp.arange(H, dtype=jnp.int32)
    edge_dist = jnp.minimum(rows, H - 1 - rows)
    longer = jax.random.randint(polar_key, (H,), NARROW + 1, S + 1)
    shorter = jax.random.randint(inner_key, (H,), 1, NARROW + 1)
    depth = jnp.where(edge_dist < POLE, longer, shorter)
    depth = jnp.where(edge_dist == 0, S, depth)
    depth = jnp.where(rows == POLE, NARROW, depth)
    return depth.astype(jnp.int32)


def block_levels(stream_key, extent, pieces, least, top_value):
    level, own = 1.0, jax.random.fold_in(stream_key, 6)
    for axis_at, blocks in pieces:
        heights = jnp.exp(jax.random.uniform(jax.random.fold_in(own, axis_at), (blocks,), jnp.float32, least / len(pieces), top_value / len(pieces)))
        level = level * jnp.repeat(heights, extent[axis_at] // blocks).reshape([-1 if axis == axis_at else 1 for axis in range(len(extent))])
    return level


def scatter_about(rng, dims, spread, bound, cuts=(), held_as=jnp.bfloat16):
    level = block_levels(rng, dims, cuts, -0.22, 0.18) if cuts else 1.0
    values = jax.random.normal(rng, dims, jnp.float32) * spread * level
    return jnp.minimum(jnp.maximum(values, -bound), bound).astype(held_as)


def setup_inputs(seed: int = 0) -> dict:
    streams_of = jax.random.split(jax.random.key(seed), 11)
    features = scatter_about(streams_of[0], (M, H, C, W), 1.0, 6.0, ((0, 2), (1, 8), (3, 8)))
    cotangent = scatter_about(streams_of[1], (M, H, C, W), 1.0, 6.0, ((0, 2), (1, 8), (3, 8)))
    basis_table = scatter_about(streams_of[2], (H, K, 3, 2 * S + 1), (3 * (2 * NARROW + 1)) ** -0.5, 1.25)
    halo_depth = draw_halo_depth(jax.random.fold_in(streams_of[10], 71), 0)
    mix_weight = scatter_about(streams_of[4], (C, K, C), (K * C) ** -0.5, 0.25)
    mix_bias = scatter_about(streams_of[5], (C,), 0.5, 3.0, (), jnp.float32)
    norm_gain = jnp.clip(1.0 + 0.18 * jax.random.normal(streams_of[6], (C,), jnp.float32), 0.1, 1.9)
    hidden_weight = scatter_about(streams_of[7], (F, C), C ** -0.5, 0.5)
    hidden_bias = scatter_about(streams_of[8], (F,), 0.5, 3.0, (), jnp.float32)
    output_weight = scatter_about(streams_of[9], (C, F), F ** -0.5, 0.375)
    return dict(features=features, cotangent=cotangent, basis_table=basis_table, halo_depth=halo_depth, mix_weight=mix_weight, mix_bias=mix_bias, norm_gain=norm_gain, hidden_weight=hidden_weight, hidden_bias=hidden_bias, output_weight=output_weight)


EPSILON = 1e-05
HIGHEST_PRECISION = lax.Precision.HIGHEST

def rounded(value):
    return lax.optimization_barrier(value.astype(jnp.bfloat16)).astype(jnp.float32)

def masked_table(basis_table, halo_depth):
    filter_len = basis_table.shape[-1]
    reach_cols = (filter_len - 1) // 2
    offsets = jnp.abs(jnp.arange(filter_len, dtype=jnp.int32) - reach_cols)
    keep = offsets[None, :] <= halo_depth.astype(jnp.int32)[:, None]
    kept = jnp.where(keep[:, None, None, :], basis_table, jnp.zeros_like(basis_table))
    return kept.astype(jnp.float32)

def band_filter(member, row_table):
    reach_cols = (row_table.shape[-1] - 1) // 2
    row_total = member.shape[0]
    padded = jnp.pad(member, ((1, 1), (0, 0), (0, 0)))
    banded = jnp.stack([padded[b:b + row_total] for b in range(3)], axis=1)
    banded = jnp.concatenate([banded[..., -reach_cols:], banded, banded[..., :reach_cols]], axis=-1)

    def one_row(paired):
        row_bands, row_filter = paired
        inputs = jnp.transpose(row_bands, (1, 0, 2))
        result = lax.conv_general_dilated(inputs, row_filter, (1,), 'VALID', dimension_numbers=('NCH', 'OIH', 'NCH'), precision=HIGHEST_PRECISION)
        return jnp.transpose(result, (1, 0, 2))
    return lax.map(one_row, (banded, row_table))

def einsum_high(form, left, right):
    return jnp.einsum(form, left, right, precision=HIGHEST_PRECISION)

def member_grads(member, cot_member, row_table, mix_weight, mix_bias, norm_gain, hidden_weight, hidden_bias, output_weight):
    features_wide = member.astype(jnp.float32)
    filtered, filter_back = jax.vjp(lambda value: band_filter(value, row_table), features_wide)
    filtered = rounded(filtered)
    mixed = einsum_high('okc,hkcw->how', mix_weight, filtered) + mix_bias[None, :, None]
    inverse_rms = lax.rsqrt(lax.optimization_barrier(jnp.mean(mixed * mixed, axis=1, keepdims=True)) + EPSILON)
    scaled = mixed * inverse_rms
    normed = rounded(scaled * norm_gain[None, :, None])
    hidden_pre = einsum_high('fc,hcw->hfw', hidden_weight, normed) + hidden_bias[None, :, None]
    activated, gelu_back = jax.vjp(jax.nn.gelu, hidden_pre)
    activated = rounded(activated)
    cot_wide = cot_member.astype(jnp.float32)
    output_grad = einsum_high('hcw,hfw->cf', cot_wide, activated)
    activated_grad = einsum_high('cf,hcw->hfw', output_weight, cot_wide)
    pre_grad = gelu_back(activated_grad)[0]
    pre_round = rounded(pre_grad)
    hidden_grad = einsum_high('hfw,hcw->fc', pre_round, normed)
    hidden_bias_grad = lax.optimization_barrier(jnp.sum(pre_grad, axis=(0, 2)))
    normed_grad = einsum_high('fc,hfw->hcw', hidden_weight, pre_round)
    gain_grad = lax.optimization_barrier(jnp.sum(normed_grad * scaled, axis=(0, 2)))
    scaled_grad = normed_grad * norm_gain[None, :, None]
    mixed_grad = inverse_rms * (scaled_grad - scaled * lax.optimization_barrier(jnp.mean(scaled_grad * scaled, axis=1, keepdims=True)))
    bias_grad = lax.optimization_barrier(jnp.sum(mixed_grad, axis=(0, 2)))
    mixed_round = rounded(mixed_grad)
    mix_grad = einsum_high('how,hkcw->okc', mixed_round, filtered)
    filtered_grad = rounded(einsum_high('okc,how->hkcw', mix_weight, mixed_round))
    feature_grad = cot_wide + filter_back(filtered_grad)[0]
    return (feature_grad, (mix_grad, bias_grad, gain_grad, hidden_grad, hidden_bias_grad, output_grad))

def reference(features, cotangent, basis_table, halo_depth, mix_weight, mix_bias, norm_gain, hidden_weight, hidden_bias, output_weight):
    row_table = masked_table(basis_table, halo_depth)
    mix_wide = mix_weight.astype(jnp.float32)
    hidden_wide = hidden_weight.astype(jnp.float32)
    output_wide = output_weight.astype(jnp.float32)
    bias_wide = mix_bias.astype(jnp.float32)
    gain_wide = norm_gain.astype(jnp.float32)
    hidden_bias_wide = hidden_bias.astype(jnp.float32)

    def one_member(paired):
        return member_grads(paired[0], paired[1], row_table, mix_wide, bias_wide, gain_wide, hidden_wide, hidden_bias_wide, output_wide)
    feature_grad, grads = lax.map(one_member, (features, cotangent))
    grad_scale = 1.0 / math.sqrt(M * H * W)
    summed = tuple((lax.optimization_barrier(jnp.sum(single, axis=0)) * grad_scale for single in grads))
    return (feature_grad, summed[0], summed[1], summed[2], summed[3], summed[4], summed[5])
```

```python
import functools
import math

import jax
import jax.numpy as jnp
from jax import lax
from jax.experimental import pallas as pl
from jax.experimental.pallas import tpu as pltpu
from jax.sharding import PartitionSpec as P

EPSILON = 1e-05
BF = jnp.bfloat16
F32 = jnp.float32
GELU_A = math.sqrt(2.0 / math.pi)
GELU_B = 0.044715
ROWS = 24
STEP_ROWS = 2


def nn(a, b):
    return lax.dot_general(a, b, (((1,), (0,)), ((), ())), preferred_element_type=F32)


def nt(a, b):
    return lax.dot_general(a, b, (((1,), (1,)), ((), ())), preferred_element_type=F32)


def build_filter(taps_ref, row, matrix_ref, slot):
    lanes = lax.broadcasted_iota(jnp.int32, (16, 128), 1)
    low = lanes < 64
    for b in range(3):
        for k in range(4):
            base = taps_ref[row, pl.ds(b * 4 + k, 1), :]
            ring = pltpu.roll(
                jnp.broadcast_to(base, (128, 128)), 0, 1, stride=1, stride_axis=0
            )
            first, last = ring[:16], ring[112:]
            zero = jnp.zeros_like(first)
            own = jnp.concatenate(
                [jnp.where(low, first, zero), ring[16:112], jnp.where(low, zero, last)], axis=0
            )
            halo = jnp.concatenate(
                [jnp.where(low, last, zero), jnp.where(low, zero, first)], axis=0
            )
            cols = pl.ds(k * 128, 128)
            matrix_ref[slot, pl.ds(b * 128, 128), cols] = own.astype(BF)
            matrix_ref[slot, pl.ds(384 + b * 32, 32), cols] = halo.astype(BF)


def forward_kernel(
    me_ref,
    taps_ref,
    feats_ref,
    top_ref,
    bottom_ref,
    sides_ref,
    sides_top_ref,
    sides_bottom_ref,
    cot_ref,
    mix_ref,
    mix_bias_ref,
    gain_ref,
    hidden_ref,
    hidden_bias_ref,
    hidden_t_ref,
    output_t_ref,
    mixed_round_ref,
    keep_ref,
    send_ref,
    grown,
    grown_sides,
    matrix,
    mix_acc,
    out_acc,
    hid_acc,
    mix_bias_acc,
    gain_acc,
    hidden_bias_acc,
    packed,
    *,
    scale,
):
    step = pl.program_id(0)

    @pl.when(step == 0)
    def _():
        for m in range(2):
            grown[m, 0] = top_ref[m]
            grown[m, ROWS + 1] = bottom_ref[m]
            grown_sides[m, 0] = sides_top_ref[m]
            grown_sides[m, ROWS + 1] = sides_bottom_ref[m]
        grown[:, 1 : ROWS + 1] = feats_ref[...]
        grown_sides[:, 1 : ROWS + 1] = sides_ref[...]
        matrix[...] = jnp.zeros_like(matrix)
        for acc in (mix_acc, out_acc, hid_acc, mix_bias_acc, gain_acc, hidden_bias_acc):
            acc[...] = jnp.zeros_like(acc)

    first_row = step * STEP_ROWS
    cells = []
    for at in range(STEP_ROWS):
        build_filter(taps_ref, at, matrix, at)
    for at in range(STEP_ROWS):
        row = first_row + at
        inputs = []
        for m in range(2):
            sides = jnp.concatenate(
                [grown_sides[m, pl.ds(row, 3)].reshape(96, 128), jnp.zeros((32, 128), BF)], axis=0
            )
            inputs.append(
                jnp.concatenate(
                    [grown[m, row], grown[m, row + 1], grown[m, row + 2], sides.T], axis=1
                )
            )
        filtered = nn(jnp.concatenate(inputs, axis=0), matrix[at]).astype(BF)
        for m in range(2):
            cells.append(
                jnp.concatenate(
                    [
                        filtered[m * 128 : m * 128 + 128, k * 128 : k * 128 + 128]
                        for k in range(4)
                    ],
                    axis=0,
                )
            )
    filtered = jnp.concatenate(cells, axis=1)
    blocks = 2 * STEP_ROWS
    wide = lambda ref: jnp.concatenate([ref[...]] * blocks, axis=1)
    fold = lambda v: functools.reduce(
        lambda a, b: a + b, [v[:, n * 128 : n * 128 + 128] for n in range(blocks)]
    )
    mixed = nn(mix_ref[...], filtered) + wide(mix_bias_ref)
    inverse = lax.rsqrt(jnp.mean(mixed * mixed, axis=0, keepdims=True) + EPSILON)
    scaled = mixed * inverse
    gain = wide(gain_ref)
    normed = (scaled * gain).astype(BF)
    hidden = nn(hidden_ref[...], normed) + wide(hidden_bias_ref)
    square = hidden * hidden
    tanh = jnp.tanh(hidden * (GELU_A + (GELU_A * GELU_B) * square))
    half = 0.5 + 0.5 * tanh
    activated = (hidden * half).astype(BF)
    slope = half + (0.5 * hidden) * (1.0 - tanh * tanh) * (
        GELU_A + (3.0 * GELU_A * GELU_B) * square
    )
    cot = jnp.concatenate(
        [cot_ref[m, at] for at in range(STEP_ROWS) for m in range(2)], axis=1
    )
    pre_grad = slope * nn(output_t_ref[...], cot)
    pre_round = pre_grad.astype(BF)
    out_acc[...] += nt(cot, activated)
    hid_acc[...] += nt(pre_round, normed)
    hidden_bias_acc[...] += fold(pre_grad)
    normed_grad = nn(hidden_t_ref[...], pre_round)
    gain_acc[...] += fold(normed_grad * scaled)
    grad = normed_grad * gain
    mixed_grad = inverse * (grad - scaled * jnp.mean(grad * scaled, axis=0, keepdims=True))
    mix_bias_acc[...] += fold(mixed_grad)
    mixed_round = mixed_grad.astype(BF)
    mix_acc[...] += nt(mixed_round, filtered)
    for at in range(STEP_ROWS):
        mixed_round_ref[at] = mixed_round[:, at * 256 : at * 256 + 256]

    @pl.when(step == pl.num_programs(0) - 1)
    def _():
        for k in range(4):
            packed[pl.ds(k, 128, stride=4), :] = mix_acc[:, k * 128 : k * 128 + 128] * scale
        packed[512:768] = hid_acc[...] * scale
        for f in range(2):
            packed[768 + f * 128 : 896 + f * 128] = out_acc[:, f * 128 : f * 128 + 128] * scale
        mine = me_ref[0]
        keep_ref[0:512] = packed[pl.ds(pl.multiple_of(mine * 512, 512), 512), :]
        send_ref[0:512] = packed[pl.ds(pl.multiple_of(512 - mine * 512, 512), 512), :]
        rows = [
            jnp.sum(v.T, axis=0, keepdims=True)
            for v in (
                mix_bias_acc[...],
                gain_acc[...],
                hidden_bias_acc[0:128],
                hidden_bias_acc[128:256],
            )
        ]
        small = jnp.concatenate(rows + [jnp.zeros((4, 128), F32)], axis=0) * scale
        keep_ref[512:520] = small
        send_ref[512:520] = small


def forward(me, taps, feats, top, bottom, sides, sides_top, sides_bottom, cot, weights, scale):
    whole = lambda v: pl.BlockSpec(v.shape, lambda i: (0,) * v.ndim)
    ins = [taps, feats, top, bottom, sides, sides_top, sides_bottom, cot, *weights]
    specs = [whole(v) for v in ins]
    specs[0] = pl.BlockSpec((STEP_ROWS, 12, 128), lambda i: (i, 0, 0))
    specs[7] = pl.BlockSpec((2, STEP_ROWS, 128, 128), lambda i: (0, i, 0, 0))
    return pl.pallas_call(
        functools.partial(forward_kernel, scale=scale),
        grid=(ROWS // STEP_ROWS,),
        in_specs=[pl.BlockSpec(memory_space=pltpu.SMEM)] + specs,
        out_specs=[
            pl.BlockSpec((STEP_ROWS, 128, 256), lambda i: (i, 0, 0)),
            pl.BlockSpec((520, 128), lambda i: (0, 0)),
            pl.BlockSpec((520, 128), lambda i: (0, 0)),
        ],
        out_shape=[
            jax.ShapeDtypeStruct((ROWS, 128, 256), BF),
            jax.ShapeDtypeStruct((520, 128), F32),
            jax.ShapeDtypeStruct((520, 128), F32),
        ],
        scratch_shapes=[
            pltpu.VMEM((2, ROWS + 2, 128, 128), BF),
            pltpu.VMEM((2, ROWS + 2, 32, 128), BF),
            pltpu.VMEM((STEP_ROWS, 512, 512), BF),
            pltpu.VMEM((128, 512), F32),
            pltpu.VMEM((128, 256), F32),
            pltpu.VMEM((256, 128), F32),
            pltpu.VMEM((128, 128), F32),
            pltpu.VMEM((128, 128), F32),
            pltpu.VMEM((256, 128), F32),
            pltpu.VMEM((1024, 128), F32),
        ],
        compiler_params=pltpu.CompilerParams(vmem_limit_bytes=40 * 1024 * 1024),
        cost_estimate=pl.CostEstimate(
            flops=15_000_000_000, bytes_accessed=8_000_000, transcendentals=1_600_000
        ),
    )(me, *ins)


def backward_kernel(
    taps_ref,
    mixed_round_ref,
    mix_t_ref,
    cot_ref,
    part_ref,
    edge_top_ref,
    edge_bottom_ref,
    sides_ref,
    acc,
    sides_acc,
    matrix,
):
    step = pl.program_id(0)

    @pl.when(step == 0)
    def _():
        acc[...] = jnp.zeros_like(acc)
        sides_acc[...] = jnp.zeros_like(sides_acc)
        matrix[...] = jnp.zeros_like(matrix)

    first_row = step * STEP_ROWS
    for at in range(STEP_ROWS):
        build_filter(taps_ref, at, matrix, at)
    for at in range(STEP_ROWS):
        row = first_row + at
        grads = nn(mix_t_ref[...], mixed_round_ref[at]).astype(BF)
        for m in range(2):
            arranged = jnp.concatenate(
                [
                    grads[k * 128 : k * 128 + 128, m * 128 : m * 128 + 128]
                    for k in range(4)
                ],
                axis=1,
            )
            spread = nt(arranged, matrix[at])
            for b in range(3):
                acc[m, row + b] += spread[:, b * 128 : b * 128 + 128]
            turned = spread[:, 384:512].T
            for b in range(3):
                sides_acc[m, row + b] += turned[b * 32 : b * 32 + 32]

    @pl.when(step == pl.num_programs(0) - 1)
    def _():
        part_ref[...] = acc[:, 1 : ROWS + 1] + cot_ref[...].astype(F32)
        sides_ref[...] = sides_acc[:, 1 : ROWS + 1].astype(BF)
        for m in range(2):
            for edge_ref, at in ((edge_top_ref, 0), (edge_bottom_ref, ROWS + 1)):
                edge_ref[m, 0:128] = acc[m, at].astype(BF)
                edge_ref[m, 128:160] = sides_acc[m, at].astype(BF)


def backward(taps, mixed_round, mix_t, cot):
    return pl.pallas_call(
        backward_kernel,
        grid=(ROWS // STEP_ROWS,),
        in_specs=[
            pl.BlockSpec((STEP_ROWS, 12, 128), lambda i: (i, 0, 0)),
            pl.BlockSpec((STEP_ROWS, 128, 256), lambda i: (i, 0, 0)),
            pl.BlockSpec((512, 128), lambda i: (0, 0)),
            pl.BlockSpec((2, ROWS, 128, 128), lambda i: (0, 0, 0, 0)),
        ],
        out_specs=[
            pl.BlockSpec((2, ROWS, 128, 128), lambda i: (0, 0, 0, 0)),
            pl.BlockSpec((2, 160, 128), lambda i: (0, 0, 0)),
            pl.BlockSpec((2, 160, 128), lambda i: (0, 0, 0)),
            pl.BlockSpec((2, ROWS, 32, 128), lambda i: (0, 0, 0, 0)),
        ],
        out_shape=[
            jax.ShapeDtypeStruct((2, ROWS, 128, 128), F32),
            jax.ShapeDtypeStruct((2, 160, 128), BF),
            jax.ShapeDtypeStruct((2, 160, 128), BF),
            jax.ShapeDtypeStruct((2, ROWS, 32, 128), BF),
        ],
        scratch_shapes=[
            pltpu.VMEM((2, ROWS + 2, 128, 128), F32),
            pltpu.VMEM((2, ROWS + 2, 32, 128), F32),
            pltpu.VMEM((STEP_ROWS, 512, 512), BF),
        ],
        compiler_params=pltpu.CompilerParams(vmem_limit_bytes=40 * 1024 * 1024),
        cost_estimate=pl.CostEstimate(
            flops=7_500_000_000, bytes_accessed=8_000_000, transcendentals=0
        ),
    )(taps, mixed_round, mix_t, cot)


BORDER_ROWS = 4


def border_kernel(part_ref, left_ref, right_ref, above_ref, below_ref, out_ref):
    step = pl.program_id(0)
    gap = jnp.zeros((96, 128), BF)
    for m in range(2):
        for at in range(BORDER_ROWS):
            border = jnp.concatenate([left_ref[m, at], gap, right_ref[m, at]], axis=0).T
            out_ref[m, at] = part_ref[m, at] + border.astype(F32)

    @pl.when(step == 0)
    def _():
        out_ref[:, 0] += above_ref[...].astype(F32)

    @pl.when(step == pl.num_programs(0) - 1)
    def _():
        out_ref[:, BORDER_ROWS - 1] += below_ref[...].astype(F32)


def add_border(part, left, right, above, below):
    rows = lambda *tail: pl.BlockSpec((2, BORDER_ROWS, *tail), lambda i: (0, i, 0, 0))
    edge = pl.BlockSpec((2, 128, 128), lambda i: (0, 0, 0))
    return pl.pallas_call(
        border_kernel,
        grid=(ROWS // BORDER_ROWS,),
        in_specs=[rows(128, 128), rows(16, 128), rows(16, 128), edge, edge],
        out_specs=rows(128, 128),
        out_shape=jax.ShapeDtypeStruct((2, ROWS, 128, 128), F32),
        compiler_params=pltpu.CompilerParams(vmem_limit_bytes=24 * 1024 * 1024),
        cost_estimate=pl.CostEstimate(flops=1_000_000, bytes_accessed=7_000_000, transcendentals=0),
    )(part, left, right, above, below)


def ring(axis, shift, periodic):
    count = lax.axis_size(axis)
    pairs = [(i, i + shift) for i in range(count)]
    if periodic:
        return [(a, b % count) for a, b in pairs]
    return [(a, b) for a, b in pairs if 0 <= b < count]


def ring_taps(basis_table, halo_depth):
    place = lax.axis_index("lat") * ROWS
    chosen = lax.dynamic_slice_in_dim(basis_table, place, ROWS, 0)
    limits = lax.dynamic_slice_in_dim(halo_depth, place, ROWS, 0)
    offsets = jnp.abs(jnp.arange(33, dtype=jnp.int32) - 16)
    keep = offsets[None, :] <= limits[:, None]
    kept = jnp.where(keep[:, None, None, :], chosen, jnp.zeros_like(chosen)).astype(F32)
    flipped = kept.transpose(0, 2, 1, 3).reshape(ROWS, 12, 33)[..., ::-1]
    return jnp.concatenate(
        [flipped[..., 16:], jnp.zeros((ROWS, 12, 95), F32), flipped[..., :16]], axis=-1
    )


def on_device(
    features,
    cotangent,
    basis_table,
    halo_depth,
    mix_weight,
    mix_bias,
    norm_gain,
    hidden_weight,
    hidden_bias,
    output_weight,
):
    top = lax.ppermute(features[:, ROWS - 1], "lat", ring("lat", 1, False))
    bottom = lax.ppermute(features[:, 0], "lat", ring("lat", -1, False))
    left = lax.ppermute(
        features[..., 112:].transpose(0, 1, 3, 2), "lon", ring("lon", 1, True)
    )
    right = lax.ppermute(
        features[..., :16].transpose(0, 1, 3, 2), "lon", ring("lon", -1, True)
    )
    sides = jnp.concatenate([left, right], axis=2)
    sides_top = lax.ppermute(sides[:, ROWS - 1], "lat", ring("lat", 1, False))
    sides_bottom = lax.ppermute(sides[:, 0], "lat", ring("lat", -1, False))

    taps = ring_taps(basis_table, halo_depth)
    mix = mix_weight.reshape(128, 512)
    column = lambda v: jnp.broadcast_to(v[:, None], (v.shape[0], 128))
    weights = (
        mix,
        column(mix_bias),
        column(norm_gain),
        hidden_weight,
        column(hidden_bias),
        hidden_weight.T,
        output_weight.T,
    )
    member = lax.axis_index("member")
    cell_total = 2 * ROWS * 128 * lax.axis_size(("member", "lat", "lon"))
    mixed_round, keep, send = forward(
        member.reshape(1).astype(jnp.int32),
        taps,
        features,
        top,
        bottom,
        sides,
        sides_top,
        sides_bottom,
        cotangent,
        weights,
        1.0 / math.sqrt(cell_total),
    )
    swap = [(0, 1), (1, 0)]
    got = lax.ppermute(send, "member", swap)
    part, edge_top, edge_bottom, out_sides = backward(taps, mixed_round, mix.T, cotangent)

    below = lax.ppermute(edge_top, "lat", ring("lat", -1, False))
    above = lax.ppermute(edge_bottom, "lat", ring("lat", 1, False))

    pair = (keep + got).reshape(65, 8, 128)
    lats, lons = lax.axis_size("lat"), lax.axis_size("lon")
    each = 64 // lats
    own = each // lons
    small = jnp.broadcast_to(pair[None, 64:], (lats, 1, 8, 128))
    to_lat = jnp.concatenate([pair[:64].reshape(lats, each, 8, 128), small], axis=1)
    from_lat = jnp.sum(lax.all_to_all(to_lat, "lat", 0, 0), axis=0)

    out_sides = jnp.concatenate(
        [
            out_sides[:, :1] + above[:, None, 128:],
            out_sides[:, 1 : ROWS - 1],
            out_sides[:, ROWS - 1 :] + below[:, None, 128:],
        ],
        axis=1,
    )
    add_left = lax.ppermute(out_sides[:, :, 16:], "lon", ring("lon", 1, True))
    add_right = lax.ppermute(out_sides[:, :, :16], "lon", ring("lon", -1, True))

    small = jnp.broadcast_to(from_lat[None, each:], (lons, 1, 8, 128))
    to_lon = jnp.concatenate([from_lat[:each].reshape(lons, own, 8, 128), small], axis=1)
    from_lon = jnp.sum(lax.all_to_all(to_lon, "lon", 0, 0), axis=0)
    summed = jnp.broadcast_to(from_lon[None, :own], (lons, own, 8, 128))
    summed = lax.all_to_all(summed, "lon", 0, 0).reshape(each, 8, 128)
    summed = lax.all_to_all(jnp.broadcast_to(summed[None], (lats, each, 8, 128)), "lat", 0, 0)
    summed = summed.reshape(512, 128)
    other = lax.ppermute(summed, "member", swap)
    feature_grad = add_border(part, add_left, add_right, above[:, :128], below[:, :128])

    mine = member == 0
    mix_grad = jnp.where(mine, summed, other).reshape(128, 4, 128)
    rest = jnp.where(mine, other, summed)
    output_grad = jnp.concatenate([rest[256:384], rest[384:512]], axis=1)
    small = from_lon[own]
    return (
        feature_grad,
        mix_grad,
        small[0],
        small[1],
        rest[:256],
        small[2:4].reshape(256),
        output_grad,
    )


def solution(mesh):
    cells = P("member", "lat", None, "lon")
    return jax.shard_map(
        on_device,
        mesh=mesh,
        in_specs=(cells, cells) + (P(),) * 8,
        out_specs=(cells,) + (P(),) * 6,
        check_vma=False,
    )
```

```python
import functools
import math

import jax
import jax.numpy as jnp
from jax import lax
from jax.experimental import pallas as pl
from jax.experimental.pallas import tpu as pltpu
from jax.sharding import PartitionSpec as P

EPSILON = 1e-05
BF = jnp.bfloat16
F32 = jnp.float32
GELU_A = math.sqrt(2.0 / math.pi)
GELU_B = 0.044715
ROWS = 24
STEP_ROWS = 2
SIDE_ROWS = 8
STEPS = ROWS // STEP_ROWS


def nn(a, b):
    return lax.dot_general(a, b, (((1,), (0,)), ((), ())), preferred_element_type=F32)


def nt(a, b):
    return lax.dot_general(a, b, (((1,), (1,)), ((), ())), preferred_element_type=F32)


def build_filter(taps_ref, row, matrix_ref, slot):
    lanes = lax.broadcasted_iota(jnp.int32, (16, 128), 1)
    low = lanes < 64
    zero = jnp.zeros((16, 128), BF)
    for b in range(3):
        for k in range(4):
            base = taps_ref[row, pl.ds(b * 4 + k, 1), :]
            head = pltpu.roll(
                jnp.broadcast_to(base, (16, 128)), 0, 1, stride=1, stride_axis=0
            ).astype(BF)
            ring = [head] + [pltpu.roll(head, 16 * g, 1) for g in range(1, 8)]
            cols = pl.ds(k * 128, 128)
            own = pl.ds(b * 128, 128)
            matrix_ref[slot, own, cols] = jnp.concatenate(
                [jnp.where(low, head, zero), *ring[1:7], jnp.where(low, zero, ring[7])], axis=0
            )
            matrix_ref[slot, pl.ds(384 + b * 32, 32), cols] = jnp.concatenate(
                [jnp.where(low, ring[7], zero), jnp.where(low, zero, head)], axis=0
            )


def sides_kernel(feats_ref, to_right_ref, to_left_ref):
    spot = lax.broadcasted_iota(jnp.int32, (32, 128), 0)
    spot = jnp.where(spot < 16, spot, spot + 96)
    pick = (lax.broadcasted_iota(jnp.int32, (32, 128), 1) == spot).astype(BF)
    for at in range(SIDE_ROWS):
        both = jnp.concatenate([feats_ref[0, at], feats_ref[1, at]], axis=0)
        turned = nt(pick, both).astype(BF)
        for m in range(2):
            to_left_ref[m, at] = turned[:16, m * 128 : m * 128 + 128]
            to_right_ref[m, at] = turned[16:, m * 128 : m * 128 + 128]


def sides_of(feats):
    rows = lambda *tail: pl.BlockSpec((2, SIDE_ROWS, *tail), lambda i: (0, i, 0, 0))
    side = jax.ShapeDtypeStruct((2, ROWS, 16, 128), BF)
    return pl.pallas_call(
        sides_kernel,
        grid=(ROWS // SIDE_ROWS,),
        in_specs=[rows(128, 128)],
        out_specs=[rows(16, 128)] * 2,
        out_shape=[side, side],
        compiler_params=pltpu.CompilerParams(vmem_limit_bytes=24 * 1024 * 1024),
        cost_estimate=pl.CostEstimate(flops=50_000_000, bytes_accessed=2_000_000, transcendentals=0),
    )(feats)


def weights_kernel(
    mix_ref, bias_ref, gain_ref, hidden_ref, hidden_bias_ref, output_ref,
    wide_ref, tall_ref, hidden_t_ref, output_t_ref, columns_ref,
):
    mix = jnp.concatenate([mix_ref[:, k, :] for k in range(4)], axis=1)
    wide_ref[...] = mix
    tall_ref[...] = mix.T
    hidden_t_ref[...] = hidden_ref[...].T
    output_t_ref[...] = output_ref[...].T
    for at, (ref, low) in enumerate(
        ((bias_ref, 0), (gain_ref, 0), (hidden_bias_ref, 0), (hidden_bias_ref, 128))
    ):
        line = jnp.broadcast_to(ref[:, low : low + 128], (128, 128))
        columns_ref[at * 128 : at * 128 + 128] = line.T


def prepare_weights(mix, bias, gain, hidden, hidden_bias, output):
    return pl.pallas_call(
        weights_kernel,
        out_shape=[
            jax.ShapeDtypeStruct((128, 512), BF),
            jax.ShapeDtypeStruct((512, 128), BF),
            jax.ShapeDtypeStruct((128, 256), BF),
            jax.ShapeDtypeStruct((256, 128), BF),
            jax.ShapeDtypeStruct((512, 128), F32),
        ],
        compiler_params=pltpu.CompilerParams(vmem_limit_bytes=24 * 1024 * 1024),
        cost_estimate=pl.CostEstimate(flops=1_000_000, bytes_accessed=1_500_000, transcendentals=0),
    )(mix, bias[None], gain[None], hidden, hidden_bias[None], output)


def forward_kernel(
    me_ref,
    taps_ref,
    feats_ref,
    next_feats_ref,
    cot_ref,
    next_cot_ref,
    left_ref,
    right_ref,
    below_ref,
    mix_ref,
    columns_ref,
    hidden_ref,
    hidden_t_ref,
    output_t_ref,
    mixed_round_ref,
    keep_ref,
    send_ref,
    sides,
    after,
    after_cot,
    matrix,
    mix_acc,
    out_acc,
    hid_acc,
    mix_bias_acc,
    gain_acc,
    hidden_bias_acc,
    packed,
    *,
    scale,
):
    step = pl.program_id(0)
    last = step == STEPS - 1

    @pl.when(step == 0)
    def _():
        for m in range(2):
            sides[m, 0:ROWS, 0:16] = left_ref[m]
            sides[m, 0:ROWS, 16:32] = right_ref[m]
            for at in range(2):
                sides[m, ROWS + at, 0:16] = below_ref[m, 256 + at * 16 : 272 + at * 16]
                sides[m, ROWS + at, 16:32] = below_ref[m, 288 + at * 16 : 304 + at * 16]
        matrix[...] = jnp.zeros_like(matrix)
        for acc in (mix_acc, out_acc, hid_acc, mix_bias_acc, gain_acc, hidden_bias_acc):
            acc[...] = jnp.zeros_like(acc)

    @pl.when(last)
    def _():
        for m in range(2):
            after[m, 0] = below_ref[m, 0:128]
            after[m, 1] = below_ref[m, 128:256]
            after_cot[m] = below_ref[m, 320:448]

    @pl.when(jnp.logical_not(last))
    def _():
        after[...] = next_feats_ref[...]
        after_cot[...] = next_cot_ref[:, 0]

    cells = []
    for at in range(STEP_ROWS):
        build_filter(taps_ref, at, matrix, at)
    for at in range(STEP_ROWS):
        row = step * STEP_ROWS + at
        inputs = []
        for m in range(2):
            halo = jnp.concatenate(
                [sides[m, pl.ds(row, 3)].reshape(96, 128), jnp.zeros((32, 128), BF)], axis=0
            )
            band = [feats_ref[m, 0], feats_ref[m, 1], after[m, 0], after[m, 1]][at : at + 3]
            inputs.append(jnp.concatenate([*band, halo.T], axis=1))
        filtered = nn(jnp.concatenate(inputs, axis=0), matrix[at]).astype(BF)
        for m in range(2):
            cells.append(
                jnp.concatenate(
                    [
                        filtered[m * 128 : m * 128 + 128, k * 128 : k * 128 + 128]
                        for k in range(4)
                    ],
                    axis=0,
                )
            )
    filtered = jnp.concatenate(cells, axis=1)
    blocks = 2 * STEP_ROWS
    wide = lambda low, high: jnp.concatenate([columns_ref[low:high]] * blocks, axis=1)
    fold = lambda v: functools.reduce(
        lambda a, b: a + b, [v[:, n * 128 : n * 128 + 128] for n in range(blocks)]
    )
    mixed = nn(mix_ref[...], filtered) + wide(0, 128)
    inverse = lax.rsqrt(jnp.mean(mixed * mixed, axis=0, keepdims=True) + EPSILON)
    scaled = mixed * inverse
    gain = wide(128, 256)
    normed = (scaled * gain).astype(BF)
    hidden = nn(hidden_ref[...], normed) + wide(256, 512)
    square = hidden * hidden
    tanh = jnp.tanh(hidden * (GELU_A + (GELU_A * GELU_B) * square))
    half = 0.5 + 0.5 * tanh
    value = hidden * half
    activated = value.astype(BF)
    slope = half + value * (1.0 - half) * (2.0 * GELU_A + (6.0 * GELU_A * GELU_B) * square)
    cot = jnp.concatenate(
        [cot_ref[0, 0], cot_ref[1, 0], after_cot[0], after_cot[1]], axis=1
    )
    pre_grad = slope * nn(output_t_ref[...], cot)
    pre_round = pre_grad.astype(BF)
    out_acc[...] += nt(cot, activated)
    hid_acc[...] += nt(pre_round, normed)
    hidden_bias_acc[...] += fold(pre_grad)
    normed_grad = nn(hidden_t_ref[...], pre_round)
    gain_acc[...] += fold(normed_grad * scaled)
    grad = normed_grad * gain
    mixed_grad = inverse * (grad - scaled * jnp.mean(grad * scaled, axis=0, keepdims=True))
    mix_bias_acc[...] += fold(mixed_grad)
    mixed_round = mixed_grad.astype(BF)
    mix_acc[...] += nt(mixed_round, filtered)
    for at in range(STEP_ROWS):
        mixed_round_ref[at] = mixed_round[:, at * 256 : at * 256 + 256]

    @pl.when(last)
    def _():
        for k in range(4):
            packed[pl.ds(k, 128, stride=4), :] = mix_acc[:, k * 128 : k * 128 + 128] * scale
        packed[512:768] = hid_acc[...] * scale
        for f in range(2):
            packed[768 + f * 128 : 896 + f * 128] = out_acc[:, f * 128 : f * 128 + 128] * scale
        lanes = lax.broadcasted_iota(jnp.int32, (128, 128), 1)
        small = jnp.zeros((128, 128), F32)
        for at, part in enumerate(
            (mix_bias_acc[...], gain_acc[...], hidden_bias_acc[0:128], hidden_bias_acc[128:256])
        ):
            total = jnp.sum(part, axis=1, keepdims=True) * scale
            small = jnp.where(lanes == at, total, small)
        mine = me_ref[0]
        for ref, half in ((keep_ref, mine), (send_ref, 1 - mine)):
            for p in range(64):
                at = pl.multiple_of(half * 512 + p * 8, 8)
                ref[p * 10 : p * 10 + 8] = packed[pl.ds(at, 8), :]
                ref[p * 10 + 8 : p * 10 + 10] = small[2 * p : 2 * p + 2]


def forward(me, taps, feats, cot, left, right, below, weights, scale):
    whole = lambda v: pl.BlockSpec(v.shape, lambda i: (0,) * v.ndim)
    rows = lambda step: pl.BlockSpec((2, STEP_ROWS, 128, 128), lambda i: (0, step(i), 0, 0))
    this, following = (lambda i: i), (lambda i: jnp.minimum(i + 1, STEPS - 1))
    return pl.pallas_call(
        functools.partial(forward_kernel, scale=scale),
        grid=(STEPS,),
        in_specs=[
            pl.BlockSpec(memory_space=pltpu.SMEM),
            pl.BlockSpec((STEP_ROWS, 12, 128), lambda i: (i, 0, 0)),
            rows(this),
            rows(following),
            pl.BlockSpec((2, 1, 128, 128), lambda i: (0, 2 * i + 1, 0, 0)),
            pl.BlockSpec((2, 1, 128, 128), lambda i: (0, jnp.minimum(2 * i + 2, ROWS - 1), 0, 0)),
            whole(left),
            whole(right),
            whole(below),
            *[whole(v) for v in weights],
        ],
        out_specs=[
            pl.BlockSpec((STEP_ROWS, 128, 256), lambda i: (i, 0, 0)),
            pl.BlockSpec((640, 128), lambda i: (0, 0)),
            pl.BlockSpec((640, 128), lambda i: (0, 0)),
        ],
        out_shape=[
            jax.ShapeDtypeStruct((ROWS, 128, 256), BF),
            jax.ShapeDtypeStruct((640, 128), F32),
            jax.ShapeDtypeStruct((640, 128), F32),
        ],
        scratch_shapes=[
            pltpu.VMEM((2, ROWS + 2, 32, 128), BF),
            pltpu.VMEM((2, 2, 128, 128), BF),
            pltpu.VMEM((2, 128, 128), BF),
            pltpu.VMEM((STEP_ROWS, 512, 512), BF),
            pltpu.VMEM((128, 512), F32),
            pltpu.VMEM((128, 256), F32),
            pltpu.VMEM((256, 128), F32),
            pltpu.VMEM((128, 128), F32),
            pltpu.VMEM((128, 128), F32),
            pltpu.VMEM((256, 128), F32),
            pltpu.VMEM((1024, 128), F32),
        ],
        compiler_params=pltpu.CompilerParams(vmem_limit_bytes=56 * 1024 * 1024),
        cost_estimate=pl.CostEstimate(
            flops=15_000_000_000, bytes_accessed=8_000_000, transcendentals=1_600_000
        ),
    )(me, taps, feats, feats, cot, cot, left, right, below, *weights)


def backward_kernel(
    taps_ref,
    mixed_round_ref,
    mix_t_ref,
    cot_ref,
    part_ref,
    edge_ref,
    to_left_ref,
    to_right_ref,
    acc,
    sides,
    matrix,
):
    step = pl.program_id(0)

    @pl.when(step == 0)
    def _():
        acc[...] = jnp.zeros_like(acc)
        sides[...] = jnp.zeros_like(sides)
        matrix[...] = jnp.zeros_like(matrix)

    for at in range(STEP_ROWS):
        build_filter(taps_ref, at, matrix, at)
    for at in range(STEP_ROWS):
        row = step * STEP_ROWS + at
        grads = nn(mix_t_ref[...], mixed_round_ref[at]).astype(BF)
        arranged = jnp.concatenate(
            [
                jnp.concatenate(
                    [grads[k * 128 : k * 128 + 128, m * 128 : m * 128 + 128] for k in range(4)],
                    axis=1,
                )
                for m in range(2)
            ],
            axis=0,
        )
        spread = nt(arranged, matrix[at, 0:384])
        halo = nt(matrix[at, 384:512], arranged)
        for m in range(2):
            for b in range(3):
                acc[m, row + b] += spread[m * 128 : m * 128 + 128, b * 128 : b * 128 + 128]
                sides[m, row + b] += halo[b * 32 : b * 32 + 32, m * 128 : m * 128 + 128]

    @pl.when(step == STEPS - 1)
    def _():
        part_ref[...] = acc[:, 0:ROWS] + cot_ref[...].astype(F32)
        to_left_ref[...] = sides[:, :, 0:16].astype(BF)
        to_right_ref[...] = sides[:, :, 16:32].astype(BF)
        edge_ref[...] = acc[:, ROWS : ROWS + 2].astype(BF)


def backward(taps, mixed_round, mix_t, cot):
    whole = lambda *shape: pl.BlockSpec(shape, lambda i: (0,) * len(shape))
    return pl.pallas_call(
        backward_kernel,
        grid=(STEPS,),
        in_specs=[
            pl.BlockSpec((STEP_ROWS, 12, 128), lambda i: (i, 0, 0)),
            pl.BlockSpec((STEP_ROWS, 128, 256), lambda i: (i, 0, 0)),
            whole(512, 128),
            whole(2, ROWS, 128, 128),
        ],
        out_specs=[
            whole(2, ROWS, 128, 128),
            whole(2, 2, 128, 128),
            whole(2, ROWS + 2, 16, 128),
            whole(2, ROWS + 2, 16, 128),
        ],
        out_shape=[
            jax.ShapeDtypeStruct((2, ROWS, 128, 128), F32),
            jax.ShapeDtypeStruct((2, 2, 128, 128), BF),
            jax.ShapeDtypeStruct((2, ROWS + 2, 16, 128), BF),
            jax.ShapeDtypeStruct((2, ROWS + 2, 16, 128), BF),
        ],
        scratch_shapes=[
            pltpu.VMEM((2, ROWS + 2, 128, 128), F32),
            pltpu.VMEM((2, ROWS + 2, 32, 128), F32),
            pltpu.VMEM((STEP_ROWS, 512, 512), BF),
        ],
        compiler_params=pltpu.CompilerParams(vmem_limit_bytes=40 * 1024 * 1024),
        cost_estimate=pl.CostEstimate(
            flops=7_500_000_000, bytes_accessed=8_000_000, transcendentals=0
        ),
    )(taps, mixed_round, mix_t, cot)


BORDER_ROWS = 4


def border_kernel(part_ref, left_ref, right_ref, above_ref, out_ref):
    step = pl.program_id(0)
    gap = jnp.zeros((96, 128), BF)
    turn = lambda low, high: jnp.concatenate([low, gap, high], axis=0).T.astype(F32)
    for m in range(2):
        for at in range(BORDER_ROWS):
            out_ref[m, at] = part_ref[m, at] + turn(left_ref[m, at], right_ref[m, at])

    @pl.when(step == 0)
    def _():
        for m in range(2):
            for at in range(2):
                inner = above_ref[m, at * 128 : at * 128 + 128].astype(F32)
                left = above_ref[m, 256 + at * 16 : 272 + at * 16]
                right = above_ref[m, 288 + at * 16 : 304 + at * 16]
                out_ref[m, at] += inner + turn(left, right)


def add_border(part, left, right, above):
    rows = lambda *tail: pl.BlockSpec((2, BORDER_ROWS, *tail), lambda i: (0, i, 0, 0))
    return pl.pallas_call(
        border_kernel,
        grid=(ROWS // BORDER_ROWS,),
        in_specs=[
            rows(128, 128),
            rows(16, 128),
            rows(16, 128),
            pl.BlockSpec((2, 320, 128), lambda i: (0, 0, 0)),
        ],
        out_specs=rows(128, 128),
        out_shape=jax.ShapeDtypeStruct((2, ROWS, 128, 128), F32),
        compiler_params=pltpu.CompilerParams(vmem_limit_bytes=24 * 1024 * 1024),
        cost_estimate=pl.CostEstimate(flops=1_000_000, bytes_accessed=7_000_000, transcendentals=0),
    )(part, left, right, above)


def finish_kernel(me_ref, own_ref, other_ref, mix_ref, hidden_ref, output_ref, small_ref):
    def place(first_ref, second_ref):
        for p in range(64):
            mix_ref[p * 8 : p * 8 + 8] = first_ref[p * 10 : p * 10 + 8]
            rest = second_ref[p * 10 : p * 10 + 8]
            if p < 32:
                hidden_ref[p * 8 : p * 8 + 8] = rest
            else:
                at, half = (p - 32) % 16, (p - 32) // 16
                output_ref[at * 8 : at * 8 + 8, half * 128 : half * 128 + 128] = rest

    pl.when(me_ref[0] == 0)(lambda: place(own_ref, other_ref))
    pl.when(me_ref[0] == 1)(lambda: place(other_ref, own_ref))
    small = jnp.concatenate([own_ref[p * 10 + 8 : p * 10 + 10] for p in range(64)], axis=0)
    small_ref[...] = small.T[0:8]


def finish(me, own, other):
    return pl.pallas_call(
        finish_kernel,
        in_specs=[pl.BlockSpec(memory_space=pltpu.SMEM)]
        + [pl.BlockSpec(memory_space=pltpu.VMEM)] * 2,
        out_shape=[
            jax.ShapeDtypeStruct((512, 128), F32),
            jax.ShapeDtypeStruct((256, 128), F32),
            jax.ShapeDtypeStruct((128, 256), F32),
            jax.ShapeDtypeStruct((8, 128), F32),
        ],
        compiler_params=pltpu.CompilerParams(vmem_limit_bytes=24 * 1024 * 1024),
        cost_estimate=pl.CostEstimate(flops=1_000_000, bytes_accessed=1_200_000, transcendentals=0),
    )(me, own, other)


def ring(axis, shift):
    count = lax.axis_size(axis)
    return [(i, (i + shift) % count) for i in range(count)]


def ring_taps(basis_table, halo_depth):
    total = basis_table.shape[0]
    first = lax.axis_index("lat") * ROWS + 1
    rows = (first + jnp.arange(ROWS, dtype=jnp.int32)) % total
    closed = lambda v: jnp.concatenate([v, v[:1]], axis=0)
    chosen = lax.dynamic_slice_in_dim(closed(basis_table), first, ROWS, 0)
    limits = lax.dynamic_slice_in_dim(closed(halo_depth), first, ROWS, 0)
    taps = jnp.arange(33, dtype=jnp.int32)
    keep = jnp.abs(taps - 16)[None, :] <= limits[:, None]
    offsets = jnp.arange(3, dtype=jnp.int32)[None, :] + rows[:, None]
    inside = (offsets >= 1) & (offsets <= total)
    keep = keep[:, None, None, :] & inside[:, None, :, None]
    kept = jnp.where(keep, chosen, jnp.zeros_like(chosen)).astype(F32)
    spots = (16 - jnp.arange(128, dtype=jnp.int32)) % 128
    place = (taps[:, None] == spots[None, :]).astype(kept.dtype)
    lines = jnp.einsum("rkbt,tv->rbkv", kept, place, preferred_element_type=F32)
    return lines.reshape(ROWS, 12, 128)


def on_device(
    features,
    cotangent,
    basis_table,
    halo_depth,
    mix_weight,
    mix_bias,
    norm_gain,
    hidden_weight,
    hidden_bias,
    output_weight,
):
    to_right, to_left = sides_of(features)
    left = lax.ppermute(to_right, "lon", ring("lon", 1))
    right = lax.ppermute(to_left, "lon", ring("lon", -1))
    wide, tall, hidden_t, output_t, columns = prepare_weights(
        mix_weight, mix_bias, norm_gain, hidden_weight, hidden_bias, output_weight
    )
    taps = ring_taps(basis_table, halo_depth)
    pack = [
        features[:, 0:2].reshape(2, 256, 128),
        left[:, 0:2].reshape(2, 32, 128),
        right[:, 0:2].reshape(2, 32, 128),
        cotangent[:, 0],
    ]
    below = lax.ppermute(jnp.concatenate(pack, axis=1), "lat", ring("lat", -1))

    me = lax.axis_index("member").reshape(1).astype(jnp.int32)
    cell_total = 2 * ROWS * 128 * lax.axis_size(("member", "lat", "lon"))
    mixed_round, keep, send = forward(
        me,
        taps,
        features,
        cotangent,
        left,
        right,
        below,
        (wide, columns, hidden_weight, hidden_t, output_t),
        1.0 / math.sqrt(cell_total),
    )
    swap = [(0, 1), (1, 0)]
    band = ("lat", "lon")
    peers = lax.axis_size(band)
    pair = keep + lax.ppermute(send, "member", swap)
    pieces = lax.all_to_all(pair.reshape(peers, 640 // peers, 1, 128), band, 0, 0)

    part, edge, to_left, to_right = backward(taps, mixed_round, tall, cotangent)
    add_left = lax.ppermute(to_right, "lon", ring("lon", 1))
    add_right = lax.ppermute(to_left, "lon", ring("lon", -1))
    pack = [
        edge.reshape(2, 256, 128),
        add_left[:, ROWS:].reshape(2, 32, 128),
        add_right[:, ROWS:].reshape(2, 32, 128),
    ]
    above = lax.ppermute(jnp.concatenate(pack, axis=1), "lat", ring("lat", 1))

    total = jnp.sum(pieces, axis=0)
    copies = jnp.broadcast_to(total[None], pieces.shape)
    own = lax.all_to_all(copies, band, 0, 0).reshape(640, 128)
    other = lax.ppermute(own, "member", swap)
    feature_grad = add_border(part, add_left, add_right, above)
    mix_grad, hidden_grad, output_grad, small = finish(me, own, other)
    return (
        feature_grad,
        mix_grad.reshape(128, 4, 128),
        small[0],
        small[1],
        hidden_grad,
        small[2:4].reshape(256),
        output_grad,
    )


def solution(mesh):
    cells = P("member", "lat", None, "lon")
    return jax.shard_map(
        on_device,
        mesh=mesh,
        in_specs=(cells, cells) + (P(),) * 8,
        out_specs=(cells,) + (P(),) * 6,
        check_vma=False,
    )
```

```python
import functools
import math

import jax
import jax.numpy as jnp
from jax import lax
from jax.experimental import pallas as pl
from jax.experimental.pallas import tpu as pltpu
from jax.sharding import PartitionSpec as P

EPSILON = 1e-05
BF = jnp.bfloat16
F32 = jnp.float32
GELU_A = math.sqrt(2.0 / math.pi)
GELU_B = 0.044715
ROWS = 24
STEP_ROWS = 6
SIDE_ROWS = 8
STEPS = ROWS // STEP_ROWS


def nn(a, b):
    return lax.dot_general(a, b, (((1,), (0,)), ((), ())), preferred_element_type=F32)


def nt(a, b):
    return lax.dot_general(a, b, (((1,), (1,)), ((), ())), preferred_element_type=F32)


def build_filter(taps_ref, row, matrix_ref, slot):
    lanes = lax.broadcasted_iota(jnp.int32, (16, 128), 1)
    low = lanes < 64
    zero = jnp.zeros((16, 128), BF)
    for b in range(3):
        for k in range(4):
            base = taps_ref[row, pl.ds(b * 4 + k, 1), :]
            head = pltpu.roll(
                jnp.broadcast_to(base, (16, 128)), 0, 1, stride=1, stride_axis=0
            ).astype(BF)
            ring = [head] + [pltpu.roll(head, 16 * g, 1) for g in range(1, 8)]
            cols = pl.ds(k * 128, 128)
            own = pl.ds(b * 128, 128)
            matrix_ref[slot, own, cols] = jnp.concatenate(
                [jnp.where(low, head, zero), *ring[1:7], jnp.where(low, zero, ring[7])], axis=0
            )
            matrix_ref[slot, pl.ds(384 + b * 32, 32), cols] = jnp.concatenate(
                [jnp.where(low, ring[7], zero), jnp.where(low, zero, head)], axis=0
            )


def pack_kernel(*refs):
    *parts, out_ref = refs
    for m in range(2):
        at = 0
        for part in parts:
            for row in range(part.shape[1]):
                size = part.shape[2]
                out_ref[m, at : at + size] = part[m, row]
                at += size


def pack(arrays, starts, counts, vmem):
    specs = [
        pl.BlockSpec((2, n, v.shape[2], 128), functools.partial(lambda b, i: (0, b, 0, 0), s // n))
        for v, s, n in zip(arrays, starts, counts)
    ]
    length = sum(n * v.shape[2] for v, n in zip(arrays, counts))
    return pl.pallas_call(
        pack_kernel,
        grid=(1,),
        in_specs=specs,
        out_specs=pl.BlockSpec((2, length, 128), lambda i: (0, 0, 0)),
        out_shape=jax.ShapeDtypeStruct((2, length, 128), BF),
        compiler_params=pltpu.CompilerParams(vmem_limit_bytes=vmem * 1024 * 1024),
        cost_estimate=pl.CostEstimate(flops=1_000, bytes_accessed=400_000, transcendentals=0),
    )(*arrays)


def sides_kernel(feats_ref, below_ref, to_right_ref, to_left_ref):
    step = pl.program_id(0)
    spot = lax.broadcasted_iota(jnp.int32, (32, 128), 0)
    spot = jnp.where(spot < 16, spot, spot + 96)
    pick = (lax.broadcasted_iota(jnp.int32, (32, 128), 1) == spot).astype(BF)

    def cut(row, blocks):
        turned = nt(pick, jnp.concatenate(blocks, axis=0)).astype(BF)
        for m in range(2):
            to_left_ref[m, row] = turned[:16, m * 128 : m * 128 + 128]
            to_right_ref[m, row] = turned[16:, m * 128 : m * 128 + 128]

    for at in range(SIDE_ROWS):
        cut(step * SIDE_ROWS + at, [feats_ref[0, at], feats_ref[1, at]])

    @pl.when(step == 0)
    def _():
        for at in range(2):
            cut(ROWS + at, [below_ref[m, at * 128 : at * 128 + 128] for m in range(2)])


def sides_of(feats, below):
    side = jax.ShapeDtypeStruct((2, ROWS + 2, 16, 128), BF)
    full = pl.BlockSpec((2, ROWS + 2, 16, 128), lambda i: (0, 0, 0, 0))
    return pl.pallas_call(
        sides_kernel,
        grid=(ROWS // SIDE_ROWS,),
        in_specs=[
            pl.BlockSpec((2, SIDE_ROWS, 128, 128), lambda i: (0, i, 0, 0)),
            pl.BlockSpec((2, 384, 128), lambda i: (0, 0, 0)),
        ],
        out_specs=[full, full],
        out_shape=[side, side],
        compiler_params=pltpu.CompilerParams(vmem_limit_bytes=24 * 1024 * 1024),
        cost_estimate=pl.CostEstimate(flops=50_000_000, bytes_accessed=2_000_000, transcendentals=0),
    )(feats, below)


def forward_kernel(
    me_ref,
    taps_ref,
    feats_ref,
    next_feats_ref,
    cot_ref,
    next_cot_ref,
    left_ref,
    right_ref,
    below_ref,
    mix_ref,
    mix_bias_ref,
    gain_ref,
    hidden_ref,
    hidden_bias_ref,
    output_ref,
    mixed_round_ref,
    keep_ref,
    send_ref,
    mix,
    hidden_t,
    output_t,
    columns,
    sides,
    after,
    after_cot,
    matrix,
    mix_acc,
    out_acc,
    hid_acc,
    mix_bias_acc,
    gain_acc,
    hidden_bias_acc,
    packed,
    *,
    scale,
):
    step = pl.program_id(0)
    last = step == STEPS - 1

    @pl.when(step == 0)
    def _():
        for m in range(2):
            sides[m, :, 0:16] = left_ref[m]
            sides[m, :, 16:32] = right_ref[m]
        mix[...] = jnp.concatenate([mix_ref[:, k, :] for k in range(4)], axis=1)
        hidden_t[...] = hidden_ref[...].T
        output_t[...] = output_ref[...].T
        for at, line in enumerate(
            (mix_bias_ref[...], gain_ref[...], hidden_bias_ref[:, :128], hidden_bias_ref[:, 128:])
        ):
            columns[at * 128 : at * 128 + 128] = jnp.broadcast_to(line, (128, 128)).T
        matrix[...] = jnp.zeros_like(matrix)
        for acc in (mix_acc, out_acc, hid_acc, mix_bias_acc, gain_acc, hidden_bias_acc):
            acc[...] = jnp.zeros_like(acc)

    @pl.when(last)
    def _():
        for m in range(2):
            after[m, 0] = below_ref[m, 0:128]
            after[m, 1] = below_ref[m, 128:256]
            after_cot[m] = below_ref[m, 256:384]

    @pl.when(jnp.logical_not(last))
    def _():
        after[...] = next_feats_ref[...]
        after_cot[...] = next_cot_ref[:, 0]

    cells = []
    for at in range(STEP_ROWS):
        build_filter(taps_ref, at, matrix, at)
        row = step * STEP_ROWS + at
        inputs = []
        for m in range(2):
            halo = jnp.concatenate(
                [sides[m, pl.ds(row, 3)].reshape(96, 128), jnp.zeros((32, 128), BF)], axis=0
            )
            band = [
                feats_ref[m, r] if r < STEP_ROWS else after[m, r - STEP_ROWS]
                for r in range(at, at + 3)
            ]
            inputs.append(jnp.concatenate([*band, halo.T], axis=1))
        filtered = nn(jnp.concatenate(inputs, axis=0), matrix[at]).astype(BF)
        for m in range(2):
            cells.append(
                jnp.concatenate(
                    [
                        filtered[m * 128 : m * 128 + 128, k * 128 : k * 128 + 128]
                        for k in range(4)
                    ],
                    axis=0,
                )
            )
    filtered = jnp.concatenate(cells, axis=1)
    blocks = 2 * STEP_ROWS
    wide = lambda low, high: jnp.concatenate([columns[low:high]] * blocks, axis=1)
    fold = lambda v: functools.reduce(
        lambda a, b: a + b, [v[:, n * 128 : n * 128 + 128] for n in range(blocks)]
    )
    mixed = nn(mix[...], filtered) + wide(0, 128)
    inverse = lax.rsqrt(jnp.mean(mixed * mixed, axis=0, keepdims=True) + EPSILON)
    scaled = mixed * inverse
    gain = wide(128, 256)
    normed = (scaled * gain).astype(BF)
    hidden = nn(hidden_ref[...], normed) + wide(256, 512)
    square = hidden * hidden
    tanh = jnp.tanh(hidden * (GELU_A + (GELU_A * GELU_B) * square))
    half = 0.5 + 0.5 * tanh
    value = hidden * half
    activated = value.astype(BF)
    slope = half + value * (1.0 - half) * (2.0 * GELU_A + (6.0 * GELU_A * GELU_B) * square)
    cot = jnp.concatenate(
        [cot_ref[m, at] for at in range(1, STEP_ROWS) for m in range(2)]
        + [after_cot[0], after_cot[1]],
        axis=1,
    )
    pre_grad = slope * nn(output_t[...], cot)
    pre_round = pre_grad.astype(BF)
    out_acc[...] += nt(cot, activated)
    hid_acc[...] += nt(pre_round, normed)
    hidden_bias_acc[...] += fold(pre_grad)
    normed_grad = nn(hidden_t[...], pre_round)
    gain_acc[...] += fold(normed_grad * scaled)
    grad = normed_grad * gain
    mixed_grad = inverse * (grad - scaled * jnp.mean(grad * scaled, axis=0, keepdims=True))
    mix_bias_acc[...] += fold(mixed_grad)
    mixed_round = mixed_grad.astype(BF)
    mix_acc[...] += nt(mixed_round, filtered)
    for at in range(STEP_ROWS):
        mixed_round_ref[at] = mixed_round[:, at * 256 : at * 256 + 256]

    @pl.when(last)
    def _():
        for k in range(4):
            packed[pl.ds(k, 128, stride=4), :] = mix_acc[:, k * 128 : k * 128 + 128] * scale
        packed[512:768] = hid_acc[...] * scale
        for f in range(2):
            packed[768 + f * 128 : 896 + f * 128] = out_acc[:, f * 128 : f * 128 + 128] * scale
        lanes = lax.broadcasted_iota(jnp.int32, (128, 128), 1)
        small = jnp.zeros((128, 128), F32)
        for at, part in enumerate(
            (mix_bias_acc[...], gain_acc[...], hidden_bias_acc[0:128], hidden_bias_acc[128:256])
        ):
            total = jnp.sum(part, axis=1, keepdims=True) * scale
            small = jnp.where(lanes == at, total, small)
        mine = me_ref[0]
        for ref, half in ((keep_ref, mine), (send_ref, 1 - mine)):
            for p in range(64):
                at = pl.multiple_of(half * 512 + p * 8, 8)
                ref[p * 10 : p * 10 + 8] = packed[pl.ds(at, 8), :]
                ref[p * 10 + 8 : p * 10 + 10] = small[2 * p : 2 * p + 2]


def forward(me, taps, feats, cot, left, right, below, weights, scale):
    whole = lambda v: pl.BlockSpec(v.shape, lambda i: (0,) * v.ndim)
    rows = lambda count, ahead: pl.BlockSpec(
        (2, count, 128, 128),
        lambda i: (0, jnp.minimum((i + ahead) * STEP_ROWS, ROWS - count) // count, 0, 0),
    )
    return pl.pallas_call(
        functools.partial(forward_kernel, scale=scale),
        grid=(STEPS,),
        in_specs=[
            pl.BlockSpec(memory_space=pltpu.SMEM),
            pl.BlockSpec((STEP_ROWS, 12, 128), lambda i: (i, 0, 0)),
            rows(STEP_ROWS, 0),
            rows(2, 1),
            rows(STEP_ROWS, 0),
            rows(1, 1),
            whole(left),
            whole(right),
            whole(below),
            *[whole(v) for v in weights],
        ],
        out_specs=[
            pl.BlockSpec((STEP_ROWS, 128, 256), lambda i: (i, 0, 0)),
            pl.BlockSpec((640, 128), lambda i: (0, 0)),
            pl.BlockSpec((640, 128), lambda i: (0, 0)),
        ],
        out_shape=[
            jax.ShapeDtypeStruct((ROWS, 128, 256), BF),
            jax.ShapeDtypeStruct((640, 128), F32),
            jax.ShapeDtypeStruct((640, 128), F32),
        ],
        scratch_shapes=[
            pltpu.VMEM((128, 512), BF),
            pltpu.VMEM((128, 256), BF),
            pltpu.VMEM((256, 128), BF),
            pltpu.VMEM((512, 128), F32),
            pltpu.VMEM((2, ROWS + 2, 32, 128), BF),
            pltpu.VMEM((2, 2, 128, 128), BF),
            pltpu.VMEM((2, 128, 128), BF),
            pltpu.VMEM((STEP_ROWS, 512, 512), BF),
            pltpu.VMEM((128, 512), F32),
            pltpu.VMEM((128, 256), F32),
            pltpu.VMEM((256, 128), F32),
            pltpu.VMEM((128, 128), F32),
            pltpu.VMEM((128, 128), F32),
            pltpu.VMEM((256, 128), F32),
            pltpu.VMEM((1024, 128), F32),
        ],
        compiler_params=pltpu.CompilerParams(vmem_limit_bytes=32 * 1024 * 1024),
        cost_estimate=pl.CostEstimate(
            flops=15_000_000_000, bytes_accessed=8_000_000, transcendentals=1_600_000
        ),
    )(me, taps, feats, feats, cot, cot, left, right, below, *weights)


def backward_kernel(
    taps_ref,
    mixed_round_ref,
    mix_ref,
    cot_ref,
    part_ref,
    edge_ref,
    to_left_ref,
    to_right_ref,
    acc,
    sides,
    matrix,
    mix_t,
):
    step = pl.program_id(0)

    @pl.when(step == 0)
    def _():
        acc[...] = jnp.zeros_like(acc)
        sides[...] = jnp.zeros_like(sides)
        for k in range(4):
            mix_t[k * 128 : k * 128 + 128] = mix_ref[:, k, :].T
        matrix[...] = jnp.zeros_like(matrix)

    for at in range(STEP_ROWS):
        build_filter(taps_ref, at, matrix, at)
        row = step * STEP_ROWS + at
        grads = nn(mix_t[...], mixed_round_ref[at]).astype(BF)
        arranged = jnp.concatenate(
            [
                jnp.concatenate(
                    [grads[k * 128 : k * 128 + 128, m * 128 : m * 128 + 128] for k in range(4)],
                    axis=1,
                )
                for m in range(2)
            ],
            axis=0,
        )
        spread = nt(arranged, matrix[at, 0:384])
        halo = nt(matrix[at, 384:512], arranged)
        for m in range(2):
            for b in range(3):
                acc[m, row + b] += spread[m * 128 : m * 128 + 128, b * 128 : b * 128 + 128]
                sides[m, row + b] += halo[b * 32 : b * 32 + 32, m * 128 : m * 128 + 128]

    @pl.when(step == STEPS - 1)
    def _():
        part_ref[...] = acc[:, 0:ROWS] + cot_ref[...].astype(F32)
        to_left_ref[...] = sides[:, :, 0:16].astype(BF)
        to_right_ref[...] = sides[:, :, 16:32].astype(BF)
        edge_ref[...] = acc[:, ROWS : ROWS + 2].astype(BF)


def backward(taps, mixed_round, mix, cot):
    whole = lambda *shape: pl.BlockSpec(shape, lambda i: (0,) * len(shape))
    return pl.pallas_call(
        backward_kernel,
        grid=(STEPS,),
        in_specs=[
            pl.BlockSpec((STEP_ROWS, 12, 128), lambda i: (i, 0, 0)),
            pl.BlockSpec((STEP_ROWS, 128, 256), lambda i: (i, 0, 0)),
            whole(128, 4, 128),
            whole(2, ROWS, 128, 128),
        ],
        out_specs=[
            whole(2, ROWS, 128, 128),
            whole(2, 2, 128, 128),
            whole(2, ROWS + 2, 16, 128),
            whole(2, ROWS + 2, 16, 128),
        ],
        out_shape=[
            jax.ShapeDtypeStruct((2, ROWS, 128, 128), F32),
            jax.ShapeDtypeStruct((2, 2, 128, 128), BF),
            jax.ShapeDtypeStruct((2, ROWS + 2, 16, 128), BF),
            jax.ShapeDtypeStruct((2, ROWS + 2, 16, 128), BF),
        ],
        scratch_shapes=[
            pltpu.VMEM((2, ROWS + 2, 128, 128), F32),
            pltpu.VMEM((2, ROWS + 2, 32, 128), F32),
            pltpu.VMEM((STEP_ROWS, 512, 512), BF),
            pltpu.VMEM((512, 128), BF),
        ],
        compiler_params=pltpu.CompilerParams(vmem_limit_bytes=40 * 1024 * 1024),
        cost_estimate=pl.CostEstimate(
            flops=7_500_000_000, bytes_accessed=8_000_000, transcendentals=0
        ),
    )(taps, mixed_round, mix, cot)


BORDER_ROWS = 4


def border_kernel(part_ref, left_ref, right_ref, above_ref, out_ref):
    step = pl.program_id(0)
    gap = jnp.zeros((96, 128), BF)
    turn = lambda low, high: jnp.concatenate([low, gap, high], axis=0).T.astype(F32)
    for m in range(2):
        for at in range(BORDER_ROWS):
            out_ref[m, at] = part_ref[m, at] + turn(left_ref[m, at], right_ref[m, at])

    @pl.when(step == 0)
    def _():
        for m in range(2):
            for at in range(2):
                inner = above_ref[m, at * 128 : at * 128 + 128].astype(F32)
                left = above_ref[m, 256 + at * 16 : 272 + at * 16]
                right = above_ref[m, 288 + at * 16 : 304 + at * 16]
                out_ref[m, at] += inner + turn(left, right)


def add_border(part, left, right, above):
    rows = lambda *tail: pl.BlockSpec((2, BORDER_ROWS, *tail), lambda i: (0, i, 0, 0))
    return pl.pallas_call(
        border_kernel,
        grid=(ROWS // BORDER_ROWS,),
        in_specs=[
            rows(128, 128),
            rows(16, 128),
            rows(16, 128),
            pl.BlockSpec((2, 320, 128), lambda i: (0, 0, 0)),
        ],
        out_specs=rows(128, 128),
        out_shape=jax.ShapeDtypeStruct((2, ROWS, 128, 128), F32),
        compiler_params=pltpu.CompilerParams(vmem_limit_bytes=24 * 1024 * 1024),
        cost_estimate=pl.CostEstimate(flops=1_000_000, bytes_accessed=7_000_000, transcendentals=0),
    )(part, left, right, above)


def finish_kernel(
    me_ref, own_ref, other_ref, mix_ref, hidden_ref, output_ref, bias_ref, gain_ref, hidden_bias_ref
):
    def place(first_ref, second_ref):
        for p in range(64):
            mix_ref[p * 8 : p * 8 + 8] = first_ref[p * 10 : p * 10 + 8]
            rest = second_ref[p * 10 : p * 10 + 8]
            if p < 32:
                hidden_ref[p * 8 : p * 8 + 8] = rest
            else:
                at, half = (p - 32) % 16, (p - 32) // 16
                output_ref[at * 8 : at * 8 + 8, half * 128 : half * 128 + 128] = rest

    pl.when(me_ref[0] == 0)(lambda: place(own_ref, other_ref))
    pl.when(me_ref[0] == 1)(lambda: place(other_ref, own_ref))
    small = jnp.concatenate([own_ref[p * 10 + 8 : p * 10 + 10] for p in range(64)], axis=0)
    small = small.T
    bias_ref[...] = small[0:1]
    gain_ref[...] = small[1:2]
    hidden_bias_ref[...] = jnp.concatenate([small[2:3], small[3:4]], axis=1)


def finish(me, own, other):
    return pl.pallas_call(
        finish_kernel,
        in_specs=[pl.BlockSpec(memory_space=pltpu.SMEM)]
        + [pl.BlockSpec(memory_space=pltpu.VMEM)] * 2,
        out_shape=[
            jax.ShapeDtypeStruct((512, 128), F32),
            jax.ShapeDtypeStruct((256, 128), F32),
            jax.ShapeDtypeStruct((128, 256), F32),
            jax.ShapeDtypeStruct((1, 128), F32),
            jax.ShapeDtypeStruct((1, 128), F32),
            jax.ShapeDtypeStruct((1, 256), F32),
        ],
        compiler_params=pltpu.CompilerParams(vmem_limit_bytes=24 * 1024 * 1024),
        cost_estimate=pl.CostEstimate(flops=1_000_000, bytes_accessed=1_200_000, transcendentals=0),
    )(me, own, other)


def ring(axis, shift):
    count = lax.axis_size(axis)
    return [(i, (i + shift) % count) for i in range(count)]


def ring_taps(basis_table, halo_depth):
    total = basis_table.shape[0]
    first = lax.axis_index("lat") * ROWS + 1
    rows = (first + jnp.arange(ROWS, dtype=jnp.int32)) % total
    closed = lambda v: jnp.concatenate([v, v[:1]], axis=0)
    chosen = lax.dynamic_slice_in_dim(closed(basis_table), first, ROWS, 0)
    limits = lax.dynamic_slice_in_dim(closed(halo_depth), first, ROWS, 0)
    taps = jnp.arange(33, dtype=jnp.int32)
    keep = jnp.abs(taps - 16)[None, :] <= limits[:, None]
    offsets = jnp.arange(3, dtype=jnp.int32)[None, :] + rows[:, None]
    inside = (offsets >= 1) & (offsets <= total)
    keep = keep[:, None, None, :] & inside[:, None, :, None]
    kept = jnp.where(keep, chosen, jnp.zeros_like(chosen)).astype(F32)
    spots = (16 - jnp.arange(128, dtype=jnp.int32)) % 128
    place = (taps[:, None] == spots[None, :]).astype(kept.dtype)
    lines = jnp.einsum("rkbt,tv->rbkv", kept, place, preferred_element_type=F32)
    return lines.reshape(ROWS, 12, 128)


def on_device(
    features,
    cotangent,
    basis_table,
    halo_depth,
    mix_weight,
    mix_bias,
    norm_gain,
    hidden_weight,
    hidden_bias,
    output_weight,
):
    below = lax.ppermute(pack((features, cotangent), (0, 0), (2, 1), 56), "lat", ring("lat", -1))
    taps = ring_taps(basis_table, halo_depth)
    to_right, to_left = sides_of(features, below)
    left = lax.ppermute(to_right, "lon", ring("lon", 1))
    right = lax.ppermute(to_left, "lon", ring("lon", -1))

    me = lax.axis_index("member").reshape(1).astype(jnp.int32)
    cell_total = 2 * ROWS * 128 * lax.axis_size(("member", "lat", "lon"))
    weights = (
        mix_weight,
        mix_bias[None],
        norm_gain[None],
        hidden_weight,
        hidden_bias[None],
        output_weight,
    )
    mixed_round, keep, send = forward(
        me, taps, features, cotangent, left, right, below, weights, 1.0 / math.sqrt(cell_total)
    )
    swap = [(0, 1), (1, 0)]
    band = ("lat", "lon")
    peers = lax.axis_size(band)
    pair = keep + lax.ppermute(send, "member", swap)
    pair, mixed_round = lax.optimization_barrier((pair, mixed_round))
    pieces = lax.all_to_all(pair.reshape(peers, 640 // peers, 1, 128), band, 0, 0)
    part, edge, to_left, to_right = backward(taps, mixed_round, mix_weight, cotangent)

    total, edge = lax.optimization_barrier((jnp.sum(pieces, axis=0), edge))
    add_left = lax.ppermute(to_right, "lon", ring("lon", 1))
    add_right = lax.ppermute(to_left, "lon", ring("lon", -1))
    above = pack((edge, add_left, add_right), (0, ROWS, ROWS), (2, 2, 2), 24)
    above = lax.ppermute(above, "lat", ring("lat", 1))

    copies = jnp.broadcast_to(total[None], pieces.shape)
    own = lax.all_to_all(copies, band, 0, 0).reshape(640, 128)
    other = lax.ppermute(own, "member", swap)
    feature_grad = add_border(part, add_left, add_right, above)
    mix_grad, hidden_grad, output_grad, bias, gain, hidden_bias = finish(me, own, other)
    return (
        feature_grad,
        mix_grad.reshape(128, 4, 128),
        bias.reshape(128),
        gain.reshape(128),
        hidden_grad,
        hidden_bias.reshape(256),
        output_grad,
    )


def solution(mesh):
    cells = P("member", "lat", None, "lon")
    return jax.shard_map(
        on_device,
        mesh=mesh,
        in_specs=(cells, cells) + (P(),) * 8,
        out_specs=(cells,) + (P(),) * 6,
        check_vma=False,
    )
```

```python
import functools
import math

import jax
import jax.numpy as jnp
from jax import lax
from jax.experimental import pallas as pl
from jax.experimental.pallas import tpu as pltpu
from jax.sharding import PartitionSpec as P

EPSILON = 1e-05
BF = jnp.bfloat16
F32 = jnp.float32
GELU_A = math.sqrt(2.0 / math.pi)
GELU_B = 0.044715
ROWS = 24
STEP_ROWS = 6
SIDE_ROWS = 8
STEPS = ROWS // STEP_ROWS


def nn(a, b):
    return lax.dot_general(a, b, (((1,), (0,)), ((), ())), preferred_element_type=F32)


def nt(a, b):
    return lax.dot_general(a, b, (((1,), (1,)), ((), ())), preferred_element_type=F32)


def build_filter(taps_ref, row, matrix_ref, slot):
    lanes = lax.broadcasted_iota(jnp.int32, (16, 128), 1)
    low = lanes < 64
    zero = jnp.zeros((16, 128), BF)
    for b in range(3):
        for k in range(4):
            base = taps_ref[row, pl.ds(b * 4 + k, 1), :]
            head = pltpu.roll(
                jnp.broadcast_to(base, (16, 128)), 0, 1, stride=1, stride_axis=0
            ).astype(BF)
            ring = [head] + [pltpu.roll(head, 16 * g, 1) for g in range(1, 8)]
            cols = pl.ds(k * 128, 128)
            own = pl.ds(b * 128, 128)
            matrix_ref[slot, own, cols] = jnp.concatenate(
                [jnp.where(low, head, zero), *ring[1:7], jnp.where(low, zero, ring[7])], axis=0
            )
            matrix_ref[slot, pl.ds(384 + b * 32, 32), cols] = jnp.concatenate(
                [jnp.where(low, ring[7], zero), jnp.where(low, zero, head)], axis=0
            )


def pack_kernel(*refs):
    *parts, out_ref = refs
    for m in range(2):
        at = 0
        for part in parts:
            for row in range(part.shape[1]):
                size = part.shape[2]
                out_ref[m, at : at + size] = part[m, row]
                at += size


def pack(arrays, starts, counts, vmem):
    specs = [
        pl.BlockSpec((2, n, v.shape[2], 128), functools.partial(lambda b, i: (0, b, 0, 0), s // n))
        for v, s, n in zip(arrays, starts, counts)
    ]
    length = sum(n * v.shape[2] for v, n in zip(arrays, counts))
    return pl.pallas_call(
        pack_kernel,
        grid=(1,),
        in_specs=specs,
        out_specs=pl.BlockSpec((2, length, 128), lambda i: (0, 0, 0)),
        out_shape=jax.ShapeDtypeStruct((2, length, 128), BF),
        compiler_params=pltpu.CompilerParams(vmem_limit_bytes=vmem * 1024 * 1024),
        cost_estimate=pl.CostEstimate(flops=1_000, bytes_accessed=400_000, transcendentals=0),
    )(*arrays)


def sides_kernel(feats_ref, below_ref, to_right_ref, to_left_ref):
    step = pl.program_id(0)
    spot = lax.broadcasted_iota(jnp.int32, (32, 128), 0)
    spot = jnp.where(spot < 16, spot, spot + 96)
    pick = (lax.broadcasted_iota(jnp.int32, (32, 128), 1) == spot).astype(BF)

    def cut(row, blocks):
        turned = nt(pick, jnp.concatenate(blocks, axis=0)).astype(BF)
        for m in range(2):
            to_left_ref[m, row] = turned[:16, m * 128 : m * 128 + 128]
            to_right_ref[m, row] = turned[16:, m * 128 : m * 128 + 128]

    for at in range(SIDE_ROWS):
        cut(step * SIDE_ROWS + at, [feats_ref[0, at], feats_ref[1, at]])

    @pl.when(step == 0)
    def _():
        for at in range(2):
            cut(ROWS + at, [below_ref[m, at * 128 : at * 128 + 128] for m in range(2)])


def sides_of(feats, below):
    side = jax.ShapeDtypeStruct((2, ROWS + 2, 16, 128), BF)
    full = pl.BlockSpec((2, ROWS + 2, 16, 128), lambda i: (0, 0, 0, 0))
    return pl.pallas_call(
        sides_kernel,
        grid=(ROWS // SIDE_ROWS,),
        in_specs=[
            pl.BlockSpec((2, SIDE_ROWS, 128, 128), lambda i: (0, i, 0, 0)),
            pl.BlockSpec((2, 384, 128), lambda i: (0, 0, 0)),
        ],
        out_specs=[full, full],
        out_shape=[side, side],
        compiler_params=pltpu.CompilerParams(vmem_limit_bytes=24 * 1024 * 1024),
        cost_estimate=pl.CostEstimate(flops=50_000_000, bytes_accessed=2_000_000, transcendentals=0),
    )(feats, below)


def forward_kernel(
    me_ref,
    taps_ref,
    feats_ref,
    next_feats_ref,
    cot_ref,
    next_cot_ref,
    left_ref,
    right_ref,
    below_ref,
    mix_ref,
    mix_bias_ref,
    gain_ref,
    hidden_ref,
    hidden_bias_ref,
    output_ref,
    mixed_round_ref,
    keep_ref,
    send_ref,
    mix,
    hidden_t,
    output_t,
    columns,
    sides,
    after,
    after_cot,
    matrix,
    mix_acc,
    out_acc,
    hid_acc,
    mix_bias_acc,
    gain_acc,
    hidden_bias_acc,
    packed,
    *,
    scale,
):
    step = pl.program_id(0)
    last = step == STEPS - 1

    @pl.when(step == 0)
    def _():
        for m in range(2):
            sides[m, :, 0:16] = left_ref[m]
            sides[m, :, 16:32] = right_ref[m]
        matrix[...] = jnp.zeros_like(matrix)
        mix[...] = jnp.concatenate([mix_ref[:, k, :] for k in range(4)], axis=1)
        hidden_t[...] = hidden_ref[...].T
        output_t[...] = output_ref[...].T
        for at, line in enumerate(
            (mix_bias_ref[...], gain_ref[...], hidden_bias_ref[:, :128], hidden_bias_ref[:, 128:])
        ):
            columns[at * 128 : at * 128 + 128] = jnp.broadcast_to(line, (128, 128)).T
        for acc in (mix_acc, out_acc, hid_acc, mix_bias_acc, gain_acc, hidden_bias_acc):
            acc[...] = jnp.zeros_like(acc)

    @pl.when(last)
    def _():
        for m in range(2):
            after[m, 0] = below_ref[m, 0:128]
            after[m, 1] = below_ref[m, 128:256]
            after_cot[m] = below_ref[m, 256:384]

    @pl.when(jnp.logical_not(last))
    def _():
        after[...] = next_feats_ref[...]
        after_cot[...] = next_cot_ref[:, 0]

    cells = []
    for at in range(STEP_ROWS):
        build_filter(taps_ref, at, matrix, at)
        row = step * STEP_ROWS + at
        inputs = []
        for m in range(2):
            halo = jnp.concatenate(
                [sides[m, pl.ds(row, 3)].reshape(96, 128), jnp.zeros((32, 128), BF)], axis=0
            )
            band = [
                feats_ref[m, r] if r < STEP_ROWS else after[m, r - STEP_ROWS]
                for r in range(at, at + 3)
            ]
            inputs.append(jnp.concatenate([*band, halo.T], axis=1))
        filtered = nn(jnp.concatenate(inputs, axis=0), matrix[at]).astype(BF)
        for m in range(2):
            cells.append(
                jnp.concatenate(
                    [
                        filtered[m * 128 : m * 128 + 128, k * 128 : k * 128 + 128]
                        for k in range(4)
                    ],
                    axis=0,
                )
            )
    filtered = jnp.concatenate(cells, axis=1)
    blocks = 2 * STEP_ROWS
    wide = lambda low, high: jnp.concatenate([columns[low:high]] * blocks, axis=1)
    fold = lambda v: functools.reduce(
        lambda a, b: a + b, [v[:, n * 128 : n * 128 + 128] for n in range(blocks)]
    )
    mixed = nn(mix[...], filtered) + wide(0, 128)
    inverse = lax.rsqrt(jnp.mean(mixed * mixed, axis=0, keepdims=True) + EPSILON)
    scaled = mixed * inverse
    gain = wide(128, 256)
    normed = (scaled * gain).astype(BF)
    hidden = nn(hidden_ref[...], normed) + wide(256, 512)
    square = hidden * hidden
    tanh = jnp.tanh(hidden * (GELU_A + (GELU_A * GELU_B) * square))
    half = 0.5 + 0.5 * tanh
    value = hidden * half
    activated = value.astype(BF)
    slope = half + value * (1.0 - half) * (2.0 * GELU_A + (6.0 * GELU_A * GELU_B) * square)
    cot = jnp.concatenate(
        [cot_ref[m, at] for at in range(1, STEP_ROWS) for m in range(2)]
        + [after_cot[0], after_cot[1]],
        axis=1,
    )
    pre_grad = slope * nn(output_t[...], cot)
    pre_round = pre_grad.astype(BF)
    out_acc[...] += nt(cot, activated)
    hid_acc[...] += nt(pre_round, normed)
    hidden_bias_acc[...] += fold(pre_grad)
    normed_grad = nn(hidden_t[...], pre_round)
    gain_acc[...] += fold(normed_grad * scaled)
    grad = normed_grad * gain
    mixed_grad = inverse * (grad - scaled * jnp.mean(grad * scaled, axis=0, keepdims=True))
    mix_bias_acc[...] += fold(mixed_grad)
    mixed_round = mixed_grad.astype(BF)
    mix_acc[...] += nt(mixed_round, filtered)
    for at in range(STEP_ROWS):
        mixed_round_ref[at] = mixed_round[:, at * 256 : at * 256 + 256]

    @pl.when(last)
    def _():
        for k in range(4):
            packed[pl.ds(k, 128, stride=4), :] = mix_acc[:, k * 128 : k * 128 + 128] * scale
        packed[512:768] = hid_acc[...] * scale
        for f in range(2):
            packed[768 + f * 128 : 896 + f * 128] = out_acc[:, f * 128 : f * 128 + 128] * scale
        lanes = lax.broadcasted_iota(jnp.int32, (128, 128), 1)
        small = jnp.zeros((128, 128), F32)
        for at, part in enumerate(
            (mix_bias_acc[...], gain_acc[...], hidden_bias_acc[0:128], hidden_bias_acc[128:256])
        ):
            total = jnp.sum(part, axis=1, keepdims=True) * scale
            small = jnp.where(lanes == at, total, small)
        mine = me_ref[0]
        for ref, half in ((keep_ref, mine), (send_ref, 1 - mine)):
            for p in range(64):
                at = pl.multiple_of(half * 512 + p * 8, 8)
                ref[p * 10 : p * 10 + 8] = packed[pl.ds(at, 8), :]
                ref[p * 10 + 8 : p * 10 + 10] = small[2 * p : 2 * p + 2]


def forward(me, taps, feats, cot, left, right, below, weights, scale):
    whole = lambda v: pl.BlockSpec(v.shape, lambda i: (0,) * v.ndim)
    rows = lambda count, ahead: pl.BlockSpec(
        (2, count, 128, 128),
        lambda i: (0, jnp.minimum((i + ahead) * STEP_ROWS, ROWS - count) // count, 0, 0),
    )
    return pl.pallas_call(
        functools.partial(forward_kernel, scale=scale),
        grid=(STEPS,),
        in_specs=[
            pl.BlockSpec(memory_space=pltpu.SMEM),
            pl.BlockSpec((STEP_ROWS, 12, 128), lambda i: (i, 0, 0)),
            rows(STEP_ROWS, 0),
            rows(2, 1),
            rows(STEP_ROWS, 0),
            rows(1, 1),
            whole(left),
            whole(right),
            whole(below),
            *[whole(v) for v in weights],
        ],
        out_specs=[
            pl.BlockSpec((STEP_ROWS, 128, 256), lambda i: (i, 0, 0)),
            pl.BlockSpec((640, 128), lambda i: (0, 0)),
            pl.BlockSpec((640, 128), lambda i: (0, 0)),
        ],
        out_shape=[
            jax.ShapeDtypeStruct((ROWS, 128, 256), BF),
            jax.ShapeDtypeStruct((640, 128), F32),
            jax.ShapeDtypeStruct((640, 128), F32),
        ],
        scratch_shapes=[
            pltpu.VMEM((128, 512), BF),
            pltpu.VMEM((128, 256), BF),
            pltpu.VMEM((256, 128), BF),
            pltpu.VMEM((512, 128), F32),
            pltpu.VMEM((2, ROWS + 2, 32, 128), BF),
            pltpu.VMEM((2, 2, 128, 128), BF),
            pltpu.VMEM((2, 128, 128), BF),
            pltpu.VMEM((STEP_ROWS, 512, 512), BF),
            pltpu.VMEM((128, 512), F32),
            pltpu.VMEM((128, 256), F32),
            pltpu.VMEM((256, 128), F32),
            pltpu.VMEM((128, 128), F32),
            pltpu.VMEM((128, 128), F32),
            pltpu.VMEM((256, 128), F32),
            pltpu.VMEM((1024, 128), F32),
        ],
        compiler_params=pltpu.CompilerParams(vmem_limit_bytes=32 * 1024 * 1024),
        cost_estimate=pl.CostEstimate(
            flops=15_000_000_000, bytes_accessed=8_000_000, transcendentals=1_600_000
        ),
    )(me, taps, feats, feats, cot, cot, left, right, below, *weights)


def backward_kernel(
    taps_ref,
    mixed_round_ref,
    mix_ref,
    part_ref,
    edge_ref,
    to_left_ref,
    to_right_ref,
    acc,
    sides,
    matrix,
    mix_t,
    sems,
):
    step = pl.program_id(0)

    @pl.when(step == 0)
    def _():
        acc[...] = jnp.zeros_like(acc)
        sides[...] = jnp.zeros_like(sides)
        matrix[...] = jnp.zeros_like(matrix)
        for k in range(4):
            mix_t[k * 128 : k * 128 + 128] = mix_ref[:, k, :].T

    for at in range(STEP_ROWS):
        build_filter(taps_ref, at, matrix, at)
        row = step * STEP_ROWS + at
        grads = nn(mix_t[...], mixed_round_ref[at]).astype(BF)
        arranged = jnp.concatenate(
            [
                jnp.concatenate(
                    [grads[k * 128 : k * 128 + 128, m * 128 : m * 128 + 128] for k in range(4)],
                    axis=1,
                )
                for m in range(2)
            ],
            axis=0,
        )
        spread = nt(arranged, matrix[at, 0:384])
        halo = nt(matrix[at, 384:512], arranged)
        for m in range(2):
            for b in range(3):
                acc[m, row + b] += spread[m * 128 : m * 128 + 128, b * 128 : b * 128 + 128]
                sides[m, row + b] += halo[b * 32 : b * 32 + 32, m * 128 : m * 128 + 128]

    def write(at):
        rows = pl.ds(at * STEP_ROWS, STEP_ROWS)
        return pltpu.make_async_copy(acc.at[:, rows], part_ref.at[:, rows], sems.at[at])

    for at in range(STEPS):
        pl.when(step == at)(lambda: write(at).start())

    @pl.when(step == STEPS - 1)
    def _():
        to_left_ref[...] = sides[:, :, 0:16].astype(BF)
        to_right_ref[...] = sides[:, :, 16:32].astype(BF)
        edge_ref[...] = acc[:, ROWS : ROWS + 2].astype(BF)
        for at in range(STEPS):
            write(at).wait()


def backward(taps, mixed_round, mix):
    whole = lambda *shape: pl.BlockSpec(shape, lambda i: (0,) * len(shape))
    return pl.pallas_call(
        backward_kernel,
        grid=(STEPS,),
        in_specs=[
            pl.BlockSpec((STEP_ROWS, 12, 128), lambda i: (i, 0, 0)),
            pl.BlockSpec((STEP_ROWS, 128, 256), lambda i: (i, 0, 0)),
            whole(128, 4, 128),
        ],
        out_specs=[
            pl.BlockSpec(memory_space=pltpu.MemorySpace.HBM),
            whole(2, 2, 128, 128),
            whole(2, ROWS + 2, 16, 128),
            whole(2, ROWS + 2, 16, 128),
        ],
        out_shape=[
            jax.ShapeDtypeStruct((2, ROWS, 128, 128), F32),
            jax.ShapeDtypeStruct((2, 2, 128, 128), BF),
            jax.ShapeDtypeStruct((2, ROWS + 2, 16, 128), BF),
            jax.ShapeDtypeStruct((2, ROWS + 2, 16, 128), BF),
        ],
        scratch_shapes=[
            pltpu.VMEM((2, ROWS + 2, 128, 128), F32),
            pltpu.VMEM((2, ROWS + 2, 32, 128), F32),
            pltpu.VMEM((STEP_ROWS, 512, 512), BF),
            pltpu.VMEM((512, 128), BF),
            pltpu.SemaphoreType.DMA((STEPS,)),
        ],
        compiler_params=pltpu.CompilerParams(vmem_limit_bytes=58 * 1024 * 1024),
        cost_estimate=pl.CostEstimate(
            flops=7_500_000_000, bytes_accessed=8_000_000, transcendentals=0
        ),
    )(taps, mixed_round, mix)


BORDER_ROWS = 8


def border_kernel(part_ref, cot_ref, left_ref, right_ref, above_ref, out_ref):
    step = pl.program_id(0)
    gap = jnp.zeros((96, 128), BF)
    turn = lambda low, high: jnp.concatenate([low, gap, high], axis=0).T.astype(F32)
    for m in range(2):
        for at in range(BORDER_ROWS):
            out_ref[m, at] = (part_ref[m, at] + cot_ref[m, at].astype(F32)) + turn(
                left_ref[m, at], right_ref[m, at]
            )

    @pl.when(step == 0)
    def _():
        for m in range(2):
            for at in range(2):
                inner = above_ref[m, at * 128 : at * 128 + 128].astype(F32)
                left = above_ref[m, 256 + at * 16 : 272 + at * 16]
                right = above_ref[m, 288 + at * 16 : 304 + at * 16]
                out_ref[m, at] += inner + turn(left, right)


def add_border(part, cot, left, right, above):
    rows = lambda *tail: pl.BlockSpec((2, BORDER_ROWS, *tail), lambda i: (0, i, 0, 0))
    return pl.pallas_call(
        border_kernel,
        grid=(ROWS // BORDER_ROWS,),
        in_specs=[
            rows(128, 128),
            rows(128, 128),
            rows(16, 128),
            rows(16, 128),
            pl.BlockSpec((2, 320, 128), lambda i: (0, 0, 0)),
        ],
        out_specs=rows(128, 128),
        out_shape=jax.ShapeDtypeStruct((2, ROWS, 128, 128), F32),
        compiler_params=pltpu.CompilerParams(vmem_limit_bytes=56 * 1024 * 1024),
        cost_estimate=pl.CostEstimate(flops=1_000_000, bytes_accessed=7_000_000, transcendentals=0),
    )(part, cot, left, right, above)


def finish_kernel(
    me_ref, own_ref, other_ref, mix_ref, hidden_ref, output_ref, bias_ref, gain_ref, hidden_bias_ref
):
    def place(first_ref, second_ref):
        for p in range(64):
            mix_ref[p * 8 : p * 8 + 8] = first_ref[p * 10 : p * 10 + 8]
            rest = second_ref[p * 10 : p * 10 + 8]
            if p < 32:
                hidden_ref[p * 8 : p * 8 + 8] = rest
            else:
                at, half = (p - 32) % 16, (p - 32) // 16
                output_ref[at * 8 : at * 8 + 8, half * 128 : half * 128 + 128] = rest

    pl.when(me_ref[0] == 0)(lambda: place(own_ref, other_ref))
    pl.when(me_ref[0] == 1)(lambda: place(other_ref, own_ref))
    small = jnp.concatenate([own_ref[p * 10 + 8 : p * 10 + 10] for p in range(64)], axis=0)
    small = small.T
    bias_ref[...] = small[0:1]
    gain_ref[...] = small[1:2]
    hidden_bias_ref[...] = jnp.concatenate([small[2:3], small[3:4]], axis=1)


def finish(me, own, other):
    return pl.pallas_call(
        finish_kernel,
        in_specs=[pl.BlockSpec(memory_space=pltpu.SMEM)]
        + [pl.BlockSpec(memory_space=pltpu.VMEM)] * 2,
        out_shape=[
            jax.ShapeDtypeStruct((512, 128), F32),
            jax.ShapeDtypeStruct((256, 128), F32),
            jax.ShapeDtypeStruct((128, 256), F32),
            jax.ShapeDtypeStruct((1, 128), F32),
            jax.ShapeDtypeStruct((1, 128), F32),
            jax.ShapeDtypeStruct((1, 256), F32),
        ],
        compiler_params=pltpu.CompilerParams(vmem_limit_bytes=24 * 1024 * 1024),
        cost_estimate=pl.CostEstimate(flops=1_000_000, bytes_accessed=1_200_000, transcendentals=0),
    )(me, own, other)


def ring(axis, shift):
    count = lax.axis_size(axis)
    return [(i, (i + shift) % count) for i in range(count)]


def ring_taps(basis_table, halo_depth):
    total = basis_table.shape[0]
    first = lax.axis_index("lat") * ROWS + 1
    rows = (first + jnp.arange(ROWS, dtype=jnp.int32)) % total
    closed = lambda v: jnp.concatenate([v, v[:1]], axis=0)
    chosen = lax.dynamic_slice_in_dim(closed(basis_table), first, ROWS, 0)
    limits = lax.dynamic_slice_in_dim(closed(halo_depth), first, ROWS, 0)
    taps = jnp.arange(33, dtype=jnp.int32)
    keep = jnp.abs(taps - 16)[None, :] <= limits[:, None]
    offsets = jnp.arange(3, dtype=jnp.int32)[None, :] + rows[:, None]
    inside = (offsets >= 1) & (offsets <= total)
    keep = keep[:, None, None, :] & inside[:, None, :, None]
    kept = jnp.where(keep, chosen, jnp.zeros_like(chosen)).astype(F32)
    spots = (16 - jnp.arange(128, dtype=jnp.int32)) % 128
    place = (taps[:, None] == spots[None, :]).astype(kept.dtype)
    lines = jnp.einsum("rkbt,tv->rbkv", kept, place, preferred_element_type=F32)
    return lines.reshape(ROWS, 12, 128)


def on_device(
    features,
    cotangent,
    basis_table,
    halo_depth,
    mix_weight,
    mix_bias,
    norm_gain,
    hidden_weight,
    hidden_bias,
    output_weight,
):
    below = lax.ppermute(pack((features, cotangent), (0, 0), (2, 1), 56), "lat", ring("lat", -1))
    taps = ring_taps(basis_table, halo_depth)
    to_right, to_left = sides_of(features, below)
    left = lax.ppermute(to_right, "lon", ring("lon", 1))
    right = lax.ppermute(to_left, "lon", ring("lon", -1))

    me = lax.axis_index("member").reshape(1).astype(jnp.int32)
    cell_total = 2 * ROWS * 128 * lax.axis_size(("member", "lat", "lon"))
    weights = (
        mix_weight,
        mix_bias[None],
        norm_gain[None],
        hidden_weight,
        hidden_bias[None],
        output_weight,
    )
    mixed_round, keep, send = forward(
        me, taps, features, cotangent, left, right, below, weights, 1.0 / math.sqrt(cell_total)
    )
    swap = [(0, 1), (1, 0)]
    band = ("lat", "lon")
    peers = lax.axis_size(band)
    pair = keep + lax.ppermute(send, "member", swap)
    part, edge, to_left, to_right = backward(taps, mixed_round, mix_weight)
    pair, edge = lax.optimization_barrier((pair, edge))
    pieces = lax.all_to_all(pair.reshape(peers, 640 // peers, 1, 128), band, 0, 0)
    add_left = lax.ppermute(to_right, "lon", ring("lon", 1))
    add_right = lax.ppermute(to_left, "lon", ring("lon", -1))
    above = pack((edge, add_left, add_right), (0, ROWS, ROWS), (2, 2, 2), 56)
    total, above = lax.optimization_barrier((jnp.sum(pieces, axis=0), above))
    above = lax.ppermute(above, "lat", ring("lat", 1))

    copies = jnp.broadcast_to(total[None], pieces.shape)
    own = lax.all_to_all(copies, band, 0, 0).reshape(640, 128)
    feature_grad = add_border(part, cotangent, add_left, add_right, above)
    own, feature_grad = lax.optimization_barrier((own, feature_grad))
    other = lax.ppermute(own, "member", swap)
    mix_grad, hidden_grad, output_grad, bias, gain, hidden_bias = finish(me, own, other)
    return (
        feature_grad,
        mix_grad.reshape(128, 4, 128),
        bias.reshape(128),
        gain.reshape(128),
        hidden_grad,
        hidden_bias.reshape(256),
        output_grad,
    )


def solution(mesh):
    cells = P("member", "lat", None, "lon")
    return jax.shard_map(
        on_device,
        mesh=mesh,
        in_specs=(cells, cells) + (P(),) * 8,
        out_specs=(cells,) + (P(),) * 6,
        check_vma=False,
    )
```

```python
import functools
import math

import jax
import jax.numpy as jnp
from jax import lax
from jax.experimental import pallas as pl
from jax.experimental.pallas import tpu as pltpu
from jax.sharding import PartitionSpec as P

EPSILON = 1e-05
BF = jnp.bfloat16
F32 = jnp.float32
GELU_A = math.sqrt(2.0 / math.pi)
GELU_B = 0.044715
ROWS = 24
STEP_ROWS = 6
SIDE_ROWS = 8
STEPS = ROWS // STEP_ROWS + 1
HALO = 2


def nn(a, b):
    return lax.dot_general(a, b, (((1,), (0,)), ((), ())), preferred_element_type=F32)


def nt(a, b):
    return lax.dot_general(a, b, (((1,), (1,)), ((), ())), preferred_element_type=F32)


def build_filter(taps_ref, row, matrix_ref, slot):
    lanes = lax.broadcasted_iota(jnp.int32, (16, 128), 1)
    low = lanes < 64
    zero = jnp.zeros((16, 128), BF)
    for b in range(3):
        for k in range(4):
            base = taps_ref[row, pl.ds(b * 4 + k, 1), :]
            head = pltpu.roll(
                jnp.broadcast_to(base, (16, 128)), 0, 1, stride=1, stride_axis=0
            ).astype(BF)
            ring = [head] + [pltpu.roll(head, 16 * g, 1) for g in range(1, 8)]
            cols = pl.ds(k * 128, 128)
            own = pl.ds(b * 128, 128)
            matrix_ref[slot, own, cols] = jnp.concatenate(
                [jnp.where(low, head, zero), *ring[1:7], jnp.where(low, zero, ring[7])], axis=0
            )
            matrix_ref[slot, pl.ds(384 + b * 32, 32), cols] = jnp.concatenate(
                [jnp.where(low, ring[7], zero), jnp.where(low, zero, head)], axis=0
            )


def edges_kernel(low_ref, high_ref, low_cot_ref, high_cot_ref, to_above_ref, to_below_ref):
    for out_ref, rows, cot in (
        (to_above_ref, low_ref, low_cot_ref),
        (to_below_ref, high_ref, high_cot_ref),
    ):
        for m in range(2):
            out_ref[m, 0:128] = rows[m, 0]
            out_ref[m, 128:256] = rows[m, 1]
            out_ref[m, 256:384] = cot[m, 0]


def edges_of(feats, cot):
    rows = lambda count, at: pl.BlockSpec((2, count, 128, 128), lambda i: (0, at // count, 0, 0))
    full = pl.BlockSpec((2, 384, 128), lambda i: (0, 0, 0))
    edge = jax.ShapeDtypeStruct((2, 384, 128), BF)
    return pl.pallas_call(
        edges_kernel,
        grid=(1,),
        in_specs=[rows(2, 0), rows(2, ROWS - 2), rows(1, 0), rows(1, ROWS - 1)],
        out_specs=[full, full],
        out_shape=[edge, edge],
        compiler_params=pltpu.CompilerParams(vmem_limit_bytes=56 * 1024 * 1024),
        cost_estimate=pl.CostEstimate(flops=1_000, bytes_accessed=800_000, transcendentals=0),
    )(feats, feats, cot, cot)


def sides_kernel(feats_ref, above_ref, below_ref, to_right_ref, to_left_ref):
    step = pl.program_id(0)
    spot = lax.broadcasted_iota(jnp.int32, (32, 128), 0)
    spot = jnp.where(spot < 16, spot, spot + 96)
    pick = (lax.broadcasted_iota(jnp.int32, (32, 128), 1) == spot).astype(BF)

    def cut(row, blocks):
        turned = nt(pick, jnp.concatenate(blocks, axis=0)).astype(BF)
        for m in range(2):
            to_left_ref[m, row] = turned[:16, m * 128 : m * 128 + 128]
            to_right_ref[m, row] = turned[16:, m * 128 : m * 128 + 128]

    for at in range(SIDE_ROWS):
        cut(HALO + step * SIDE_ROWS + at, [feats_ref[0, at], feats_ref[1, at]])

    @pl.when(step == 0)
    def _():
        for first, ref in ((0, above_ref), (HALO + ROWS, below_ref)):
            for at in range(HALO):
                cut(first + at, [ref[m, at * 128 : at * 128 + 128] for m in range(2)])


def sides_of(feats, above, below):
    side = jax.ShapeDtypeStruct((2, ROWS + 2 * HALO, 16, 128), BF)
    full = pl.BlockSpec((2, ROWS + 2 * HALO, 16, 128), lambda i: (0, 0, 0, 0))
    edge = pl.BlockSpec((2, 384, 128), lambda i: (0, 0, 0))
    return pl.pallas_call(
        sides_kernel,
        grid=(ROWS // SIDE_ROWS,),
        in_specs=[
            pl.BlockSpec((2, SIDE_ROWS, 128, 128), lambda i: (0, i, 0, 0)),
            edge,
            edge,
        ],
        out_specs=[full, full],
        out_shape=[side, side],
        compiler_params=pltpu.CompilerParams(vmem_limit_bytes=24 * 1024 * 1024),
        cost_estimate=pl.CostEstimate(flops=50_000_000, bytes_accessed=2_000_000, transcendentals=0),
    )(feats, above, below)


def forward_kernel(
    me_ref,
    taps_ref,
    feats_ref,
    before_ref,
    after_ref,
    cot_ref,
    left_ref,
    right_ref,
    above_ref,
    below_ref,
    mix_ref,
    mix_bias_ref,
    gain_ref,
    hidden_ref,
    hidden_bias_ref,
    output_ref,
    mixed_round_ref,
    keep_ref,
    send_ref,
    mix,
    hidden_t,
    output_t,
    columns,
    sides,
    before,
    after,
    matrix,
    mix_acc,
    out_acc,
    hid_acc,
    mix_bias_acc,
    gain_acc,
    hidden_bias_acc,
    packed,
    *,
    scale,
):
    step = pl.program_id(0)
    last = step == STEPS - 1

    def work(bands, side_rows, cots, counted):
        count = len(bands)
        blocks = 2 * count
        cells = []
        for at in range(count):
            start = side_rows + at if counted else side_rows[at]
            build_filter(taps_ref, start, matrix, at)
            inputs = []
            for m in range(2):
                halo = jnp.concatenate(
                    [
                        sides[m, pl.ds(start, 3)].reshape(96, 128),
                        jnp.zeros((32, 128), BF),
                    ],
                    axis=0,
                )
                inputs.append(jnp.concatenate([*bands[at][m], halo.T], axis=1))
            filtered = nn(jnp.concatenate(inputs, axis=0), matrix[at]).astype(BF)
            for m in range(2):
                cells.append(
                    jnp.concatenate(
                        [
                            filtered[m * 128 : m * 128 + 128, k * 128 : k * 128 + 128]
                            for k in range(4)
                        ],
                        axis=0,
                    )
                )
        filtered = jnp.concatenate(cells, axis=1)
        wide = lambda low, high: jnp.concatenate([columns[low:high]] * blocks, axis=1)
        fold = lambda v: functools.reduce(
            lambda a, b: a + b, [v[:, n * 128 : n * 128 + 128] for n in range(blocks)]
        )
        mixed = nn(mix[...], filtered) + wide(0, 128)
        inverse = lax.rsqrt(jnp.mean(mixed * mixed, axis=0, keepdims=True) + EPSILON)
        scaled = mixed * inverse
        gain = wide(128, 256)
        normed = (scaled * gain).astype(BF)
        hidden = nn(hidden_ref[...], normed) + wide(256, 512)
        square = hidden * hidden
        tanh = jnp.tanh(hidden * (GELU_A + (GELU_A * GELU_B) * square))
        half = 0.5 + 0.5 * tanh
        value = hidden * half
        slope = half + value * (1.0 - half) * (2.0 * GELU_A + (6.0 * GELU_A * GELU_B) * square)
        cot = jnp.concatenate(cots, axis=1)
        pre_grad = slope * nn(output_t[...], cot)
        pre_round = pre_grad.astype(BF)
        normed_grad = nn(hidden_t[...], pre_round)
        grad = normed_grad * gain
        mixed_grad = inverse * (grad - scaled * jnp.mean(grad * scaled, axis=0, keepdims=True))
        mixed_round = mixed_grad.astype(BF)
        if counted:
            out_acc[...] += nt(cot, value.astype(BF))
            hid_acc[...] += nt(pre_round, normed)
            hidden_bias_acc[...] += fold(pre_grad)
            gain_acc[...] += fold(normed_grad * scaled)
            mix_bias_acc[...] += fold(mixed_grad)
            mix_acc[...] += nt(mixed_round, filtered)
        for at in range(count):
            mixed_round_ref[at] = mixed_round[:, at * 256 : at * 256 + 256]

    @pl.when(step == 0)
    def _():
        for m in range(2):
            sides[m, :, 0:16] = left_ref[m]
            sides[m, :, 16:32] = right_ref[m]
        matrix[...] = jnp.zeros_like(matrix)
        mix[...] = jnp.concatenate([mix_ref[:, k, :] for k in range(4)], axis=1)
        hidden_t[...] = hidden_ref[...].T
        output_t[...] = output_ref[...].T
        for at, line in enumerate(
            (mix_bias_ref[...], gain_ref[...], hidden_bias_ref[:, :128], hidden_bias_ref[:, 128:])
        ):
            columns[at * 128 : at * 128 + 128] = jnp.broadcast_to(line, (128, 128)).T
        for acc in (mix_acc, out_acc, hid_acc, mix_bias_acc, gain_acc, hidden_bias_acc):
            acc[...] = jnp.zeros_like(acc)
        mixed_round_ref[...] = jnp.zeros_like(mixed_round_ref)
        first = lambda ref, m: ref[m, 0:128]
        second = lambda ref, m: ref[m, 128:256]
        cot_of = lambda ref, m: ref[m, 256:384]
        work(
            [
                [(first(above_ref, m), second(above_ref, m), feats_ref[m, 0]) for m in range(2)],
                [(before_ref[m, 0], first(below_ref, m), second(below_ref, m)) for m in range(2)],
            ],
            (0, ROWS + 1),
            [cot_of(ref, m) for ref in (above_ref, below_ref) for m in range(2)],
            False,
        )

    @pl.when(step == 1)
    def _():
        for m in range(2):
            before[m] = above_ref[m, 128:256]

    @pl.when(step > 1)
    def _():
        before[...] = before_ref[:, 0]

    @pl.when(last)
    def _():
        for m in range(2):
            after[m] = below_ref[m, 0:128]

    @pl.when(jnp.logical_not(last))
    def _():
        after[...] = after_ref[:, 0]

    @pl.when(step > 0)
    def _():
        band = [
            [before[m], *[feats_ref[m, r] for r in range(STEP_ROWS)], after[m]] for m in range(2)
        ]
        work(
            [[tuple(band[m][at : at + 3]) for m in range(2)] for at in range(STEP_ROWS)],
            (step - 1) * STEP_ROWS + 1,
            [cot_ref[m, at] for at in range(STEP_ROWS) for m in range(2)],
            True,
        )

    @pl.when(last)
    def _():
        for k in range(4):
            packed[pl.ds(k, 128, stride=4), :] = mix_acc[:, k * 128 : k * 128 + 128] * scale
        packed[512:768] = hid_acc[...] * scale
        for f in range(2):
            packed[768 + f * 128 : 896 + f * 128] = out_acc[:, f * 128 : f * 128 + 128] * scale
        lanes = lax.broadcasted_iota(jnp.int32, (128, 128), 1)
        small = jnp.zeros((128, 128), F32)
        for at, part in enumerate(
            (mix_bias_acc[...], gain_acc[...], hidden_bias_acc[0:128], hidden_bias_acc[128:256])
        ):
            total = jnp.sum(part, axis=1, keepdims=True) * scale
            small = jnp.where(lanes == at, total, small)
        mine = me_ref[0]
        for ref, half in ((keep_ref, mine), (send_ref, 1 - mine)):
            for p in range(64):
                at = pl.multiple_of(half * 512 + p * 8, 8)
                ref[p * 10 : p * 10 + 8] = packed[pl.ds(at, 8), :]
                ref[p * 10 + 8 : p * 10 + 10] = small[2 * p : 2 * p + 2]


def forward(me, taps, feats, cot, left, right, above, below, weights, scale):
    whole = lambda v: pl.BlockSpec(v.shape, lambda i: (0,) * v.ndim)
    rows = lambda count, first: pl.BlockSpec(
        (2, count, 128, 128), lambda i: (0, first(i), 0, 0)
    )
    own = rows(STEP_ROWS, lambda i: jnp.maximum(i - 1, 0))
    ahead = lambda i: jnp.where(i == 0, ROWS - 1, jnp.maximum((i - 1) * STEP_ROWS - 1, 0))
    return pl.pallas_call(
        functools.partial(forward_kernel, scale=scale),
        grid=(STEPS,),
        in_specs=[
            pl.BlockSpec(memory_space=pltpu.SMEM),
            pl.BlockSpec((ROWS + 2, 12, 128), lambda i: (0, 0, 0)),
            own,
            rows(1, ahead),
            rows(1, lambda i: jnp.minimum(i * STEP_ROWS, ROWS - 1)),
            own,
            whole(left),
            whole(right),
            whole(above),
            whole(below),
            *[whole(v) for v in weights],
        ],
        out_specs=[
            pl.BlockSpec((STEP_ROWS, 128, 256), lambda i: (i, 0, 0)),
            pl.BlockSpec((640, 128), lambda i: (0, 0)),
            pl.BlockSpec((640, 128), lambda i: (0, 0)),
        ],
        out_shape=[
            jax.ShapeDtypeStruct((STEPS * STEP_ROWS, 128, 256), BF),
            jax.ShapeDtypeStruct((640, 128), F32),
            jax.ShapeDtypeStruct((640, 128), F32),
        ],
        scratch_shapes=[
            pltpu.VMEM((128, 512), BF),
            pltpu.VMEM((128, 256), BF),
            pltpu.VMEM((256, 128), BF),
            pltpu.VMEM((512, 128), F32),
            pltpu.VMEM((2, ROWS + 2 * HALO, 32, 128), BF),
            pltpu.VMEM((2, 128, 128), BF),
            pltpu.VMEM((2, 128, 128), BF),
            pltpu.VMEM((STEP_ROWS, 512, 512), BF),
            pltpu.VMEM((128, 512), F32),
            pltpu.VMEM((128, 256), F32),
            pltpu.VMEM((256, 128), F32),
            pltpu.VMEM((128, 128), F32),
            pltpu.VMEM((128, 128), F32),
            pltpu.VMEM((256, 128), F32),
            pltpu.VMEM((1024, 128), F32),
        ],
        compiler_params=pltpu.CompilerParams(vmem_limit_bytes=32 * 1024 * 1024),
        cost_estimate=pl.CostEstimate(
            flops=15_000_000_000, bytes_accessed=8_000_000, transcendentals=1_600_000
        ),
    )(me, taps, feats, feats, feats, cot, left, right, above, below, *weights)


def backward_kernel(
    taps_ref,
    mixed_round_ref,
    mix_ref,
    part_ref,
    to_left_ref,
    to_right_ref,
    acc,
    sides,
    matrix,
    mix_t,
    sems,
):
    step = pl.program_id(0)

    def spread_row(at, targets, row):
        build_filter(taps_ref, row + 1, matrix, at)
        grads = nn(mix_t[...], mixed_round_ref[at]).astype(BF)
        arranged = jnp.concatenate(
            [
                jnp.concatenate(
                    [grads[k * 128 : k * 128 + 128, m * 128 : m * 128 + 128] for k in range(4)],
                    axis=1,
                )
                for m in range(2)
            ],
            axis=0,
        )
        low, high = targets[0], targets[-1] + 1
        spread = nt(arranged, matrix[at, low * 128 : high * 128])
        halo = nt(matrix[at, 384:512], arranged)
        for m in range(2):
            for b in targets:
                cols = slice((b - low) * 128, (b - low) * 128 + 128)
                acc[m, row + b] += spread[m * 128 : m * 128 + 128, cols]
                sides[m, row + b] += halo[b * 32 : b * 32 + 32, m * 128 : m * 128 + 128]

    @pl.when(step == 0)
    def _():
        acc[...] = jnp.zeros_like(acc)
        sides[...] = jnp.zeros_like(sides)
        matrix[...] = jnp.zeros_like(matrix)
        for k in range(4):
            mix_t[k * 128 : k * 128 + 128] = mix_ref[:, k, :].T
        spread_row(0, (2,), -1)
        spread_row(1, (0,), ROWS)

    @pl.when(step > 0)
    def _():
        for at in range(STEP_ROWS):
            spread_row(at, (0, 1, 2), (step - 1) * STEP_ROWS + at)

    def write(at):
        low = max((at - 1) * STEP_ROWS - 1, 0)
        high = ROWS if at == STEPS - 1 else at * STEP_ROWS - 1
        return pltpu.make_async_copy(
            acc.at[:, 1 + low : 1 + high], part_ref.at[:, low:high], sems.at[at - 1]
        )

    for at in range(1, STEPS):
        pl.when(step == at)(lambda: write(at).start())

    @pl.when(step == STEPS - 1)
    def _():
        to_left_ref[...] = sides[:, 1 : ROWS + 1, 0:16].astype(BF)
        to_right_ref[...] = sides[:, 1 : ROWS + 1, 16:32].astype(BF)
        for at in range(1, STEPS):
            write(at).wait()


def backward(taps, mixed_round, mix):
    whole = lambda *shape: pl.BlockSpec(shape, lambda i: (0,) * len(shape))
    side = jax.ShapeDtypeStruct((2, ROWS, 16, 128), BF)
    return pl.pallas_call(
        backward_kernel,
        grid=(STEPS,),
        in_specs=[
            pl.BlockSpec((ROWS + 2, 12, 128), lambda i: (0, 0, 0)),
            pl.BlockSpec((STEP_ROWS, 128, 256), lambda i: (i, 0, 0)),
            whole(128, 4, 128),
        ],
        out_specs=[
            pl.BlockSpec(memory_space=pltpu.MemorySpace.HBM),
            whole(2, ROWS, 16, 128),
            whole(2, ROWS, 16, 128),
        ],
        out_shape=[jax.ShapeDtypeStruct((2, ROWS, 128, 128), F32), side, side],
        scratch_shapes=[
            pltpu.VMEM((2, ROWS + 2, 128, 128), F32),
            pltpu.VMEM((2, ROWS + 2, 32, 128), F32),
            pltpu.VMEM((STEP_ROWS, 512, 512), BF),
            pltpu.VMEM((512, 128), BF),
            pltpu.SemaphoreType.DMA((STEPS - 1,)),
        ],
        compiler_params=pltpu.CompilerParams(vmem_limit_bytes=40 * 1024 * 1024),
        cost_estimate=pl.CostEstimate(
            flops=7_500_000_000, bytes_accessed=8_000_000, transcendentals=0
        ),
    )(taps, mixed_round, mix)


BORDER_ROWS = 4


def border_kernel(part_ref, cot_ref, left_ref, right_ref, out_ref):
    gap = jnp.zeros((96, 128), BF)
    turn = lambda low, high: jnp.concatenate([low, gap, high], axis=0).T.astype(F32)
    for m in range(2):
        for at in range(BORDER_ROWS):
            out_ref[m, at] = (part_ref[m, at] + cot_ref[m, at].astype(F32)) + turn(
                left_ref[m, at], right_ref[m, at]
            )


def add_border(part, cot, left, right):
    rows = lambda *tail: pl.BlockSpec((2, BORDER_ROWS, *tail), lambda i: (0, i, 0, 0))
    return pl.pallas_call(
        border_kernel,
        grid=(ROWS // BORDER_ROWS,),
        in_specs=[
            rows(128, 128),
            rows(128, 128),
            rows(16, 128),
            rows(16, 128),
        ],
        out_specs=rows(128, 128),
        out_shape=jax.ShapeDtypeStruct((2, ROWS, 128, 128), F32),
        compiler_params=pltpu.CompilerParams(vmem_limit_bytes=56 * 1024 * 1024),
        cost_estimate=pl.CostEstimate(flops=1_000_000, bytes_accessed=7_000_000, transcendentals=0),
    )(part, cot, left, right)


def finish_kernel(
    me_ref, own_ref, other_ref, mix_ref, hidden_ref, output_ref, bias_ref, gain_ref, hidden_bias_ref
):
    def place(first_ref, second_ref):
        for p in range(64):
            mix_ref[p * 8 : p * 8 + 8] = first_ref[p * 10 : p * 10 + 8]
            rest = second_ref[p * 10 : p * 10 + 8]
            if p < 32:
                hidden_ref[p * 8 : p * 8 + 8] = rest
            else:
                at, half = (p - 32) % 16, (p - 32) // 16
                output_ref[at * 8 : at * 8 + 8, half * 128 : half * 128 + 128] = rest

    pl.when(me_ref[0] == 0)(lambda: place(own_ref, other_ref))
    pl.when(me_ref[0] == 1)(lambda: place(other_ref, own_ref))
    small = jnp.concatenate([own_ref[p * 10 + 8 : p * 10 + 10] for p in range(64)], axis=0)
    small = small.T
    bias_ref[...] = small[0:1]
    gain_ref[...] = small[1:2]
    hidden_bias_ref[...] = jnp.concatenate([small[2:3], small[3:4]], axis=1)


def finish(me, own, other):
    return pl.pallas_call(
        finish_kernel,
        in_specs=[pl.BlockSpec(memory_space=pltpu.SMEM)]
        + [pl.BlockSpec(memory_space=pltpu.VMEM)] * 2,
        out_shape=[
            jax.ShapeDtypeStruct((512, 128), F32),
            jax.ShapeDtypeStruct((256, 128), F32),
            jax.ShapeDtypeStruct((128, 256), F32),
            jax.ShapeDtypeStruct((1, 128), F32),
            jax.ShapeDtypeStruct((1, 128), F32),
            jax.ShapeDtypeStruct((1, 256), F32),
        ],
        compiler_params=pltpu.CompilerParams(vmem_limit_bytes=24 * 1024 * 1024),
        cost_estimate=pl.CostEstimate(flops=1_000_000, bytes_accessed=1_200_000, transcendentals=0),
    )(me, own, other)


def ring(axis, shift):
    count = lax.axis_size(axis)
    return [(i, (i + shift) % count) for i in range(count)]


def ring_taps(basis_table, halo_depth):
    total = basis_table.shape[0]
    first = lax.axis_index("lat") * ROWS
    rows = (first - 1 + jnp.arange(ROWS + 2, dtype=jnp.int32) + total) % total
    closed = lambda v: jnp.concatenate([v[-1:], v, v[:1]], axis=0)
    chosen = lax.dynamic_slice_in_dim(closed(basis_table), first, ROWS + 2, 0)
    limits = lax.dynamic_slice_in_dim(closed(halo_depth), first, ROWS + 2, 0)
    taps = jnp.arange(33, dtype=jnp.int32)
    keep = jnp.abs(taps - 16)[None, :] <= limits[:, None]
    offsets = jnp.arange(3, dtype=jnp.int32)[None, :] + rows[:, None]
    inside = (offsets >= 1) & (offsets <= total)
    keep = keep[:, None, None, :] & inside[:, None, :, None]
    kept = jnp.where(keep, chosen, jnp.zeros_like(chosen)).astype(F32)
    spots = (16 - jnp.arange(128, dtype=jnp.int32)) % 128
    place = (taps[:, None] == spots[None, :]).astype(kept.dtype)
    lines = jnp.einsum("rkbt,tv->rbkv", kept, place, preferred_element_type=F32)
    return lines.reshape(ROWS + 2, 12, 128)


def on_device(
    features,
    cotangent,
    basis_table,
    halo_depth,
    mix_weight,
    mix_bias,
    norm_gain,
    hidden_weight,
    hidden_bias,
    output_weight,
):
    to_above, to_below = edges_of(features, cotangent)
    above = lax.ppermute(to_below, "lat", ring("lat", 1))
    below = lax.ppermute(to_above, "lat", ring("lat", -1))
    to_right, to_left = sides_of(features, above, below)
    left = lax.ppermute(to_right, "lon", ring("lon", 1))
    right = lax.ppermute(to_left, "lon", ring("lon", -1))
    taps = ring_taps(basis_table, halo_depth)

    me = lax.axis_index("member").reshape(1).astype(jnp.int32)
    cell_total = 2 * ROWS * 128 * lax.axis_size(("member", "lat", "lon"))
    weights = (
        mix_weight,
        mix_bias[None],
        norm_gain[None],
        hidden_weight,
        hidden_bias[None],
        output_weight,
    )
    scale = 1.0 / math.sqrt(cell_total)
    mixed_round, keep, send = forward(
        me, taps, features, cotangent, left, right, above, below, weights, scale
    )
    swap = [(0, 1), (1, 0)]
    band = ("lat", "lon")
    peers = lax.axis_size(band)
    pair = keep + lax.ppermute(send, "member", swap)
    pair, mixed_round = lax.optimization_barrier((pair, mixed_round))
    pieces = lax.all_to_all(pair.reshape(peers, 640 // peers, 1, 128), band, 0, 0)
    part, to_left, to_right = backward(taps, mixed_round, mix_weight)
    add_left = lax.ppermute(to_right, "lon", ring("lon", 1))
    add_right = lax.ppermute(to_left, "lon", ring("lon", -1))
    total, add_left, add_right = lax.optimization_barrier(
        (jnp.sum(pieces, axis=0), add_left, add_right)
    )

    copies = jnp.broadcast_to(total[None], pieces.shape)
    own = lax.all_to_all(copies, band, 0, 0).reshape(640, 128)
    feature_grad = add_border(part, cotangent, add_left, add_right)
    own, feature_grad = lax.optimization_barrier((own, feature_grad))
    other = lax.ppermute(own, "member", swap)
    mix_grad, hidden_grad, output_grad, bias, gain, hidden_bias = finish(me, own, other)
    return (
        feature_grad,
        mix_grad.reshape(128, 4, 128),
        bias.reshape(128),
        gain.reshape(128),
        hidden_grad,
        hidden_bias.reshape(256),
        output_grad,
    )


def solution(mesh):
    cells = P("member", "lat", None, "lon")
    return jax.shard_map(
        on_device,
        mesh=mesh,
        in_specs=(cells, cells) + (P(),) * 8,
        out_specs=(cells,) + (P(),) * 6,
        check_vma=False,
    )
```

```python
import functools
import math

import jax
import jax.numpy as jnp
from jax import lax
from jax.experimental import pallas as pl
from jax.experimental.pallas import tpu as pltpu
from jax.sharding import PartitionSpec as P

EPSILON = 1e-05
BF = jnp.bfloat16
F32 = jnp.float32
GELU_A = math.sqrt(2.0 / math.pi)
GELU_B = 0.044715
ROWS = 24
STEP_ROWS = 6
SIDE_ROWS = 8
STEPS = ROWS // STEP_ROWS + 1
HALO = 2


def nn(a, b):
    return lax.dot_general(a, b, (((1,), (0,)), ((), ())), preferred_element_type=F32)


def nt(a, b):
    return lax.dot_general(a, b, (((1,), (1,)), ((), ())), preferred_element_type=F32)


def build_filter(taps_ref, row, matrix_ref, slot):
    lanes = lax.broadcasted_iota(jnp.int32, (16, 128), 1)
    low = lanes < 64
    zero = jnp.zeros((16, 128), BF)
    for b in range(3):
        for k in range(4):
            base = taps_ref[b * 4 + k, pl.ds(row, 1), :]
            head = pltpu.roll(
                jnp.broadcast_to(base, (16, 128)), 0, 1, stride=1, stride_axis=0
            ).astype(BF)
            ring = [head] + [pltpu.roll(head, 16 * g, 1) for g in range(1, 8)]
            cols = pl.ds(k * 128, 128)
            own = pl.ds(b * 128, 128)
            matrix_ref[slot, own, cols] = jnp.concatenate(
                [jnp.where(low, head, zero), *ring[1:7], jnp.where(low, zero, ring[7])], axis=0
            )
            matrix_ref[slot, pl.ds(384 + b * 32, 32), cols] = jnp.concatenate(
                [jnp.where(low, ring[7], zero), jnp.where(low, zero, head)], axis=0
            )


def edges_kernel(feats_ref, cot_ref, to_above_ref, to_below_ref, sems):
    copies = []
    for out_ref, first, outer in ((to_above_ref, 0, 0), (to_below_ref, ROWS - 2, ROWS - 1)):
        copies.append((feats_ref.at[:, first : first + 2], out_ref.at[:, 0:2]))
        copies.append((cot_ref.at[:, outer : outer + 1], out_ref.at[:, 2:3]))
    copies = [pltpu.make_async_copy(*c, sems.at[n]) for n, c in enumerate(copies)]
    for copy in copies:
        copy.start()
    for copy in copies:
        copy.wait()


def edges_of(feats, cot):
    anywhere = pl.BlockSpec(memory_space=pl.ANY)
    edge = jax.ShapeDtypeStruct((2, 3, 128, 128), BF)
    return pl.pallas_call(
        edges_kernel,
        in_specs=[anywhere, anywhere],
        out_specs=[anywhere, anywhere],
        out_shape=[edge, edge],
        scratch_shapes=[pltpu.SemaphoreType.DMA((4,))],
        compiler_params=pltpu.CompilerParams(vmem_limit_bytes=56 * 1024 * 1024),
        cost_estimate=pl.CostEstimate(flops=1_000, bytes_accessed=800_000, transcendentals=0),
    )(feats, cot)


def prepare_kernel(
    first_ref,
    basis_ref,
    depth_ref,
    mix_ref,
    mix_bias_ref,
    gain_ref,
    hidden_ref,
    hidden_bias_ref,
    output_ref,
    lines_ref,
    mix_out_ref,
    hidden_t_ref,
    output_t_ref,
    columns_ref,
):
    total = depth_ref.shape[1]
    iota = lambda shape, axis: lax.broadcasted_iota(jnp.int32, shape, axis)
    row = lax.rem(iota((32, total), 0) + (first_ref[0] + total - 1), total)
    chosen = (iota((32, total), 1) == row).astype(F32)
    depth = jnp.sum(chosen * depth_ref[...].astype(F32), axis=1, keepdims=True)
    chosen = chosen.astype(BF)
    taps = iota((32, 33), 1)
    near = jnp.abs(taps - 16).astype(F32) <= depth
    place = (lax.rem(16 - iota((33, 128), 1) + 128, 128) == iota((33, 128), 0)).astype(BF)
    own = lax.rem(iota((32, 33), 0) + (first_ref[0] + total - 1), total)
    for b in range(3):
        keep = near & (own + b >= 1) & (own + b <= total)
        for k in range(4):
            kept = jnp.where(keep, nt(chosen, basis_ref[b, :, k, :]), 0.0).astype(BF)
            lines_ref[b * 4 + k] = nn(kept, place)
    mix_out_ref[...] = jnp.concatenate([mix_ref[:, k, :] for k in range(4)], axis=1)
    hidden_t_ref[...] = hidden_ref[...].T
    output_t_ref[...] = output_ref[...].T
    for at, line in enumerate(
        (mix_bias_ref[...], gain_ref[...], hidden_bias_ref[:, :128], hidden_bias_ref[:, 128:])
    ):
        columns_ref[at * 128 : at * 128 + 128] = jnp.broadcast_to(line, (128, 128)).T


def prepare(first, basis, depth, mix, mix_bias, gain, hidden, hidden_bias, output):
    vmem = pl.BlockSpec(memory_space=pltpu.VMEM)
    return pl.pallas_call(
        prepare_kernel,
        in_specs=[pl.BlockSpec(memory_space=pltpu.SMEM)] + [vmem] * 8,
        out_specs=[vmem] * 5,
        out_shape=[
            jax.ShapeDtypeStruct((12, 32, 128), F32),
            jax.ShapeDtypeStruct((128, 512), BF),
            jax.ShapeDtypeStruct((128, 256), BF),
            jax.ShapeDtypeStruct((256, 128), BF),
            jax.ShapeDtypeStruct((512, 128), F32),
        ],
        compiler_params=pltpu.CompilerParams(vmem_limit_bytes=58 * 1024 * 1024),
        cost_estimate=pl.CostEstimate(
            flops=300_000_000, bytes_accessed=2_000_000, transcendentals=0
        ),
    )(
        first,
        basis.transpose(2, 3, 1, 0),
        depth[None],
        mix,
        mix_bias[None],
        gain[None],
        hidden,
        hidden_bias[None],
        output,
    )


def sides_kernel(feats_ref, above_ref, below_ref, to_right_ref, to_left_ref):
    step = pl.program_id(0)
    spot = lax.broadcasted_iota(jnp.int32, (32, 128), 0)
    spot = jnp.where(spot < 16, spot, spot + 96)
    pick = (lax.broadcasted_iota(jnp.int32, (32, 128), 1) == spot).astype(BF)

    def cut(row, blocks):
        turned = nt(pick, jnp.concatenate(blocks, axis=0)).astype(BF)
        for m in range(2):
            to_left_ref[m, row] = turned[:16, m * 128 : m * 128 + 128]
            to_right_ref[m, row] = turned[16:, m * 128 : m * 128 + 128]

    for at in range(SIDE_ROWS):
        cut(HALO + step * SIDE_ROWS + at, [feats_ref[0, at], feats_ref[1, at]])

    @pl.when(step == 0)
    def _():
        for first, ref in ((0, above_ref), (HALO + ROWS, below_ref)):
            for at in range(HALO):
                cut(first + at, [ref[m, at] for m in range(2)])


def sides_of(feats, above, below):
    side = jax.ShapeDtypeStruct((2, ROWS + 2 * HALO, 16, 128), BF)
    full = pl.BlockSpec((2, ROWS + 2 * HALO, 16, 128), lambda i: (0, 0, 0, 0))
    edge = pl.BlockSpec((2, 3, 128, 128), lambda i: (0, 0, 0, 0))
    return pl.pallas_call(
        sides_kernel,
        grid=(ROWS // SIDE_ROWS,),
        in_specs=[
            pl.BlockSpec((2, SIDE_ROWS, 128, 128), lambda i: (0, i, 0, 0)),
            edge,
            edge,
        ],
        out_specs=[full, full],
        out_shape=[side, side],
        compiler_params=pltpu.CompilerParams(vmem_limit_bytes=24 * 1024 * 1024),
        cost_estimate=pl.CostEstimate(flops=50_000_000, bytes_accessed=2_000_000, transcendentals=0),
    )(feats, above, below)


def forward_kernel(
    me_ref,
    taps_ref,
    feats_ref,
    before_ref,
    after_ref,
    cot_ref,
    left_ref,
    right_ref,
    above_ref,
    below_ref,
    hidden_ref,
    mix,
    hidden_t,
    output_t,
    columns,
    mixed_round_ref,
    keep_ref,
    send_ref,
    sides,
    before,
    after,
    matrix,
    mix_acc,
    out_acc,
    hid_acc,
    mix_bias_acc,
    gain_acc,
    hidden_bias_acc,
    packed,
    *,
    scale,
):
    step = pl.program_id(0)
    last = step == STEPS - 1

    def work(bands, side_rows, cots, counted):
        count = len(bands)
        blocks = 2 * count
        cells = []
        for at in range(count):
            start = side_rows + at if counted else side_rows[at]
            build_filter(taps_ref, start, matrix, at)
            inputs = []
            for m in range(2):
                halo = jnp.concatenate(
                    [
                        sides[m, pl.ds(start, 3)].reshape(96, 128),
                        jnp.zeros((32, 128), BF),
                    ],
                    axis=0,
                )
                inputs.append(jnp.concatenate([*bands[at][m], halo.T], axis=1))
            filtered = nn(jnp.concatenate(inputs, axis=0), matrix[at]).astype(BF)
            for m in range(2):
                cells.append(
                    jnp.concatenate(
                        [
                            filtered[m * 128 : m * 128 + 128, k * 128 : k * 128 + 128]
                            for k in range(4)
                        ],
                        axis=0,
                    )
                )
        filtered = jnp.concatenate(cells, axis=1)
        wide = lambda low, high: jnp.concatenate([columns[low:high]] * blocks, axis=1)
        fold = lambda v: functools.reduce(
            lambda a, b: a + b, [v[:, n * 128 : n * 128 + 128] for n in range(blocks)]
        )
        mixed = nn(mix[...], filtered) + wide(0, 128)
        inverse = lax.rsqrt(jnp.mean(mixed * mixed, axis=0, keepdims=True) + EPSILON)
        scaled = mixed * inverse
        gain = wide(128, 256)
        normed = (scaled * gain).astype(BF)
        hidden = nn(hidden_ref[...], normed) + wide(256, 512)
        square = hidden * hidden
        tanh = jnp.tanh(hidden * (GELU_A + (GELU_A * GELU_B) * square))
        half = 0.5 + 0.5 * tanh
        value = hidden * half
        slope = half + value * (1.0 - half) * (2.0 * GELU_A + (6.0 * GELU_A * GELU_B) * square)
        cot = jnp.concatenate(cots, axis=1)
        pre_grad = slope * nn(output_t[...], cot)
        pre_round = pre_grad.astype(BF)
        normed_grad = nn(hidden_t[...], pre_round)
        grad = normed_grad * gain
        mixed_grad = inverse * (grad - scaled * jnp.mean(grad * scaled, axis=0, keepdims=True))
        mixed_round = mixed_grad.astype(BF)
        if counted:
            out_acc[...] += nt(cot, value.astype(BF))
            hid_acc[...] += nt(pre_round, normed)
            hidden_bias_acc[...] += fold(pre_grad)
            gain_acc[...] += fold(normed_grad * scaled)
            mix_bias_acc[...] += fold(mixed_grad)
            mix_acc[...] += nt(mixed_round, filtered)
        for at in range(count):
            mixed_round_ref[at] = mixed_round[:, at * 256 : at * 256 + 256]

    @pl.when(step == 0)
    def _():
        for m in range(2):
            sides[m, :, 0:16] = left_ref[m]
            sides[m, :, 16:32] = right_ref[m]
        matrix[...] = jnp.zeros_like(matrix)
        for acc in (mix_acc, out_acc, hid_acc, mix_bias_acc, gain_acc, hidden_bias_acc):
            acc[...] = jnp.zeros_like(acc)
        mixed_round_ref[...] = jnp.zeros_like(mixed_round_ref)
        first = lambda ref, m: ref[m, 0]
        second = lambda ref, m: ref[m, 1]
        cot_of = lambda ref, m: ref[m, 2]
        work(
            [
                [(first(above_ref, m), second(above_ref, m), feats_ref[m, 0]) for m in range(2)],
                [(before_ref[m, 0], first(below_ref, m), second(below_ref, m)) for m in range(2)],
            ],
            (0, ROWS + 1),
            [cot_of(ref, m) for ref in (above_ref, below_ref) for m in range(2)],
            False,
        )

    @pl.when(step == 1)
    def _():
        for m in range(2):
            before[m] = above_ref[m, 1]

    @pl.when(step > 1)
    def _():
        before[...] = before_ref[:, 0]

    @pl.when(last)
    def _():
        for m in range(2):
            after[m] = below_ref[m, 0]

    @pl.when(jnp.logical_not(last))
    def _():
        after[...] = after_ref[:, 0]

    @pl.when(step > 0)
    def _():
        band = [
            [before[m], *[feats_ref[m, r] for r in range(STEP_ROWS)], after[m]] for m in range(2)
        ]
        work(
            [[tuple(band[m][at : at + 3]) for m in range(2)] for at in range(STEP_ROWS)],
            (step - 1) * STEP_ROWS + 1,
            [cot_ref[m, at] for at in range(STEP_ROWS) for m in range(2)],
            True,
        )

    @pl.when(last)
    def _():
        for k in range(4):
            packed[pl.ds(k, 128, stride=4), :] = mix_acc[:, k * 128 : k * 128 + 128] * scale
        packed[512:768] = hid_acc[...] * scale
        for f in range(2):
            packed[768 + f * 128 : 896 + f * 128] = out_acc[:, f * 128 : f * 128 + 128] * scale
        lanes = lax.broadcasted_iota(jnp.int32, (128, 128), 1)
        small = jnp.zeros((128, 128), F32)
        for at, part in enumerate(
            (mix_bias_acc[...], gain_acc[...], hidden_bias_acc[0:128], hidden_bias_acc[128:256])
        ):
            total = jnp.sum(part, axis=1, keepdims=True) * scale
            small = jnp.where(lanes == at, total, small)
        mine = me_ref[0]
        for ref, half in ((keep_ref, mine), (send_ref, 1 - mine)):
            for p in range(64):
                at = pl.multiple_of(half * 512 + p * 8, 8)
                ref[p * 10 : p * 10 + 8] = packed[pl.ds(at, 8), :]
                ref[p * 10 + 8 : p * 10 + 10] = small[2 * p : 2 * p + 2]


def forward(me, taps, feats, cot, left, right, above, below, weights, scale):
    whole = lambda v: pl.BlockSpec(v.shape, lambda i: (0,) * v.ndim)
    rows = lambda count, first: pl.BlockSpec(
        (2, count, 128, 128), lambda i: (0, first(i), 0, 0)
    )
    own = rows(STEP_ROWS, lambda i: jnp.maximum(i - 1, 0))
    ahead = lambda i: jnp.where(i == 0, ROWS - 1, jnp.maximum((i - 1) * STEP_ROWS - 1, 0))
    return pl.pallas_call(
        functools.partial(forward_kernel, scale=scale),
        grid=(STEPS,),
        in_specs=[
            pl.BlockSpec(memory_space=pltpu.SMEM),
            pl.BlockSpec((12, 32, 128), lambda i: (0, 0, 0)),
            own,
            rows(1, ahead),
            rows(1, lambda i: jnp.minimum(i * STEP_ROWS, ROWS - 1)),
            own,
            whole(left),
            whole(right),
            whole(above),
            whole(below),
            *[whole(v) for v in weights],
        ],
        out_specs=[
            pl.BlockSpec((STEP_ROWS, 128, 256), lambda i: (i, 0, 0)),
            pl.BlockSpec((640, 128), lambda i: (0, 0)),
            pl.BlockSpec((640, 128), lambda i: (0, 0)),
        ],
        out_shape=[
            jax.ShapeDtypeStruct((STEPS * STEP_ROWS, 128, 256), BF),
            jax.ShapeDtypeStruct((640, 128), F32),
            jax.ShapeDtypeStruct((640, 128), F32),
        ],
        scratch_shapes=[
            pltpu.VMEM((2, ROWS + 2 * HALO, 32, 128), BF),
            pltpu.VMEM((2, 128, 128), BF),
            pltpu.VMEM((2, 128, 128), BF),
            pltpu.VMEM((STEP_ROWS, 512, 512), BF),
            pltpu.VMEM((128, 512), F32),
            pltpu.VMEM((128, 256), F32),
            pltpu.VMEM((256, 128), F32),
            pltpu.VMEM((128, 128), F32),
            pltpu.VMEM((128, 128), F32),
            pltpu.VMEM((256, 128), F32),
            pltpu.VMEM((1024, 128), F32),
        ],
        compiler_params=pltpu.CompilerParams(vmem_limit_bytes=58 * 1024 * 1024),
        cost_estimate=pl.CostEstimate(
            flops=15_000_000_000, bytes_accessed=8_000_000, transcendentals=1_600_000
        ),
    )(me, taps, feats, feats, feats, cot, left, right, above, below, *weights)


def backward_kernel(
    taps_ref,
    mixed_round_ref,
    mix_ref,
    part_ref,
    to_left_ref,
    to_right_ref,
    acc,
    sides,
    matrix,
    mix_t,
    sems,
):
    step = pl.program_id(0)

    def spread_row(at, targets, row):
        build_filter(taps_ref, row + 1, matrix, at)
        grads = nn(mix_t[...], mixed_round_ref[at]).astype(BF)
        arranged = jnp.concatenate(
            [
                jnp.concatenate(
                    [grads[k * 128 : k * 128 + 128, m * 128 : m * 128 + 128] for k in range(4)],
                    axis=1,
                )
                for m in range(2)
            ],
            axis=0,
        )
        low, high = targets[0], targets[-1] + 1
        spread = nt(arranged, matrix[at, low * 128 : high * 128])
        halo = nt(matrix[at, 384:512], arranged)
        for m in range(2):
            for b in targets:
                cols = slice((b - low) * 128, (b - low) * 128 + 128)
                acc[m, row + b] += spread[m * 128 : m * 128 + 128, cols]
                sides[m, row + b] += halo[b * 32 : b * 32 + 32, m * 128 : m * 128 + 128]

    @pl.when(step == 0)
    def _():
        acc[...] = jnp.zeros_like(acc)
        sides[...] = jnp.zeros_like(sides)
        matrix[...] = jnp.zeros_like(matrix)
        for k in range(4):
            mix_t[k * 128 : k * 128 + 128] = mix_ref[:, k * 128 : k * 128 + 128].T
        spread_row(0, (2,), -1)
        spread_row(1, (0,), ROWS)

    @pl.when(step > 0)
    def _():
        for at in range(STEP_ROWS):
            spread_row(at, (0, 1, 2), (step - 1) * STEP_ROWS + at)

    def write(at):
        low = max((at - 1) * STEP_ROWS - 1, 0)
        high = ROWS if at == STEPS - 1 else at * STEP_ROWS - 1
        return pltpu.make_async_copy(
            acc.at[:, 1 + low : 1 + high], part_ref.at[:, low:high], sems.at[at - 1]
        )

    for at in range(1, STEPS):
        pl.when(step == at)(lambda: write(at).start())

    @pl.when(step == STEPS - 1)
    def _():
        to_left_ref[...] = sides[:, 1 : ROWS + 1, 0:16].astype(BF)
        to_right_ref[...] = sides[:, 1 : ROWS + 1, 16:32].astype(BF)
        for at in range(1, STEPS):
            write(at).wait()


def backward(taps, mixed_round, mix):
    whole = lambda *shape: pl.BlockSpec(shape, lambda i: (0,) * len(shape))
    side = jax.ShapeDtypeStruct((2, ROWS, 16, 128), BF)
    return pl.pallas_call(
        backward_kernel,
        grid=(STEPS,),
        in_specs=[
            pl.BlockSpec((12, 32, 128), lambda i: (0, 0, 0)),
            pl.BlockSpec((STEP_ROWS, 128, 256), lambda i: (i, 0, 0)),
            whole(128, 512),
        ],
        out_specs=[
            pl.BlockSpec(memory_space=pltpu.MemorySpace.HBM),
            whole(2, ROWS, 16, 128),
            whole(2, ROWS, 16, 128),
        ],
        out_shape=[jax.ShapeDtypeStruct((2, ROWS, 128, 128), F32), side, side],
        scratch_shapes=[
            pltpu.VMEM((2, ROWS + 2, 128, 128), F32),
            pltpu.VMEM((2, ROWS + 2, 32, 128), F32),
            pltpu.VMEM((STEP_ROWS, 512, 512), BF),
            pltpu.VMEM((512, 128), BF),
            pltpu.SemaphoreType.DMA((STEPS - 1,)),
        ],
        compiler_params=pltpu.CompilerParams(vmem_limit_bytes=58 * 1024 * 1024),
        cost_estimate=pl.CostEstimate(
            flops=7_500_000_000, bytes_accessed=8_000_000, transcendentals=0
        ),
    )(taps, mixed_round, mix)


BORDER_ROWS = 4


def border_kernel(part_ref, cot_ref, left_ref, right_ref, out_ref):
    gap = jnp.zeros((96, 128), BF)
    turn = lambda low, high: jnp.concatenate([low, gap, high], axis=0).T.astype(F32)
    for m in range(2):
        for at in range(BORDER_ROWS):
            out_ref[m, at] = (part_ref[m, at] + cot_ref[m, at].astype(F32)) + turn(
                left_ref[m, at], right_ref[m, at]
            )


def add_border(part, cot, left, right):
    rows = lambda *tail: pl.BlockSpec((2, BORDER_ROWS, *tail), lambda i: (0, i, 0, 0))
    return pl.pallas_call(
        border_kernel,
        grid=(ROWS // BORDER_ROWS,),
        in_specs=[
            rows(128, 128),
            rows(128, 128),
            rows(16, 128),
            rows(16, 128),
        ],
        out_specs=rows(128, 128),
        out_shape=jax.ShapeDtypeStruct((2, ROWS, 128, 128), F32),
        compiler_params=pltpu.CompilerParams(vmem_limit_bytes=58 * 1024 * 1024),
        cost_estimate=pl.CostEstimate(flops=1_000_000, bytes_accessed=7_000_000, transcendentals=0),
    )(part, cot, left, right)


def finish_kernel(
    me_ref, own_ref, other_ref, mix_ref, hidden_ref, output_ref, bias_ref, gain_ref, hidden_bias_ref
):
    def place(first_ref, second_ref):
        for p in range(64):
            mix_ref[p * 8 : p * 8 + 8] = first_ref[p * 10 : p * 10 + 8]
            rest = second_ref[p * 10 : p * 10 + 8]
            if p < 32:
                hidden_ref[p * 8 : p * 8 + 8] = rest
            else:
                at, half = (p - 32) % 16, (p - 32) // 16
                output_ref[at * 8 : at * 8 + 8, half * 128 : half * 128 + 128] = rest

    pl.when(me_ref[0] == 0)(lambda: place(own_ref, other_ref))
    pl.when(me_ref[0] == 1)(lambda: place(other_ref, own_ref))
    small = jnp.concatenate([own_ref[p * 10 + 8 : p * 10 + 10] for p in range(64)], axis=0)
    small = small.T
    bias_ref[...] = small[0:1]
    gain_ref[...] = small[1:2]
    hidden_bias_ref[...] = jnp.concatenate([small[2:3], small[3:4]], axis=1)


def finish(me, own, other):
    return pl.pallas_call(
        finish_kernel,
        in_specs=[pl.BlockSpec(memory_space=pltpu.SMEM)]
        + [pl.BlockSpec(memory_space=pltpu.VMEM)] * 2,
        out_shape=[
            jax.ShapeDtypeStruct((512, 128), F32),
            jax.ShapeDtypeStruct((256, 128), F32),
            jax.ShapeDtypeStruct((128, 256), F32),
            jax.ShapeDtypeStruct((1, 128), F32),
            jax.ShapeDtypeStruct((1, 128), F32),
            jax.ShapeDtypeStruct((1, 256), F32),
        ],
        compiler_params=pltpu.CompilerParams(vmem_limit_bytes=24 * 1024 * 1024),
        cost_estimate=pl.CostEstimate(flops=1_000_000, bytes_accessed=1_200_000, transcendentals=0),
    )(me, own, other)


def ring(axis, shift):
    count = lax.axis_size(axis)
    return [(i, (i + shift) % count) for i in range(count)]


def on_device(
    features,
    cotangent,
    basis_table,
    halo_depth,
    mix_weight,
    mix_bias,
    norm_gain,
    hidden_weight,
    hidden_bias,
    output_weight,
):
    to_above, to_below = edges_of(features, cotangent)
    above = lax.ppermute(to_below, "lat", ring("lat", 1))
    below = lax.ppermute(to_above, "lat", ring("lat", -1))
    to_right, to_left = sides_of(features, above, below)
    left = lax.ppermute(to_right, "lon", ring("lon", 1))
    right = lax.ppermute(to_left, "lon", ring("lon", -1))
    first = (lax.axis_index("lat") * ROWS).reshape(1).astype(jnp.int32)
    taps, wide, hidden_t, output_t, columns = prepare(
        first,
        basis_table,
        halo_depth,
        mix_weight,
        mix_bias,
        norm_gain,
        hidden_weight,
        hidden_bias,
        output_weight,
    )

    me = lax.axis_index("member").reshape(1).astype(jnp.int32)
    cell_total = 2 * ROWS * 128 * lax.axis_size(("member", "lat", "lon"))
    weights = (hidden_weight, wide, hidden_t, output_t, columns)
    scale = 1.0 / math.sqrt(cell_total)
    mixed_round, keep, send = forward(
        me, taps, features, cotangent, left, right, above, below, weights, scale
    )
    swap = [(0, 1), (1, 0)]
    band = ("lat", "lon")
    peers = lax.axis_size(band)
    pair = keep + lax.ppermute(send, "member", swap)
    pair, mixed_round = lax.optimization_barrier((pair, mixed_round))
    pieces = lax.all_to_all(pair.reshape(peers, 640 // peers, 1, 128), band, 0, 0)
    part, to_left, to_right = backward(taps, mixed_round, wide)
    add_left = lax.ppermute(to_right, "lon", ring("lon", 1))
    add_right = lax.ppermute(to_left, "lon", ring("lon", -1))
    total, add_left, add_right = lax.optimization_barrier(
        (jnp.sum(pieces, axis=0), add_left, add_right)
    )

    copies = jnp.broadcast_to(total[None], pieces.shape)
    own = lax.all_to_all(copies, band, 0, 0).reshape(640, 128)
    feature_grad = add_border(part, cotangent, add_left, add_right)
    own, feature_grad = lax.optimization_barrier((own, feature_grad))
    other = lax.ppermute(own, "member", swap)
    mix_grad, hidden_grad, output_grad, bias, gain, hidden_bias = finish(me, own, other)
    return (
        feature_grad,
        mix_grad.reshape(128, 4, 128),
        bias.reshape(128),
        gain.reshape(128),
        hidden_grad,
        hidden_bias.reshape(256),
        output_grad,
    )


def solution(mesh):
    cells = P("member", "lat", None, "lon")
    return jax.shard_map(
        on_device,
        mesh=mesh,
        in_specs=(cells, cells) + (P(),) * 8,
        out_specs=(cells,) + (P(),) * 6,
        check_vma=False,
    )
```

```python
import functools
import math

import jax
import jax.numpy as jnp
from jax import lax
from jax.experimental import pallas as pl
from jax.experimental.pallas import tpu as pltpu
from jax.sharding import PartitionSpec as P

EPSILON = 1e-05
BF = jnp.bfloat16
F32 = jnp.float32
GELU_A = math.sqrt(2.0 / math.pi)
GELU_B = 0.044715
ROWS = 24
STEP_ROWS = 6
SIDE_ROWS = 8
STEPS = ROWS // STEP_ROWS + 1
HALO = 2


def nn(a, b):
    return lax.dot_general(a, b, (((1,), (0,)), ((), ())), preferred_element_type=F32)


def nt(a, b):
    return lax.dot_general(a, b, (((1,), (1,)), ((), ())), preferred_element_type=F32)


def build_filter(taps_ref, row, matrix_ref, slot):
    lanes = lax.broadcasted_iota(jnp.int32, (16, 128), 1)
    low = lanes < 64
    zero = jnp.zeros((16, 128), BF)
    for b in range(3):
        for k in range(4):
            base = taps_ref[b * 4 + k, pl.ds(row, 1), :]
            head = pltpu.roll(
                jnp.broadcast_to(base, (16, 128)), 0, 1, stride=1, stride_axis=0
            ).astype(BF)
            ring = [head] + [pltpu.roll(head, 16 * g, 1) for g in range(1, 8)]
            cols = pl.ds(k * 128, 128)
            own = pl.ds(b * 128, 128)
            matrix_ref[slot, own, cols] = jnp.concatenate(
                [jnp.where(low, head, zero), *ring[1:7], jnp.where(low, zero, ring[7])], axis=0
            )
            matrix_ref[slot, pl.ds(384 + b * 32, 32), cols] = jnp.concatenate(
                [jnp.where(low, ring[7], zero), jnp.where(low, zero, head)], axis=0
            )


def edges_kernel(low_ref, high_ref, low_cot_ref, high_cot_ref, to_above_ref, to_below_ref):
    for out_ref, rows, cot in (
        (to_above_ref, low_ref, low_cot_ref),
        (to_below_ref, high_ref, high_cot_ref),
    ):
        out_ref[:, 0:2] = rows[...]
        out_ref[:, 2:3] = cot[...]


def edges_of(feats, cot):
    rows = lambda count, at: pl.BlockSpec((2, count, 128, 128), lambda i: (0, at // count, 0, 0))
    edge = jax.ShapeDtypeStruct((2, 3, 128, 128), BF)
    return pl.pallas_call(
        edges_kernel,
        grid=(1,),
        in_specs=[rows(2, 0), rows(2, ROWS - 2), rows(1, 0), rows(1, ROWS - 1)],
        out_specs=[pl.BlockSpec((2, 3, 128, 128), lambda i: (0, 0, 0, 0))] * 2,
        out_shape=[edge, edge],
        compiler_params=pltpu.CompilerParams(vmem_limit_bytes=56 * 1024 * 1024),
        cost_estimate=pl.CostEstimate(flops=1_000, bytes_accessed=800_000, transcendentals=0),
    )(feats, feats, cot, cot)


def prepare_kernel(
    first_ref,
    basis_ref,
    depth_ref,
    mix_ref,
    mix_bias_ref,
    gain_ref,
    hidden_ref,
    hidden_bias_ref,
    output_ref,
    lines_ref,
    mix_out_ref,
    hidden_t_ref,
    output_t_ref,
    columns_ref,
):
    total = depth_ref.shape[1]
    iota = lambda shape, axis: lax.broadcasted_iota(jnp.int32, shape, axis)
    row = lax.rem(iota((32, total), 0) + (first_ref[0] + total - 1), total)
    chosen = (iota((32, total), 1) == row).astype(F32)
    depth = jnp.sum(chosen * depth_ref[...].astype(F32), axis=1, keepdims=True)
    chosen = chosen.astype(BF)
    taps = iota((32, 33), 1)
    near = jnp.abs(taps - 16).astype(F32) <= depth
    place = (lax.rem(16 - iota((33, 128), 1) + 128, 128) == iota((33, 128), 0)).astype(BF)
    own = lax.rem(iota((32, 33), 0) + (first_ref[0] + total - 1), total)
    for b in range(3):
        keep = near & (own + b >= 1) & (own + b <= total)
        for k in range(4):
            kept = jnp.where(keep, nt(chosen, basis_ref[b, :, k, :]), 0.0).astype(BF)
            lines_ref[b * 4 + k] = nn(kept, place)
    mix_out_ref[...] = jnp.concatenate([mix_ref[:, k, :] for k in range(4)], axis=1)
    hidden_t_ref[...] = hidden_ref[...].T
    output_t_ref[...] = output_ref[...].T
    for at, line in enumerate(
        (mix_bias_ref[...], gain_ref[...], hidden_bias_ref[:, :128], hidden_bias_ref[:, 128:])
    ):
        columns_ref[at * 128 : at * 128 + 128] = jnp.broadcast_to(line, (128, 128)).T


def prepare(first, basis, depth, mix, mix_bias, gain, hidden, hidden_bias, output):
    vmem = pl.BlockSpec(memory_space=pltpu.VMEM)
    return pl.pallas_call(
        prepare_kernel,
        in_specs=[pl.BlockSpec(memory_space=pltpu.SMEM)] + [vmem] * 8,
        out_specs=[vmem] * 5,
        out_shape=[
            jax.ShapeDtypeStruct((12, 32, 128), F32),
            jax.ShapeDtypeStruct((128, 512), BF),
            jax.ShapeDtypeStruct((128, 256), BF),
            jax.ShapeDtypeStruct((256, 128), BF),
            jax.ShapeDtypeStruct((512, 128), F32),
        ],
        compiler_params=pltpu.CompilerParams(vmem_limit_bytes=16 * 1024 * 1024),
        cost_estimate=pl.CostEstimate(
            flops=300_000_000, bytes_accessed=2_000_000, transcendentals=0
        ),
    )(
        first,
        basis.transpose(2, 3, 1, 0),
        depth[None],
        mix,
        mix_bias[None],
        gain[None],
        hidden,
        hidden_bias[None],
        output,
    )


def sides_kernel(feats_ref, above_ref, below_ref, to_right_ref, to_left_ref):
    step = pl.program_id(0)
    spot = lax.broadcasted_iota(jnp.int32, (32, 128), 0)
    spot = jnp.where(spot < 16, spot, spot + 96)
    pick = (lax.broadcasted_iota(jnp.int32, (32, 128), 1) == spot).astype(BF)

    def cut(row, blocks):
        turned = nt(pick, jnp.concatenate(blocks, axis=0)).astype(BF)
        for m in range(2):
            to_left_ref[m, row] = turned[:16, m * 128 : m * 128 + 128]
            to_right_ref[m, row] = turned[16:, m * 128 : m * 128 + 128]

    for at in range(SIDE_ROWS):
        cut(HALO + step * SIDE_ROWS + at, [feats_ref[0, at], feats_ref[1, at]])

    @pl.when(step == 0)
    def _():
        for first, ref in ((0, above_ref), (HALO + ROWS, below_ref)):
            for at in range(HALO):
                cut(first + at, [ref[m, at] for m in range(2)])


def sides_of(feats, above, below):
    side = jax.ShapeDtypeStruct((2, ROWS + 2 * HALO, 16, 128), BF)
    full = pl.BlockSpec((2, ROWS + 2 * HALO, 16, 128), lambda i: (0, 0, 0, 0))
    edge = pl.BlockSpec((2, 3, 128, 128), lambda i: (0, 0, 0, 0))
    return pl.pallas_call(
        sides_kernel,
        grid=(ROWS // SIDE_ROWS,),
        in_specs=[
            pl.BlockSpec((2, SIDE_ROWS, 128, 128), lambda i: (0, i, 0, 0)),
            edge,
            edge,
        ],
        out_specs=[full, full],
        out_shape=[side, side],
        compiler_params=pltpu.CompilerParams(vmem_limit_bytes=24 * 1024 * 1024),
        cost_estimate=pl.CostEstimate(flops=50_000_000, bytes_accessed=2_000_000, transcendentals=0),
    )(feats, above, below)


def forward_kernel(
    me_ref,
    taps_ref,
    feats_ref,
    before_ref,
    after_ref,
    cot_ref,
    left_ref,
    right_ref,
    above_ref,
    below_ref,
    hidden_ref,
    mix,
    hidden_t,
    output_t,
    columns,
    mixed_round_ref,
    keep_ref,
    send_ref,
    sides,
    before,
    after,
    matrix,
    mix_acc,
    out_acc,
    hid_acc,
    mix_bias_acc,
    gain_acc,
    hidden_bias_acc,
    packed,
    *,
    scale,
):
    step = pl.program_id(0)
    last = step == STEPS - 1

    def work(bands, side_rows, cots, counted):
        count = len(bands)
        blocks = 2 * count
        cells = []
        for at in range(count):
            start = side_rows + at if counted else side_rows[at]
            build_filter(taps_ref, start, matrix, at)
            inputs = []
            for m in range(2):
                halo = jnp.concatenate(
                    [
                        sides[m, pl.ds(start, 3)].reshape(96, 128),
                        jnp.zeros((32, 128), BF),
                    ],
                    axis=0,
                )
                inputs.append(jnp.concatenate([*bands[at][m], halo.T], axis=1))
            filtered = nn(jnp.concatenate(inputs, axis=0), matrix[at]).astype(BF)
            for m in range(2):
                cells.append(
                    jnp.concatenate(
                        [
                            filtered[m * 128 : m * 128 + 128, k * 128 : k * 128 + 128]
                            for k in range(4)
                        ],
                        axis=0,
                    )
                )
        filtered = jnp.concatenate(cells, axis=1)
        wide = lambda low, high: jnp.concatenate([columns[low:high]] * blocks, axis=1)
        fold = lambda v: functools.reduce(
            lambda a, b: a + b, [v[:, n * 128 : n * 128 + 128] for n in range(blocks)]
        )
        mixed = nn(mix[...], filtered) + wide(0, 128)
        inverse = lax.rsqrt(jnp.mean(mixed * mixed, axis=0, keepdims=True) + EPSILON)
        scaled = mixed * inverse
        gain = wide(128, 256)
        normed = (scaled * gain).astype(BF)
        hidden = nn(hidden_ref[...], normed) + wide(256, 512)
        square = hidden * hidden
        tanh = jnp.tanh(hidden * (GELU_A + (GELU_A * GELU_B) * square))
        half = 0.5 + 0.5 * tanh
        value = hidden * half
        slope = half + value * (1.0 - half) * (2.0 * GELU_A + (6.0 * GELU_A * GELU_B) * square)
        cot = jnp.concatenate(cots, axis=1)
        pre_grad = slope * nn(output_t[...], cot)
        pre_round = pre_grad.astype(BF)
        normed_grad = nn(hidden_t[...], pre_round)
        grad = normed_grad * gain
        mixed_grad = inverse * (grad - scaled * jnp.mean(grad * scaled, axis=0, keepdims=True))
        mixed_round = mixed_grad.astype(BF)
        if counted:
            out_acc[...] += nt(cot, value.astype(BF))
            hid_acc[...] += nt(pre_round, normed)
            hidden_bias_acc[...] += fold(pre_grad)
            gain_acc[...] += fold(normed_grad * scaled)
            mix_bias_acc[...] += fold(mixed_grad)
            mix_acc[...] += nt(mixed_round, filtered)
        for at in range(count):
            mixed_round_ref[at] = mixed_round[:, at * 256 : at * 256 + 256]

    @pl.when(step == 0)
    def _():
        for m in range(2):
            sides[m, :, 0:16] = left_ref[m]
            sides[m, :, 16:32] = right_ref[m]
        matrix[...] = jnp.zeros_like(matrix)
        for acc in (mix_acc, out_acc, hid_acc, mix_bias_acc, gain_acc, hidden_bias_acc):
            acc[...] = jnp.zeros_like(acc)
        mixed_round_ref[...] = jnp.zeros_like(mixed_round_ref)
        first = lambda ref, m: ref[m, 0]
        second = lambda ref, m: ref[m, 1]
        cot_of = lambda ref, m: ref[m, 2]
        work(
            [
                [(first(above_ref, m), second(above_ref, m), feats_ref[m, 0]) for m in range(2)],
                [(before_ref[m, 0], first(below_ref, m), second(below_ref, m)) for m in range(2)],
            ],
            (0, ROWS + 1),
            [cot_of(ref, m) for ref in (above_ref, below_ref) for m in range(2)],
            False,
        )

    @pl.when(step == 1)
    def _():
        for m in range(2):
            before[m] = above_ref[m, 1]

    @pl.when(step > 1)
    def _():
        before[...] = before_ref[:, 0]

    @pl.when(last)
    def _():
        for m in range(2):
            after[m] = below_ref[m, 0]

    @pl.when(jnp.logical_not(last))
    def _():
        after[...] = after_ref[:, 0]

    @pl.when(step > 0)
    def _():
        band = [
            [before[m], *[feats_ref[m, r] for r in range(STEP_ROWS)], after[m]] for m in range(2)
        ]
        work(
            [[tuple(band[m][at : at + 3]) for m in range(2)] for at in range(STEP_ROWS)],
            (step - 1) * STEP_ROWS + 1,
            [cot_ref[m, at] for at in range(STEP_ROWS) for m in range(2)],
            True,
        )

    @pl.when(last)
    def _():
        for k in range(4):
            packed[pl.ds(k, 128, stride=4), :] = mix_acc[:, k * 128 : k * 128 + 128] * scale
        packed[512:768] = hid_acc[...] * scale
        for f in range(2):
            packed[768 + f * 128 : 896 + f * 128] = out_acc[:, f * 128 : f * 128 + 128] * scale
        lanes = lax.broadcasted_iota(jnp.int32, (128, 128), 1)
        small = jnp.zeros((128, 128), F32)
        for at, part in enumerate(
            (mix_bias_acc[...], gain_acc[...], hidden_bias_acc[0:128], hidden_bias_acc[128:256])
        ):
            total = jnp.sum(part, axis=1, keepdims=True) * scale
            small = jnp.where(lanes == at, total, small)
        mine = me_ref[0]
        for ref, half in ((keep_ref, mine), (send_ref, 1 - mine)):
            for p in range(64):
                at = pl.multiple_of(half * 512 + p * 8, 8)
                ref[p * 10 : p * 10 + 8] = packed[pl.ds(at, 8), :]
                ref[p * 10 + 8 : p * 10 + 10] = small[2 * p : 2 * p + 2]


def forward(me, taps, feats, cot, left, right, above, below, weights, scale):
    whole = lambda v: pl.BlockSpec(v.shape, lambda i: (0,) * v.ndim)
    rows = lambda count, first: pl.BlockSpec(
        (2, count, 128, 128), lambda i: (0, first(i), 0, 0)
    )
    own = rows(STEP_ROWS, lambda i: jnp.maximum(i - 1, 0))
    ahead = lambda i: jnp.where(i == 0, ROWS - 1, jnp.maximum((i - 1) * STEP_ROWS - 1, 0))
    return pl.pallas_call(
        functools.partial(forward_kernel, scale=scale),
        grid=(STEPS,),
        in_specs=[
            pl.BlockSpec(memory_space=pltpu.SMEM),
            pl.BlockSpec((12, 32, 128), lambda i: (0, 0, 0)),
            own,
            rows(1, ahead),
            rows(1, lambda i: jnp.minimum(i * STEP_ROWS, ROWS - 1)),
            own,
            whole(left),
            whole(right),
            whole(above),
            whole(below),
            *[whole(v) for v in weights],
        ],
        out_specs=[
            pl.BlockSpec((STEP_ROWS, 128, 256), lambda i: (i, 0, 0)),
            pl.BlockSpec((640, 128), lambda i: (0, 0)),
            pl.BlockSpec((640, 128), lambda i: (0, 0)),
        ],
        out_shape=[
            jax.ShapeDtypeStruct((STEPS * STEP_ROWS, 128, 256), BF),
            jax.ShapeDtypeStruct((640, 128), F32),
            jax.ShapeDtypeStruct((640, 128), F32),
        ],
        scratch_shapes=[
            pltpu.VMEM((2, ROWS + 2 * HALO, 32, 128), BF),
            pltpu.VMEM((2, 128, 128), BF),
            pltpu.VMEM((2, 128, 128), BF),
            pltpu.VMEM((STEP_ROWS, 512, 512), BF),
            pltpu.VMEM((128, 512), F32),
            pltpu.VMEM((128, 256), F32),
            pltpu.VMEM((256, 128), F32),
            pltpu.VMEM((128, 128), F32),
            pltpu.VMEM((128, 128), F32),
            pltpu.VMEM((256, 128), F32),
            pltpu.VMEM((1024, 128), F32),
        ],
        compiler_params=pltpu.CompilerParams(vmem_limit_bytes=24 * 1024 * 1024),
        cost_estimate=pl.CostEstimate(
            flops=15_000_000_000, bytes_accessed=8_000_000, transcendentals=1_600_000
        ),
    )(me, taps, feats, feats, feats, cot, left, right, above, below, *weights)


def backward_kernel(
    taps_ref,
    mixed_round_ref,
    mix_ref,
    part_ref,
    to_left_ref,
    to_right_ref,
    acc,
    sides,
    matrix,
    mix_t,
    sems,
):
    step = pl.program_id(0)

    def spread_row(at, targets, row):
        build_filter(taps_ref, row + 1, matrix, at)
        grads = nn(mix_t[...], mixed_round_ref[at]).astype(BF)
        arranged = jnp.concatenate(
            [
                jnp.concatenate(
                    [grads[k * 128 : k * 128 + 128, m * 128 : m * 128 + 128] for k in range(4)],
                    axis=1,
                )
                for m in range(2)
            ],
            axis=0,
        )
        low, high = targets[0], targets[-1] + 1
        spread = nt(arranged, matrix[at, low * 128 : high * 128])
        halo = nt(matrix[at, 384:512], arranged)
        for m in range(2):
            for b in targets:
                cols = slice((b - low) * 128, (b - low) * 128 + 128)
                acc[m, row + b] += spread[m * 128 : m * 128 + 128, cols]
                sides[m, row + b] += halo[b * 32 : b * 32 + 32, m * 128 : m * 128 + 128]

    @pl.when(step == 0)
    def _():
        acc[...] = jnp.zeros_like(acc)
        sides[...] = jnp.zeros_like(sides)
        matrix[...] = jnp.zeros_like(matrix)
        for k in range(4):
            mix_t[k * 128 : k * 128 + 128] = mix_ref[:, k * 128 : k * 128 + 128].T
        spread_row(0, (2,), -1)
        spread_row(1, (0,), ROWS)

    @pl.when(step > 0)
    def _():
        for at in range(STEP_ROWS):
            spread_row(at, (0, 1, 2), (step - 1) * STEP_ROWS + at)

    def write(at):
        low = max((at - 1) * STEP_ROWS - 1, 0)
        high = ROWS if at == STEPS - 1 else at * STEP_ROWS - 1
        return pltpu.make_async_copy(
            acc.at[:, 1 + low : 1 + high], part_ref.at[:, low:high], sems.at[at - 1]
        )

    for at in range(1, STEPS):
        pl.when(step == at)(lambda: write(at).start())

    @pl.when(step == STEPS - 1)
    def _():
        to_left_ref[...] = sides[:, 1 : ROWS + 1, 0:16].astype(BF)
        to_right_ref[...] = sides[:, 1 : ROWS + 1, 16:32].astype(BF)
        for at in range(1, STEPS):
            write(at).wait()


def backward(taps, mixed_round, mix):
    whole = lambda *shape: pl.BlockSpec(shape, lambda i: (0,) * len(shape))
    side = jax.ShapeDtypeStruct((2, ROWS, 16, 128), BF)
    return pl.pallas_call(
        backward_kernel,
        grid=(STEPS,),
        in_specs=[
            pl.BlockSpec((12, 32, 128), lambda i: (0, 0, 0)),
            pl.BlockSpec((STEP_ROWS, 128, 256), lambda i: (i, 0, 0)),
            whole(128, 512),
        ],
        out_specs=[
            pl.BlockSpec(memory_space=pltpu.MemorySpace.HBM),
            whole(2, ROWS, 16, 128),
            whole(2, ROWS, 16, 128),
        ],
        out_shape=[jax.ShapeDtypeStruct((2, ROWS, 128, 128), F32), side, side],
        scratch_shapes=[
            pltpu.VMEM((2, ROWS + 2, 128, 128), F32),
            pltpu.VMEM((2, ROWS + 2, 32, 128), F32),
            pltpu.VMEM((STEP_ROWS, 512, 512), BF),
            pltpu.VMEM((512, 128), BF),
            pltpu.SemaphoreType.DMA((STEPS - 1,)),
        ],
        compiler_params=pltpu.CompilerParams(vmem_limit_bytes=58 * 1024 * 1024),
        cost_estimate=pl.CostEstimate(
            flops=7_500_000_000, bytes_accessed=8_000_000, transcendentals=0
        ),
    )(taps, mixed_round, mix)


BORDER_ROWS = 4


def border_kernel(part_ref, cot_ref, left_ref, right_ref, out_ref):
    gap = jnp.zeros((96, 128), BF)
    turn = lambda low, high: jnp.concatenate([low, gap, high], axis=0).T.astype(F32)
    for m in range(2):
        for at in range(BORDER_ROWS):
            out_ref[m, at] = (part_ref[m, at] + cot_ref[m, at].astype(F32)) + turn(
                left_ref[m, at], right_ref[m, at]
            )


def add_border(part, cot, left, right):
    rows = lambda *tail: pl.BlockSpec((2, BORDER_ROWS, *tail), lambda i: (0, i, 0, 0))
    return pl.pallas_call(
        border_kernel,
        grid=(ROWS // BORDER_ROWS,),
        in_specs=[
            rows(128, 128),
            rows(128, 128),
            rows(16, 128),
            rows(16, 128),
        ],
        out_specs=rows(128, 128),
        out_shape=jax.ShapeDtypeStruct((2, ROWS, 128, 128), F32),
        compiler_params=pltpu.CompilerParams(vmem_limit_bytes=58 * 1024 * 1024),
        cost_estimate=pl.CostEstimate(flops=1_000_000, bytes_accessed=7_000_000, transcendentals=0),
    )(part, cot, left, right)


def finish_kernel(
    me_ref, own_ref, other_ref, mix_ref, hidden_ref, output_ref, bias_ref, gain_ref, hidden_bias_ref
):
    def place(first_ref, second_ref):
        for p in range(64):
            mix_ref[p * 8 : p * 8 + 8] = first_ref[p * 10 : p * 10 + 8]
            rest = second_ref[p * 10 : p * 10 + 8]
            if p < 32:
                hidden_ref[p * 8 : p * 8 + 8] = rest
            else:
                at, half = (p - 32) % 16, (p - 32) // 16
                output_ref[at * 8 : at * 8 + 8, half * 128 : half * 128 + 128] = rest

    pl.when(me_ref[0] == 0)(lambda: place(own_ref, other_ref))
    pl.when(me_ref[0] == 1)(lambda: place(other_ref, own_ref))
    small = jnp.concatenate([own_ref[p * 10 + 8 : p * 10 + 10] for p in range(64)], axis=0)
    small = small.T
    bias_ref[...] = small[0:1]
    gain_ref[...] = small[1:2]
    hidden_bias_ref[...] = jnp.concatenate([small[2:3], small[3:4]], axis=1)


def finish(me, own, other):
    return pl.pallas_call(
        finish_kernel,
        in_specs=[pl.BlockSpec(memory_space=pltpu.SMEM)]
        + [pl.BlockSpec(memory_space=pltpu.VMEM)] * 2,
        out_shape=[
            jax.ShapeDtypeStruct((512, 128), F32),
            jax.ShapeDtypeStruct((256, 128), F32),
            jax.ShapeDtypeStruct((128, 256), F32),
            jax.ShapeDtypeStruct((1, 128), F32),
            jax.ShapeDtypeStruct((1, 128), F32),
            jax.ShapeDtypeStruct((1, 256), F32),
        ],
        compiler_params=pltpu.CompilerParams(vmem_limit_bytes=24 * 1024 * 1024),
        cost_estimate=pl.CostEstimate(flops=1_000_000, bytes_accessed=1_200_000, transcendentals=0),
    )(me, own, other)


def ring(axis, shift):
    count = lax.axis_size(axis)
    return [(i, (i + shift) % count) for i in range(count)]


def on_device(
    features,
    cotangent,
    basis_table,
    halo_depth,
    mix_weight,
    mix_bias,
    norm_gain,
    hidden_weight,
    hidden_bias,
    output_weight,
):
    to_above, to_below = edges_of(features, cotangent)
    above = lax.ppermute(to_below, "lat", ring("lat", 1))
    below = lax.ppermute(to_above, "lat", ring("lat", -1))
    to_right, to_left = sides_of(features, above, below)
    left = lax.ppermute(to_right, "lon", ring("lon", 1))
    right = lax.ppermute(to_left, "lon", ring("lon", -1))
    first = (lax.axis_index("lat") * ROWS).reshape(1).astype(jnp.int32)
    taps, wide, hidden_t, output_t, columns = prepare(
        first,
        basis_table,
        halo_depth,
        mix_weight,
        mix_bias,
        norm_gain,
        hidden_weight,
        hidden_bias,
        output_weight,
    )

    me = lax.axis_index("member").reshape(1).astype(jnp.int32)
    cell_total = 2 * ROWS * 128 * lax.axis_size(("member", "lat", "lon"))
    weights = (hidden_weight, wide, hidden_t, output_t, columns)
    scale = 1.0 / math.sqrt(cell_total)
    mixed_round, keep, send = forward(
        me, taps, features, cotangent, left, right, above, below, weights, scale
    )
    swap = [(0, 1), (1, 0)]
    band = ("lat", "lon")
    peers = lax.axis_size(band)
    pair = keep + lax.ppermute(send, "member", swap)
    pair, mixed_round = lax.optimization_barrier((pair, mixed_round))
    pieces = lax.all_to_all(pair.reshape(peers, 640 // peers, 1, 128), band, 0, 0)
    part, to_left, to_right = backward(taps, mixed_round, wide)
    add_left = lax.ppermute(to_right, "lon", ring("lon", 1))
    add_right = lax.ppermute(to_left, "lon", ring("lon", -1))
    total, add_left, add_right = lax.optimization_barrier(
        (jnp.sum(pieces, axis=0), add_left, add_right)
    )

    copies = jnp.broadcast_to(total[None], pieces.shape)
    own = lax.all_to_all(copies, band, 0, 0).reshape(640, 128)
    feature_grad = add_border(part, cotangent, add_left, add_right)
    own, feature_grad = lax.optimization_barrier((own, feature_grad))
    other = lax.ppermute(own, "member", swap)
    mix_grad, hidden_grad, output_grad, bias, gain, hidden_bias = finish(me, own, other)
    return (
        feature_grad,
        mix_grad.reshape(128, 4, 128),
        bias.reshape(128),
        gain.reshape(128),
        hidden_grad,
        hidden_bias.reshape(256),
        output_grad,
    )


def solution(mesh):
    cells = P("member", "lat", None, "lon")
    return jax.shard_map(
        on_device,
        mesh=mesh,
        in_specs=(cells, cells) + (P(),) * 8,
        out_specs=(cells,) + (P(),) * 6,
        check_vma=False,
    )
```

```python
import functools
import math

import jax
import jax.numpy as jnp
from jax import lax
from jax.experimental import pallas as pl
from jax.experimental.pallas import tpu as pltpu
from jax.sharding import PartitionSpec as P

EPSILON = 1e-05
BF = jnp.bfloat16
F32 = jnp.float32
GELU_A = math.sqrt(2.0 / math.pi)
GELU_B = 0.044715
ROWS = 24
STEP_ROWS = 6
SIDE_ROWS = 8
STEPS = ROWS // STEP_ROWS + 1
HALO = 2


def nn(a, b):
    return lax.dot_general(a, b, (((1,), (0,)), ((), ())), preferred_element_type=F32)


def nt(a, b):
    return lax.dot_general(a, b, (((1,), (1,)), ((), ())), preferred_element_type=F32)


def build_filter(taps_ref, row, matrix_ref, slot):
    lanes = lax.broadcasted_iota(jnp.int32, (16, 128), 1)
    low = lanes < 64
    zero = jnp.zeros((16, 128), BF)
    for b in range(3):
        for k in range(4):
            base = taps_ref[b * 4 + k, pl.ds(row, 1), :]
            head = pltpu.roll(
                jnp.broadcast_to(base, (16, 128)), 0, 1, stride=1, stride_axis=0
            ).astype(BF)
            ring = [head] + [pltpu.roll(head, 16 * g, 1) for g in range(1, 8)]
            cols = pl.ds(k * 128, 128)
            own = pl.ds(b * 128, 128)
            matrix_ref[slot, own, cols] = jnp.concatenate(
                [jnp.where(low, head, zero), *ring[1:7], jnp.where(low, zero, ring[7])], axis=0
            )
            matrix_ref[slot, pl.ds(384 + b * 32, 32), cols] = jnp.concatenate(
                [jnp.where(low, ring[7], zero), jnp.where(low, zero, head)], axis=0
            )


def edges_kernel(low_ref, high_ref, low_cot_ref, high_cot_ref, to_above_ref, to_below_ref):
    for out_ref, rows, cot in (
        (to_above_ref, low_ref, low_cot_ref),
        (to_below_ref, high_ref, high_cot_ref),
    ):
        out_ref[:, 0:2] = rows[...]
        out_ref[:, 2:3] = cot[...]


def edges_of(feats, cot):
    rows = lambda count, at: pl.BlockSpec((2, count, 128, 128), lambda i: (0, at // count, 0, 0))
    edge = jax.ShapeDtypeStruct((2, 3, 128, 128), BF)
    return pl.pallas_call(
        edges_kernel,
        grid=(1,),
        in_specs=[rows(2, 0), rows(2, ROWS - 2), rows(1, 0), rows(1, ROWS - 1)],
        out_specs=[pl.BlockSpec((2, 3, 128, 128), lambda i: (0, 0, 0, 0))] * 2,
        out_shape=[edge, edge],
        compiler_params=pltpu.CompilerParams(vmem_limit_bytes=56 * 1024 * 1024),
        cost_estimate=pl.CostEstimate(flops=1_000, bytes_accessed=800_000, transcendentals=0),
    )(feats, feats, cot, cot)


def prepare_kernel(
    first_ref,
    basis_ref,
    depth_ref,
    mix_ref,
    mix_bias_ref,
    gain_ref,
    hidden_ref,
    hidden_bias_ref,
    output_ref,
    lines_ref,
    mix_out_ref,
    hidden_t_ref,
    output_t_ref,
    columns_ref,
):
    total = depth_ref.shape[1]
    iota = lambda shape, axis: lax.broadcasted_iota(jnp.int32, shape, axis)
    row = lax.rem(iota((32, total), 0) + (first_ref[0] + total - 1), total)
    chosen = (iota((32, total), 1) == row).astype(F32)
    depth = jnp.sum(chosen * depth_ref[...].astype(F32), axis=1, keepdims=True)
    chosen = chosen.astype(BF)
    taps = iota((32, 33), 1)
    near = jnp.abs(taps - 16).astype(F32) <= depth
    place = (lax.rem(16 - iota((33, 128), 1) + 128, 128) == iota((33, 128), 0)).astype(BF)
    own = lax.rem(iota((32, 33), 0) + (first_ref[0] + total - 1), total)
    for b in range(3):
        keep = near & (own + b >= 1) & (own + b <= total)
        for k in range(4):
            kept = jnp.where(keep, nt(chosen, basis_ref[b, :, k, :]), 0.0).astype(BF)
            lines_ref[b * 4 + k] = nn(kept, place)
    mix_out_ref[...] = jnp.concatenate([mix_ref[:, k, :] for k in range(4)], axis=1)
    hidden_t_ref[...] = hidden_ref[...].T
    output_t_ref[...] = output_ref[...].T
    for at, line in enumerate(
        (mix_bias_ref[...], gain_ref[...], hidden_bias_ref[:, :128], hidden_bias_ref[:, 128:])
    ):
        columns_ref[at * 128 : at * 128 + 128] = jnp.broadcast_to(line, (128, 128)).T


def prepare(first, basis, depth, mix, mix_bias, gain, hidden, hidden_bias, output):
    vmem = pl.BlockSpec(memory_space=pltpu.VMEM)
    return pl.pallas_call(
        prepare_kernel,
        in_specs=[pl.BlockSpec(memory_space=pltpu.SMEM)] + [vmem] * 8,
        out_specs=[vmem] * 5,
        out_shape=[
            jax.ShapeDtypeStruct((12, 32, 128), F32),
            jax.ShapeDtypeStruct((128, 512), BF),
            jax.ShapeDtypeStruct((128, 256), BF),
            jax.ShapeDtypeStruct((256, 128), BF),
            jax.ShapeDtypeStruct((512, 128), F32),
        ],
        compiler_params=pltpu.CompilerParams(vmem_limit_bytes=16 * 1024 * 1024),
        cost_estimate=pl.CostEstimate(
            flops=300_000_000, bytes_accessed=2_000_000, transcendentals=0
        ),
    )(
        first,
        basis.transpose(2, 3, 1, 0),
        depth[None],
        mix,
        mix_bias[None],
        gain[None],
        hidden,
        hidden_bias[None],
        output,
    )


def cut_sides(blocks):
    spot = lax.broadcasted_iota(jnp.int32, (32, 128), 0)
    spot = jnp.where(spot < 16, spot, spot + 96)
    pick = (lax.broadcasted_iota(jnp.int32, (32, 128), 1) == spot).astype(BF)
    return nt(pick, jnp.concatenate(blocks, axis=0)).astype(BF)


def sides_kernel(feats_ref, to_right_ref, to_left_ref):
    for at in range(SIDE_ROWS):
        turned = cut_sides([feats_ref[0, at], feats_ref[1, at]])
        for m in range(2):
            to_left_ref[m, at] = turned[:16, m * 128 : m * 128 + 128]
            to_right_ref[m, at] = turned[16:, m * 128 : m * 128 + 128]


def sides_of(feats):
    rows = lambda *tail: pl.BlockSpec((2, SIDE_ROWS, *tail), lambda i: (0, i, 0, 0))
    side = jax.ShapeDtypeStruct((2, ROWS, 16, 128), BF)
    return pl.pallas_call(
        sides_kernel,
        grid=(ROWS // SIDE_ROWS,),
        in_specs=[rows(128, 128)],
        out_specs=[rows(16, 128)] * 2,
        out_shape=[side, side],
        compiler_params=pltpu.CompilerParams(vmem_limit_bytes=24 * 1024 * 1024),
        cost_estimate=pl.CostEstimate(flops=50_000_000, bytes_accessed=2_000_000, transcendentals=0),
    )(feats)


def corners_kernel(above_ref, below_ref, to_right_ref, to_left_ref):
    for first, ref in ((0, above_ref), (HALO, below_ref)):
        for at in range(HALO):
            turned = cut_sides([ref[0, at], ref[1, at]])
            for m in range(2):
                to_left_ref[m, first + at] = turned[:16, m * 128 : m * 128 + 128]
                to_right_ref[m, first + at] = turned[16:, m * 128 : m * 128 + 128]


def corners_of(above, below):
    vmem = pl.BlockSpec(memory_space=pltpu.VMEM)
    side = jax.ShapeDtypeStruct((2, 2 * HALO, 16, 128), BF)
    return pl.pallas_call(
        corners_kernel,
        in_specs=[vmem, vmem],
        out_specs=[vmem, vmem],
        out_shape=[side, side],
        compiler_params=pltpu.CompilerParams(vmem_limit_bytes=24 * 1024 * 1024),
        cost_estimate=pl.CostEstimate(flops=5_000_000, bytes_accessed=500_000, transcendentals=0),
    )(above, below)


def forward_kernel(
    me_ref,
    taps_ref,
    feats_ref,
    before_ref,
    after_ref,
    cot_ref,
    left_ref,
    right_ref,
    corner_left_ref,
    corner_right_ref,
    above_ref,
    below_ref,
    hidden_ref,
    mix,
    hidden_t,
    output_t,
    columns,
    mixed_round_ref,
    keep_ref,
    send_ref,
    sides,
    before,
    after,
    matrix,
    mix_acc,
    out_acc,
    hid_acc,
    mix_bias_acc,
    gain_acc,
    hidden_bias_acc,
    packed,
    *,
    scale,
):
    step = pl.program_id(0)
    last = step == STEPS - 1

    def work(bands, side_rows, cots, counted):
        count = len(bands)
        blocks = 2 * count
        cells = []
        for at in range(count):
            start = side_rows + at if counted else side_rows[at]
            build_filter(taps_ref, start, matrix, at)
            inputs = []
            for m in range(2):
                halo = jnp.concatenate(
                    [
                        sides[m, pl.ds(start, 3)].reshape(96, 128),
                        jnp.zeros((32, 128), BF),
                    ],
                    axis=0,
                )
                inputs.append(jnp.concatenate([*bands[at][m], halo.T], axis=1))
            filtered = nn(jnp.concatenate(inputs, axis=0), matrix[at]).astype(BF)
            for m in range(2):
                cells.append(
                    jnp.concatenate(
                        [
                            filtered[m * 128 : m * 128 + 128, k * 128 : k * 128 + 128]
                            for k in range(4)
                        ],
                        axis=0,
                    )
                )
        filtered = jnp.concatenate(cells, axis=1)
        wide = lambda low, high: jnp.concatenate([columns[low:high]] * blocks, axis=1)
        fold = lambda v: functools.reduce(
            lambda a, b: a + b, [v[:, n * 128 : n * 128 + 128] for n in range(blocks)]
        )
        mixed = nn(mix[...], filtered) + wide(0, 128)
        inverse = lax.rsqrt(jnp.mean(mixed * mixed, axis=0, keepdims=True) + EPSILON)
        scaled = mixed * inverse
        gain = wide(128, 256)
        normed = (scaled * gain).astype(BF)
        hidden = nn(hidden_ref[...], normed) + wide(256, 512)
        square = hidden * hidden
        tanh = jnp.tanh(hidden * (GELU_A + (GELU_A * GELU_B) * square))
        half = 0.5 + 0.5 * tanh
        value = hidden * half
        slope = half + value * (1.0 - half) * (2.0 * GELU_A + (6.0 * GELU_A * GELU_B) * square)
        cot = jnp.concatenate(cots, axis=1)
        pre_grad = slope * nn(output_t[...], cot)
        pre_round = pre_grad.astype(BF)
        normed_grad = nn(hidden_t[...], pre_round)
        grad = normed_grad * gain
        mixed_grad = inverse * (grad - scaled * jnp.mean(grad * scaled, axis=0, keepdims=True))
        mixed_round = mixed_grad.astype(BF)
        if counted:
            out_acc[...] += nt(cot, value.astype(BF))
            hid_acc[...] += nt(pre_round, normed)
            hidden_bias_acc[...] += fold(pre_grad)
            gain_acc[...] += fold(normed_grad * scaled)
            mix_bias_acc[...] += fold(mixed_grad)
            mix_acc[...] += nt(mixed_round, filtered)
        for at in range(count):
            mixed_round_ref[at] = mixed_round[:, at * 256 : at * 256 + 256]

    @pl.when(step == 0)
    def _():
        for m in range(2):
            for low, ref, corner in (
                (0, left_ref, corner_left_ref),
                (16, right_ref, corner_right_ref),
            ):
                cols = slice(low, low + 16)
                sides[m, 0:HALO, cols] = corner[m, 0:HALO]
                sides[m, HALO : HALO + ROWS, cols] = ref[m]
                sides[m, HALO + ROWS : 2 * HALO + ROWS, cols] = corner[m, HALO : 2 * HALO]
        matrix[...] = jnp.zeros_like(matrix)
        for acc in (mix_acc, out_acc, hid_acc, mix_bias_acc, gain_acc, hidden_bias_acc):
            acc[...] = jnp.zeros_like(acc)
        mixed_round_ref[...] = jnp.zeros_like(mixed_round_ref)
        first = lambda ref, m: ref[m, 0]
        second = lambda ref, m: ref[m, 1]
        cot_of = lambda ref, m: ref[m, 2]
        work(
            [
                [(first(above_ref, m), second(above_ref, m), feats_ref[m, 0]) for m in range(2)],
                [(before_ref[m, 0], first(below_ref, m), second(below_ref, m)) for m in range(2)],
            ],
            (0, ROWS + 1),
            [cot_of(ref, m) for ref in (above_ref, below_ref) for m in range(2)],
            False,
        )

    @pl.when(step == 1)
    def _():
        for m in range(2):
            before[m] = above_ref[m, 1]

    @pl.when(step > 1)
    def _():
        before[...] = before_ref[:, 0]

    @pl.when(last)
    def _():
        for m in range(2):
            after[m] = below_ref[m, 0]

    @pl.when(jnp.logical_not(last))
    def _():
        after[...] = after_ref[:, 0]

    @pl.when(step > 0)
    def _():
        band = [
            [before[m], *[feats_ref[m, r] for r in range(STEP_ROWS)], after[m]] for m in range(2)
        ]
        work(
            [[tuple(band[m][at : at + 3]) for m in range(2)] for at in range(STEP_ROWS)],
            (step - 1) * STEP_ROWS + 1,
            [cot_ref[m, at] for at in range(STEP_ROWS) for m in range(2)],
            True,
        )

    @pl.when(last)
    def _():
        for k in range(4):
            packed[pl.ds(k, 128, stride=4), :] = mix_acc[:, k * 128 : k * 128 + 128] * scale
        packed[512:768] = hid_acc[...] * scale
        for f in range(2):
            packed[768 + f * 128 : 896 + f * 128] = out_acc[:, f * 128 : f * 128 + 128] * scale
        lanes = lax.broadcasted_iota(jnp.int32, (128, 128), 1)
        small = jnp.zeros((128, 128), F32)
        for at, part in enumerate(
            (mix_bias_acc[...], gain_acc[...], hidden_bias_acc[0:128], hidden_bias_acc[128:256])
        ):
            total = jnp.sum(part, axis=1, keepdims=True) * scale
            small = jnp.where(lanes == at, total, small)
        mine = me_ref[0]
        for ref, half in ((keep_ref, mine), (send_ref, 1 - mine)):
            for p in range(64):
                at = pl.multiple_of(half * 512 + p * 8, 8)
                ref[p * 10 : p * 10 + 8] = packed[pl.ds(at, 8), :]
                ref[p * 10 + 8 : p * 10 + 10] = small[2 * p : 2 * p + 2]


def forward(me, taps, feats, cot, halos, weights, scale):
    whole = lambda v: pl.BlockSpec(v.shape, lambda i: (0,) * v.ndim)
    rows = lambda count, first: pl.BlockSpec(
        (2, count, 128, 128), lambda i: (0, first(i), 0, 0)
    )
    own = rows(STEP_ROWS, lambda i: jnp.maximum(i - 1, 0))
    ahead = lambda i: jnp.where(i == 0, ROWS - 1, jnp.maximum((i - 1) * STEP_ROWS - 1, 0))
    return pl.pallas_call(
        functools.partial(forward_kernel, scale=scale),
        grid=(STEPS,),
        in_specs=[
            pl.BlockSpec(memory_space=pltpu.SMEM),
            pl.BlockSpec((12, 32, 128), lambda i: (0, 0, 0)),
            own,
            rows(1, ahead),
            rows(1, lambda i: jnp.minimum(i * STEP_ROWS, ROWS - 1)),
            own,
            *[whole(v) for v in halos],
            *[whole(v) for v in weights],
        ],
        out_specs=[
            pl.BlockSpec((STEP_ROWS, 128, 256), lambda i: (i, 0, 0)),
            pl.BlockSpec((640, 128), lambda i: (0, 0)),
            pl.BlockSpec((640, 128), lambda i: (0, 0)),
        ],
        out_shape=[
            jax.ShapeDtypeStruct((STEPS * STEP_ROWS, 128, 256), BF),
            jax.ShapeDtypeStruct((640, 128), F32),
            jax.ShapeDtypeStruct((640, 128), F32),
        ],
        scratch_shapes=[
            pltpu.VMEM((2, ROWS + 2 * HALO, 32, 128), BF),
            pltpu.VMEM((2, 128, 128), BF),
            pltpu.VMEM((2, 128, 128), BF),
            pltpu.VMEM((STEP_ROWS, 512, 512), BF),
            pltpu.VMEM((128, 512), F32),
            pltpu.VMEM((128, 256), F32),
            pltpu.VMEM((256, 128), F32),
            pltpu.VMEM((128, 128), F32),
            pltpu.VMEM((128, 128), F32),
            pltpu.VMEM((256, 128), F32),
            pltpu.VMEM((1024, 128), F32),
        ],
        compiler_params=pltpu.CompilerParams(vmem_limit_bytes=24 * 1024 * 1024),
        cost_estimate=pl.CostEstimate(
            flops=15_000_000_000, bytes_accessed=8_000_000, transcendentals=1_600_000
        ),
    )(me, taps, feats, feats, feats, cot, *halos, *weights)


def backward_kernel(
    taps_ref,
    mixed_round_ref,
    mix_ref,
    part_ref,
    to_left_ref,
    to_right_ref,
    acc,
    sides,
    matrix,
    mix_t,
    sems,
):
    step = pl.program_id(0)

    def spread_row(at, targets, row):
        build_filter(taps_ref, row + 1, matrix, at)
        grads = nn(mix_t[...], mixed_round_ref[at]).astype(BF)
        arranged = jnp.concatenate(
            [
                jnp.concatenate(
                    [grads[k * 128 : k * 128 + 128, m * 128 : m * 128 + 128] for k in range(4)],
                    axis=1,
                )
                for m in range(2)
            ],
            axis=0,
        )
        low, high = targets[0], targets[-1] + 1
        spread = nt(arranged, matrix[at, low * 128 : high * 128])
        halo = nt(matrix[at, 384:512], arranged)
        for m in range(2):
            for b in targets:
                cols = slice((b - low) * 128, (b - low) * 128 + 128)
                acc[m, row + b] += spread[m * 128 : m * 128 + 128, cols]
                sides[m, row + b] += halo[b * 32 : b * 32 + 32, m * 128 : m * 128 + 128]

    @pl.when(step == 0)
    def _():
        acc[...] = jnp.zeros_like(acc)
        sides[...] = jnp.zeros_like(sides)
        matrix[...] = jnp.zeros_like(matrix)
        for k in range(4):
            mix_t[k * 128 : k * 128 + 128] = mix_ref[:, k * 128 : k * 128 + 128].T
        spread_row(0, (2,), -1)
        spread_row(1, (0,), ROWS)

    @pl.when(step > 0)
    def _():
        for at in range(STEP_ROWS):
            spread_row(at, (0, 1, 2), (step - 1) * STEP_ROWS + at)

    def write(at):
        low = max((at - 1) * STEP_ROWS - 1, 0)
        high = ROWS if at == STEPS - 1 else at * STEP_ROWS - 1
        return pltpu.make_async_copy(
            acc.at[:, 1 + low : 1 + high], part_ref.at[:, low:high], sems.at[at - 1]
        )

    for at in range(1, STEPS):
        pl.when(step == at)(lambda: write(at).start())

    @pl.when(step == STEPS - 1)
    def _():
        to_left_ref[...] = sides[:, 1 : ROWS + 1, 0:16].astype(BF)
        to_right_ref[...] = sides[:, 1 : ROWS + 1, 16:32].astype(BF)
        for at in range(1, STEPS):
            write(at).wait()


def backward(taps, mixed_round, mix):
    whole = lambda *shape: pl.BlockSpec(shape, lambda i: (0,) * len(shape))
    side = jax.ShapeDtypeStruct((2, ROWS, 16, 128), BF)
    return pl.pallas_call(
        backward_kernel,
        grid=(STEPS,),
        in_specs=[
            pl.BlockSpec((12, 32, 128), lambda i: (0, 0, 0)),
            pl.BlockSpec((STEP_ROWS, 128, 256), lambda i: (i, 0, 0)),
            whole(128, 512),
        ],
        out_specs=[
            pl.BlockSpec(memory_space=pltpu.MemorySpace.HBM),
            whole(2, ROWS, 16, 128),
            whole(2, ROWS, 16, 128),
        ],
        out_shape=[jax.ShapeDtypeStruct((2, ROWS, 128, 128), F32), side, side],
        scratch_shapes=[
            pltpu.VMEM((2, ROWS + 2, 128, 128), F32),
            pltpu.VMEM((2, ROWS + 2, 32, 128), F32),
            pltpu.VMEM((STEP_ROWS, 512, 512), BF),
            pltpu.VMEM((512, 128), BF),
            pltpu.SemaphoreType.DMA((STEPS - 1,)),
        ],
        compiler_params=pltpu.CompilerParams(vmem_limit_bytes=58 * 1024 * 1024),
        cost_estimate=pl.CostEstimate(
            flops=7_500_000_000, bytes_accessed=8_000_000, transcendentals=0
        ),
    )(taps, mixed_round, mix)


BORDER_ROWS = 4


def border_kernel(part_ref, cot_ref, left_ref, right_ref, out_ref):
    gap = jnp.zeros((96, 128), BF)
    turn = lambda low, high: jnp.concatenate([low, gap, high], axis=0).T.astype(F32)
    for m in range(2):
        for at in range(BORDER_ROWS):
            out_ref[m, at] = (part_ref[m, at] + cot_ref[m, at].astype(F32)) + turn(
                left_ref[m, at], right_ref[m, at]
            )


def add_border(part, cot, left, right):
    rows = lambda *tail: pl.BlockSpec((2, BORDER_ROWS, *tail), lambda i: (0, i, 0, 0))
    return pl.pallas_call(
        border_kernel,
        grid=(ROWS // BORDER_ROWS,),
        in_specs=[
            rows(128, 128),
            rows(128, 128),
            rows(16, 128),
            rows(16, 128),
        ],
        out_specs=rows(128, 128),
        out_shape=jax.ShapeDtypeStruct((2, ROWS, 128, 128), F32),
        compiler_params=pltpu.CompilerParams(vmem_limit_bytes=58 * 1024 * 1024),
        cost_estimate=pl.CostEstimate(flops=1_000_000, bytes_accessed=7_000_000, transcendentals=0),
    )(part, cot, left, right)


def finish_kernel(
    me_ref, own_ref, other_ref, mix_ref, hidden_ref, output_ref, bias_ref, gain_ref, hidden_bias_ref
):
    def place(first_ref, second_ref):
        for p in range(64):
            mix_ref[p * 8 : p * 8 + 8] = first_ref[p * 10 : p * 10 + 8]
            rest = second_ref[p * 10 : p * 10 + 8]
            if p < 32:
                hidden_ref[p * 8 : p * 8 + 8] = rest
            else:
                at, half = (p - 32) % 16, (p - 32) // 16
                output_ref[at * 8 : at * 8 + 8, half * 128 : half * 128 + 128] = rest

    pl.when(me_ref[0] == 0)(lambda: place(own_ref, other_ref))
    pl.when(me_ref[0] == 1)(lambda: place(other_ref, own_ref))
    small = jnp.concatenate([own_ref[p * 10 + 8 : p * 10 + 10] for p in range(64)], axis=0)
    small = small.T
    bias_ref[...] = small[0:1]
    gain_ref[...] = small[1:2]
    hidden_bias_ref[...] = jnp.concatenate([small[2:3], small[3:4]], axis=1)


def finish(me, own, other):
    return pl.pallas_call(
        finish_kernel,
        in_specs=[pl.BlockSpec(memory_space=pltpu.SMEM)]
        + [pl.BlockSpec(memory_space=pltpu.VMEM)] * 2,
        out_shape=[
            jax.ShapeDtypeStruct((512, 128), F32),
            jax.ShapeDtypeStruct((256, 128), F32),
            jax.ShapeDtypeStruct((128, 256), F32),
            jax.ShapeDtypeStruct((1, 128), F32),
            jax.ShapeDtypeStruct((1, 128), F32),
            jax.ShapeDtypeStruct((1, 256), F32),
        ],
        compiler_params=pltpu.CompilerParams(vmem_limit_bytes=24 * 1024 * 1024),
        cost_estimate=pl.CostEstimate(flops=1_000_000, bytes_accessed=1_200_000, transcendentals=0),
    )(me, own, other)


def ring(axis, shift):
    count = lax.axis_size(axis)
    return [(i, (i + shift) % count) for i in range(count)]


def on_device(
    features,
    cotangent,
    basis_table,
    halo_depth,
    mix_weight,
    mix_bias,
    norm_gain,
    hidden_weight,
    hidden_bias,
    output_weight,
):
    to_above, to_below = edges_of(features, cotangent)
    above = lax.ppermute(to_below, "lat", ring("lat", 1))
    below = lax.ppermute(to_above, "lat", ring("lat", -1))
    to_right, to_left = sides_of(features)
    left = lax.ppermute(to_right, "lon", ring("lon", 1))
    right = lax.ppermute(to_left, "lon", ring("lon", -1))
    to_right, to_left = corners_of(above, below)
    corner_left = lax.ppermute(to_right, "lon", ring("lon", 1))
    corner_right = lax.ppermute(to_left, "lon", ring("lon", -1))
    halos = (left, right, corner_left, corner_right, above, below)
    first = (lax.axis_index("lat") * ROWS).reshape(1).astype(jnp.int32)
    taps, wide, hidden_t, output_t, columns = prepare(
        first,
        basis_table,
        halo_depth,
        mix_weight,
        mix_bias,
        norm_gain,
        hidden_weight,
        hidden_bias,
        output_weight,
    )

    me = lax.axis_index("member").reshape(1).astype(jnp.int32)
    cell_total = 2 * ROWS * 128 * lax.axis_size(("member", "lat", "lon"))
    weights = (hidden_weight, wide, hidden_t, output_t, columns)
    scale = 1.0 / math.sqrt(cell_total)
    mixed_round, keep, send = forward(
        me, taps, features, cotangent, halos, weights, scale
    )
    swap = [(0, 1), (1, 0)]
    band = ("lat", "lon")
    peers = lax.axis_size(band)
    pair = keep + lax.ppermute(send, "member", swap)
    pair, mixed_round = lax.optimization_barrier((pair, mixed_round))
    pieces = lax.all_to_all(pair.reshape(peers, 640 // peers, 1, 128), band, 0, 0)
    part, to_left, to_right = backward(taps, mixed_round, wide)
    add_left = lax.ppermute(to_right, "lon", ring("lon", 1))
    add_right = lax.ppermute(to_left, "lon", ring("lon", -1))
    total, add_left, add_right = lax.optimization_barrier(
        (jnp.sum(pieces, axis=0), add_left, add_right)
    )

    copies = jnp.broadcast_to(total[None], pieces.shape)
    own = lax.all_to_all(copies, band, 0, 0).reshape(640, 128)
    feature_grad = add_border(part, cotangent, add_left, add_right)
    own, feature_grad = lax.optimization_barrier((own, feature_grad))
    other = lax.ppermute(own, "member", swap)
    mix_grad, hidden_grad, output_grad, bias, gain, hidden_bias = finish(me, own, other)
    return (
        feature_grad,
        mix_grad.reshape(128, 4, 128),
        bias.reshape(128),
        gain.reshape(128),
        hidden_grad,
        hidden_bias.reshape(256),
        output_grad,
    )


def solution(mesh):
    cells = P("member", "lat", None, "lon")
    return jax.shard_map(
        on_device,
        mesh=mesh,
        in_specs=(cells, cells) + (P(),) * 8,
        out_specs=(cells,) + (P(),) * 6,
        check_vma=False,
    )
```

```python
import functools
import math

import jax
import jax.numpy as jnp
from jax import lax
from jax.experimental import pallas as pl
from jax.experimental.pallas import tpu as pltpu
from jax.sharding import PartitionSpec as P

EPSILON = 1e-05
BF = jnp.bfloat16
F32 = jnp.float32
GELU_A = math.sqrt(2.0 / math.pi)
GELU_B = 0.044715
ROWS = 24
STEP_ROWS = 6
SIDE_ROWS = 8
STEPS = ROWS // STEP_ROWS + 1
HALO = 2


def nn(a, b):
    return lax.dot_general(a, b, (((1,), (0,)), ((), ())), preferred_element_type=F32)


def nt(a, b):
    return lax.dot_general(a, b, (((1,), (1,)), ((), ())), preferred_element_type=F32)


def build_filter(taps_ref, row, matrix_ref, slot):
    lanes = lax.broadcasted_iota(jnp.int32, (16, 128), 1)
    low = lanes < 64
    zero = jnp.zeros((16, 128), BF)
    for b in range(3):
        for k in range(4):
            base = taps_ref[b * 4 + k, pl.ds(row, 1), :]
            head = pltpu.roll(
                jnp.broadcast_to(base, (16, 128)), 0, 1, stride=1, stride_axis=0
            ).astype(BF)
            ring = [head] + [pltpu.roll(head, 16 * g, 1) for g in range(1, 8)]
            cols = pl.ds(k * 128, 128)
            own = pl.ds(b * 128, 128)
            matrix_ref[slot, own, cols] = jnp.concatenate(
                [jnp.where(low, head, zero), *ring[1:7], jnp.where(low, zero, ring[7])], axis=0
            )
            matrix_ref[slot, pl.ds(384 + b * 32, 32), cols] = jnp.concatenate(
                [jnp.where(low, ring[7], zero), jnp.where(low, zero, head)], axis=0
            )


def edges_kernel(low_ref, high_ref, low_cot_ref, high_cot_ref, to_above_ref, to_below_ref):
    for out_ref, rows, cot in (
        (to_above_ref, low_ref, low_cot_ref),
        (to_below_ref, high_ref, high_cot_ref),
    ):
        out_ref[:, 0:2] = rows[...]
        out_ref[:, 2:3] = cot[...]


def edges_of(feats, cot):
    rows = lambda count, at: pl.BlockSpec((2, count, 128, 128), lambda i: (0, at // count, 0, 0))
    edge = jax.ShapeDtypeStruct((2, 3, 128, 128), BF)
    return pl.pallas_call(
        edges_kernel,
        grid=(1,),
        in_specs=[rows(2, 0), rows(2, ROWS - 2), rows(1, 0), rows(1, ROWS - 1)],
        out_specs=[pl.BlockSpec((2, 3, 128, 128), lambda i: (0, 0, 0, 0))] * 2,
        out_shape=[edge, edge],
        compiler_params=pltpu.CompilerParams(vmem_limit_bytes=56 * 1024 * 1024),
        cost_estimate=pl.CostEstimate(flops=1_000, bytes_accessed=800_000, transcendentals=0),
    )(feats, feats, cot, cot)


def prepare_kernel(
    first_ref,
    basis_ref,
    depth_ref,
    mix_bias_ref,
    gain_ref,
    hidden_bias_ref,
    lines_ref,
    columns_ref,
):
    total = depth_ref.shape[1]
    iota = lambda shape, axis: lax.broadcasted_iota(jnp.int32, shape, axis)
    row = lax.rem(iota((32, total), 0) + (first_ref[0] + total - 1), total)
    chosen = (iota((32, total), 1) == row).astype(F32)
    depth = jnp.sum(chosen * depth_ref[...].astype(F32), axis=1, keepdims=True)
    chosen = chosen.astype(BF)
    taps = iota((32, 33), 1)
    near = jnp.abs(taps - 16).astype(F32) <= depth
    place = (lax.rem(16 - iota((33, 128), 1) + 128, 128) == iota((33, 128), 0)).astype(BF)
    own = lax.rem(iota((32, 33), 0) + (first_ref[0] + total - 1), total)
    for b in range(3):
        keep = near & (own + b >= 1) & (own + b <= total)
        for k in range(4):
            kept = jnp.where(keep, nt(chosen, basis_ref[b, :, k, :]), 0.0).astype(BF)
            lines_ref[b * 4 + k] = nn(kept, place)
    for at, line in enumerate(
        (mix_bias_ref[...], gain_ref[...], hidden_bias_ref[:, :128], hidden_bias_ref[:, 128:])
    ):
        columns_ref[at * 128 : at * 128 + 128] = jnp.broadcast_to(line, (128, 128)).T


def prepare(first, basis, depth, mix_bias, gain, hidden_bias):
    vmem = pl.BlockSpec(memory_space=pltpu.VMEM)
    return pl.pallas_call(
        prepare_kernel,
        in_specs=[pl.BlockSpec(memory_space=pltpu.SMEM)] + [vmem] * 5,
        out_specs=[vmem] * 2,
        out_shape=[
            jax.ShapeDtypeStruct((12, 32, 128), F32),
            jax.ShapeDtypeStruct((512, 128), F32),
        ],
        compiler_params=pltpu.CompilerParams(vmem_limit_bytes=16 * 1024 * 1024),
        cost_estimate=pl.CostEstimate(
            flops=300_000_000, bytes_accessed=2_000_000, transcendentals=0
        ),
    )(
        first,
        basis.transpose(2, 3, 1, 0),
        depth[None],
        mix_bias[None],
        gain[None],
        hidden_bias[None],
    )


def cut_sides(blocks):
    spot = lax.broadcasted_iota(jnp.int32, (32, 128), 0)
    spot = jnp.where(spot < 16, spot, spot + 96)
    pick = (lax.broadcasted_iota(jnp.int32, (32, 128), 1) == spot).astype(BF)
    return nt(pick, jnp.concatenate(blocks, axis=0)).astype(BF)


def sides_kernel(feats_ref, to_right_ref, to_left_ref):
    for at in range(SIDE_ROWS):
        turned = cut_sides([feats_ref[0, at], feats_ref[1, at]])
        for m in range(2):
            to_left_ref[m, at] = turned[:16, m * 128 : m * 128 + 128]
            to_right_ref[m, at] = turned[16:, m * 128 : m * 128 + 128]


def sides_of(feats):
    rows = lambda *tail: pl.BlockSpec((2, SIDE_ROWS, *tail), lambda i: (0, i, 0, 0))
    side = jax.ShapeDtypeStruct((2, ROWS, 16, 128), BF)
    return pl.pallas_call(
        sides_kernel,
        grid=(ROWS // SIDE_ROWS,),
        in_specs=[rows(128, 128)],
        out_specs=[rows(16, 128)] * 2,
        out_shape=[side, side],
        compiler_params=pltpu.CompilerParams(vmem_limit_bytes=24 * 1024 * 1024),
        cost_estimate=pl.CostEstimate(flops=50_000_000, bytes_accessed=2_000_000, transcendentals=0),
    )(feats)


def corners_kernel(above_ref, below_ref, to_right_ref, to_left_ref):
    for first, ref in ((0, above_ref), (HALO, below_ref)):
        for at in range(HALO):
            turned = cut_sides([ref[0, at], ref[1, at]])
            for m in range(2):
                to_left_ref[m, first + at] = turned[:16, m * 128 : m * 128 + 128]
                to_right_ref[m, first + at] = turned[16:, m * 128 : m * 128 + 128]


def corners_of(above, below):
    vmem = pl.BlockSpec(memory_space=pltpu.VMEM)
    side = jax.ShapeDtypeStruct((2, 2 * HALO, 16, 128), BF)
    return pl.pallas_call(
        corners_kernel,
        in_specs=[vmem, vmem],
        out_specs=[vmem, vmem],
        out_shape=[side, side],
        compiler_params=pltpu.CompilerParams(vmem_limit_bytes=24 * 1024 * 1024),
        cost_estimate=pl.CostEstimate(flops=5_000_000, bytes_accessed=500_000, transcendentals=0),
    )(above, below)


def forward_kernel(
    me_ref,
    taps_ref,
    feats_ref,
    before_ref,
    after_ref,
    cot_ref,
    left_ref,
    right_ref,
    corner_left_ref,
    corner_right_ref,
    above_ref,
    below_ref,
    mix_ref,
    hidden_ref,
    output_ref,
    columns,
    mixed_round_ref,
    keep_ref,
    send_ref,
    mix,
    hidden_t,
    output_t,
    sides,
    before,
    after,
    matrix,
    mix_acc,
    out_acc,
    hid_acc,
    mix_bias_acc,
    gain_acc,
    hidden_bias_acc,
    packed,
    *,
    scale,
):
    step = pl.program_id(0)
    last = step == STEPS - 1

    def work(bands, side_rows, cots, counted):
        count = len(bands)
        blocks = 2 * count
        cells = []
        for at in range(count):
            start = side_rows + at if counted else side_rows[at]
            build_filter(taps_ref, start, matrix, at)
            inputs = []
            for m in range(2):
                halo = jnp.concatenate(
                    [
                        sides[m, pl.ds(start, 3)].reshape(96, 128),
                        jnp.zeros((32, 128), BF),
                    ],
                    axis=0,
                )
                inputs.append(jnp.concatenate([*bands[at][m], halo.T], axis=1))
            filtered = nn(jnp.concatenate(inputs, axis=0), matrix[at]).astype(BF)
            for m in range(2):
                cells.append(
                    jnp.concatenate(
                        [
                            filtered[m * 128 : m * 128 + 128, k * 128 : k * 128 + 128]
                            for k in range(4)
                        ],
                        axis=0,
                    )
                )
        filtered = jnp.concatenate(cells, axis=1)
        wide = lambda low, high: jnp.concatenate([columns[low:high]] * blocks, axis=1)
        fold = lambda v: functools.reduce(
            lambda a, b: a + b, [v[:, n * 128 : n * 128 + 128] for n in range(blocks)]
        )
        mixed = nn(mix[...], filtered) + wide(0, 128)
        inverse = lax.rsqrt(jnp.mean(mixed * mixed, axis=0, keepdims=True) + EPSILON)
        scaled = mixed * inverse
        gain = wide(128, 256)
        normed = (scaled * gain).astype(BF)
        hidden = nn(hidden_ref[...], normed) + wide(256, 512)
        square = hidden * hidden
        tanh = jnp.tanh(hidden * (GELU_A + (GELU_A * GELU_B) * square))
        half = 0.5 + 0.5 * tanh
        value = hidden * half
        slope = half + value * (1.0 - half) * (2.0 * GELU_A + (6.0 * GELU_A * GELU_B) * square)
        cot = jnp.concatenate(cots, axis=1)
        pre_grad = slope * nn(output_t[...], cot)
        pre_round = pre_grad.astype(BF)
        normed_grad = nn(hidden_t[...], pre_round)
        grad = normed_grad * gain
        mixed_grad = inverse * (grad - scaled * jnp.mean(grad * scaled, axis=0, keepdims=True))
        mixed_round = mixed_grad.astype(BF)
        if counted:
            out_acc[...] += nt(cot, value.astype(BF))
            hid_acc[...] += nt(pre_round, normed)
            hidden_bias_acc[...] += fold(pre_grad)
            gain_acc[...] += fold(normed_grad * scaled)
            mix_bias_acc[...] += fold(mixed_grad)
            mix_acc[...] += nt(mixed_round, filtered)
        for at in range(count):
            mixed_round_ref[at] = mixed_round[:, at * 256 : at * 256 + 256]

    @pl.when(step == 0)
    def _():
        for m in range(2):
            for low, ref, corner in (
                (0, left_ref, corner_left_ref),
                (16, right_ref, corner_right_ref),
            ):
                cols = slice(low, low + 16)
                sides[m, 0:HALO, cols] = corner[m, 0:HALO]
                sides[m, HALO : HALO + ROWS, cols] = ref[m]
                sides[m, HALO + ROWS : 2 * HALO + ROWS, cols] = corner[m, HALO : 2 * HALO]
        matrix[...] = jnp.zeros_like(matrix)
        mix[...] = jnp.concatenate([mix_ref[:, k, :] for k in range(4)], axis=1)
        hidden_t[...] = hidden_ref[...].T
        output_t[...] = output_ref[...].T
        for acc in (mix_acc, out_acc, hid_acc, mix_bias_acc, gain_acc, hidden_bias_acc):
            acc[...] = jnp.zeros_like(acc)
        mixed_round_ref[...] = jnp.zeros_like(mixed_round_ref)
        first = lambda ref, m: ref[m, 0]
        second = lambda ref, m: ref[m, 1]
        cot_of = lambda ref, m: ref[m, 2]
        work(
            [
                [(first(above_ref, m), second(above_ref, m), feats_ref[m, 0]) for m in range(2)],
                [(before_ref[m, 0], first(below_ref, m), second(below_ref, m)) for m in range(2)],
            ],
            (0, ROWS + 1),
            [cot_of(ref, m) for ref in (above_ref, below_ref) for m in range(2)],
            False,
        )

    @pl.when(step == 1)
    def _():
        for m in range(2):
            before[m] = above_ref[m, 1]

    @pl.when(step > 1)
    def _():
        before[...] = before_ref[:, 0]

    @pl.when(last)
    def _():
        for m in range(2):
            after[m] = below_ref[m, 0]

    @pl.when(jnp.logical_not(last))
    def _():
        after[...] = after_ref[:, 0]

    @pl.when(step > 0)
    def _():
        band = [
            [before[m], *[feats_ref[m, r] for r in range(STEP_ROWS)], after[m]] for m in range(2)
        ]
        work(
            [[tuple(band[m][at : at + 3]) for m in range(2)] for at in range(STEP_ROWS)],
            (step - 1) * STEP_ROWS + 1,
            [cot_ref[m, at] for at in range(STEP_ROWS) for m in range(2)],
            True,
        )

    @pl.when(last)
    def _():
        for k in range(4):
            packed[pl.ds(k, 128, stride=4), :] = mix_acc[:, k * 128 : k * 128 + 128] * scale
        packed[512:768] = hid_acc[...] * scale
        for f in range(2):
            packed[768 + f * 128 : 896 + f * 128] = out_acc[:, f * 128 : f * 128 + 128] * scale
        lanes = lax.broadcasted_iota(jnp.int32, (128, 128), 1)
        small = jnp.zeros((128, 128), F32)
        for at, part in enumerate(
            (mix_bias_acc[...], gain_acc[...], hidden_bias_acc[0:128], hidden_bias_acc[128:256])
        ):
            total = jnp.sum(part, axis=1, keepdims=True) * scale
            small = jnp.where(lanes == at, total, small)
        mine = me_ref[0]
        for ref, half in ((keep_ref, mine), (send_ref, 1 - mine)):
            for p in range(64):
                at = pl.multiple_of(half * 512 + p * 8, 8)
                ref[p * 10 : p * 10 + 8] = packed[pl.ds(at, 8), :]
                ref[p * 10 + 8 : p * 10 + 10] = small[2 * p : 2 * p + 2]


def forward(me, taps, feats, cot, halos, weights, scale):
    whole = lambda v: pl.BlockSpec(v.shape, lambda i: (0,) * v.ndim)
    rows = lambda count, first: pl.BlockSpec(
        (2, count, 128, 128), lambda i: (0, first(i), 0, 0)
    )
    own = rows(STEP_ROWS, lambda i: jnp.maximum(i - 1, 0))
    ahead = lambda i: jnp.where(i == 0, ROWS - 1, jnp.maximum((i - 1) * STEP_ROWS - 1, 0))
    return pl.pallas_call(
        functools.partial(forward_kernel, scale=scale),
        grid=(STEPS,),
        in_specs=[
            pl.BlockSpec(memory_space=pltpu.SMEM),
            pl.BlockSpec((12, 32, 128), lambda i: (0, 0, 0)),
            own,
            rows(1, ahead),
            rows(1, lambda i: jnp.minimum(i * STEP_ROWS, ROWS - 1)),
            own,
            *[whole(v) for v in halos],
            *[whole(v) for v in weights],
        ],
        out_specs=[
            pl.BlockSpec((STEP_ROWS, 128, 256), lambda i: (i, 0, 0)),
            pl.BlockSpec((640, 128), lambda i: (0, 0)),
            pl.BlockSpec((640, 128), lambda i: (0, 0)),
        ],
        out_shape=[
            jax.ShapeDtypeStruct((STEPS * STEP_ROWS, 128, 256), BF),
            jax.ShapeDtypeStruct((640, 128), F32),
            jax.ShapeDtypeStruct((640, 128), F32),
        ],
        scratch_shapes=[
            pltpu.VMEM((128, 512), BF),
            pltpu.VMEM((128, 256), BF),
            pltpu.VMEM((256, 128), BF),
            pltpu.VMEM((2, ROWS + 2 * HALO, 32, 128), BF),
            pltpu.VMEM((2, 128, 128), BF),
            pltpu.VMEM((2, 128, 128), BF),
            pltpu.VMEM((STEP_ROWS, 512, 512), BF),
            pltpu.VMEM((128, 512), F32),
            pltpu.VMEM((128, 256), F32),
            pltpu.VMEM((256, 128), F32),
            pltpu.VMEM((128, 128), F32),
            pltpu.VMEM((128, 128), F32),
            pltpu.VMEM((256, 128), F32),
            pltpu.VMEM((1024, 128), F32),
        ],
        compiler_params=pltpu.CompilerParams(vmem_limit_bytes=24 * 1024 * 1024),
        cost_estimate=pl.CostEstimate(
            flops=15_000_000_000, bytes_accessed=8_000_000, transcendentals=1_600_000
        ),
    )(me, taps, feats, feats, feats, cot, *halos, *weights)


def backward_kernel(
    taps_ref,
    mixed_round_ref,
    mix_ref,
    part_ref,
    to_left_ref,
    to_right_ref,
    acc,
    sides,
    matrix,
    mix_t,
    sems,
):
    step = pl.program_id(0)

    def spread_row(at, targets, row):
        build_filter(taps_ref, row + 1, matrix, at)
        grads = nn(mix_t[...], mixed_round_ref[at]).astype(BF)
        arranged = jnp.concatenate(
            [
                jnp.concatenate(
                    [grads[k * 128 : k * 128 + 128, m * 128 : m * 128 + 128] for k in range(4)],
                    axis=1,
                )
                for m in range(2)
            ],
            axis=0,
        )
        low, high = targets[0], targets[-1] + 1
        spread = nt(arranged, matrix[at, low * 128 : high * 128])
        halo = nt(matrix[at, 384:512], arranged)
        for m in range(2):
            for b in targets:
                cols = slice((b - low) * 128, (b - low) * 128 + 128)
                acc[m, row + b] += spread[m * 128 : m * 128 + 128, cols]
                sides[m, row + b] += halo[b * 32 : b * 32 + 32, m * 128 : m * 128 + 128]

    @pl.when(step == 0)
    def _():
        acc[...] = jnp.zeros_like(acc)
        sides[...] = jnp.zeros_like(sides)
        matrix[...] = jnp.zeros_like(matrix)
        for k in range(4):
            mix_t[k * 128 : k * 128 + 128] = mix_ref[:, k, :].T
        spread_row(0, (2,), -1)
        spread_row(1, (0,), ROWS)

    @pl.when(step > 0)
    def _():
        for at in range(STEP_ROWS):
            spread_row(at, (0, 1, 2), (step - 1) * STEP_ROWS + at)

    def write(at):
        low = max((at - 1) * STEP_ROWS - 1, 0)
        high = ROWS if at == STEPS - 1 else at * STEP_ROWS - 1
        return pltpu.make_async_copy(
            acc.at[:, 1 + low : 1 + high], part_ref.at[:, low:high], sems.at[at - 1]
        )

    for at in range(1, STEPS):
        pl.when(step == at)(lambda: write(at).start())

    @pl.when(step == STEPS - 1)
    def _():
        to_left_ref[...] = sides[:, 1 : ROWS + 1, 0:16].astype(BF)
        to_right_ref[...] = sides[:, 1 : ROWS + 1, 16:32].astype(BF)
        for at in range(1, STEPS):
            write(at).wait()


def backward(taps, mixed_round, mix):
    whole = lambda *shape: pl.BlockSpec(shape, lambda i: (0,) * len(shape))
    side = jax.ShapeDtypeStruct((2, ROWS, 16, 128), BF)
    return pl.pallas_call(
        backward_kernel,
        grid=(STEPS,),
        in_specs=[
            pl.BlockSpec((12, 32, 128), lambda i: (0, 0, 0)),
            pl.BlockSpec((STEP_ROWS, 128, 256), lambda i: (i, 0, 0)),
            whole(128, 4, 128),
        ],
        out_specs=[
            pl.BlockSpec(memory_space=pltpu.MemorySpace.HBM),
            whole(2, ROWS, 16, 128),
            whole(2, ROWS, 16, 128),
        ],
        out_shape=[jax.ShapeDtypeStruct((2, ROWS, 128, 128), F32), side, side],
        scratch_shapes=[
            pltpu.VMEM((2, ROWS + 2, 128, 128), F32),
            pltpu.VMEM((2, ROWS + 2, 32, 128), F32),
            pltpu.VMEM((STEP_ROWS, 512, 512), BF),
            pltpu.VMEM((512, 128), BF),
            pltpu.SemaphoreType.DMA((STEPS - 1,)),
        ],
        compiler_params=pltpu.CompilerParams(vmem_limit_bytes=58 * 1024 * 1024),
        cost_estimate=pl.CostEstimate(
            flops=7_500_000_000, bytes_accessed=8_000_000, transcendentals=0
        ),
    )(taps, mixed_round, mix)


BORDER_ROWS = 8


def border_kernel(part_ref, cot_ref, left_ref, right_ref, out_ref):
    gap = jnp.zeros((96, 128), BF)
    turn = lambda low, high: jnp.concatenate([low, gap, high], axis=0).T.astype(F32)
    for m in range(2):
        for at in range(BORDER_ROWS):
            out_ref[m, at] = (part_ref[m, at] + cot_ref[m, at].astype(F32)) + turn(
                left_ref[m, at], right_ref[m, at]
            )


def add_border(part, cot, left, right):
    rows = lambda *tail: pl.BlockSpec((2, BORDER_ROWS, *tail), lambda i: (0, i, 0, 0))
    return pl.pallas_call(
        border_kernel,
        grid=(ROWS // BORDER_ROWS,),
        in_specs=[
            rows(128, 128),
            rows(128, 128),
            rows(16, 128),
            rows(16, 128),
        ],
        out_specs=rows(128, 128),
        out_shape=jax.ShapeDtypeStruct((2, ROWS, 128, 128), F32),
        compiler_params=pltpu.CompilerParams(vmem_limit_bytes=58 * 1024 * 1024),
        cost_estimate=pl.CostEstimate(flops=1_000_000, bytes_accessed=7_000_000, transcendentals=0),
    )(part, cot, left, right)


def finish_kernel(
    me_ref, own_ref, other_ref, mix_ref, hidden_ref, output_ref, bias_ref, gain_ref, hidden_bias_ref
):
    def place(first_ref, second_ref):
        for p in range(64):
            mix_ref[p * 8 : p * 8 + 8] = first_ref[p * 10 : p * 10 + 8]
            rest = second_ref[p * 10 : p * 10 + 8]
            if p < 32:
                hidden_ref[p * 8 : p * 8 + 8] = rest
            else:
                at, half = (p - 32) % 16, (p - 32) // 16
                output_ref[at * 8 : at * 8 + 8, half * 128 : half * 128 + 128] = rest

    pl.when(me_ref[0] == 0)(lambda: place(own_ref, other_ref))
    pl.when(me_ref[0] == 1)(lambda: place(other_ref, own_ref))
    small = jnp.concatenate([own_ref[p * 10 + 8 : p * 10 + 10] for p in range(64)], axis=0)
    small = small.T
    bias_ref[...] = small[0:1]
    gain_ref[...] = small[1:2]
    hidden_bias_ref[...] = jnp.concatenate([small[2:3], small[3:4]], axis=1)


def finish(me, own, other):
    return pl.pallas_call(
        finish_kernel,
        in_specs=[pl.BlockSpec(memory_space=pltpu.SMEM)]
        + [pl.BlockSpec(memory_space=pltpu.VMEM)] * 2,
        out_shape=[
            jax.ShapeDtypeStruct((512, 128), F32),
            jax.ShapeDtypeStruct((256, 128), F32),
            jax.ShapeDtypeStruct((128, 256), F32),
            jax.ShapeDtypeStruct((1, 128), F32),
            jax.ShapeDtypeStruct((1, 128), F32),
            jax.ShapeDtypeStruct((1, 256), F32),
        ],
        compiler_params=pltpu.CompilerParams(vmem_limit_bytes=24 * 1024 * 1024),
        cost_estimate=pl.CostEstimate(flops=1_000_000, bytes_accessed=1_200_000, transcendentals=0),
    )(me, own, other)


def ring(axis, shift):
    count = lax.axis_size(axis)
    return [(i, (i + shift) % count) for i in range(count)]


def on_device(
    features,
    cotangent,
    basis_table,
    halo_depth,
    mix_weight,
    mix_bias,
    norm_gain,
    hidden_weight,
    hidden_bias,
    output_weight,
):
    to_above, to_below = edges_of(features, cotangent)
    above = lax.ppermute(to_below, "lat", ring("lat", 1))
    below = lax.ppermute(to_above, "lat", ring("lat", -1))
    to_right, to_left = sides_of(features)
    left = lax.ppermute(to_right, "lon", ring("lon", 1))
    right = lax.ppermute(to_left, "lon", ring("lon", -1))
    to_right, to_left = corners_of(above, below)
    corner_left = lax.ppermute(to_right, "lon", ring("lon", 1))
    corner_right = lax.ppermute(to_left, "lon", ring("lon", -1))
    halos = (left, right, corner_left, corner_right, above, below)
    first = (lax.axis_index("lat") * ROWS).reshape(1).astype(jnp.int32)
    taps, columns = prepare(
        first, basis_table, halo_depth, mix_bias, norm_gain, hidden_bias
    )

    me = lax.axis_index("member").reshape(1).astype(jnp.int32)
    cell_total = 2 * ROWS * 128 * lax.axis_size(("member", "lat", "lon"))
    weights = (mix_weight, hidden_weight, output_weight, columns)
    scale = 1.0 / math.sqrt(cell_total)
    mixed_round, keep, send = forward(
        me, taps, features, cotangent, halos, weights, scale
    )
    swap = [(0, 1), (1, 0)]
    band = ("lat", "lon")
    peers = lax.axis_size(band)
    pair = keep + lax.ppermute(send, "member", swap)
    pair, mixed_round = lax.optimization_barrier((pair, mixed_round))
    pieces = lax.all_to_all(pair.reshape(peers, 640 // peers, 1, 128), band, 0, 0)
    part, to_left, to_right = backward(taps, mixed_round, mix_weight)
    add_left = lax.ppermute(to_right, "lon", ring("lon", 1))
    add_right = lax.ppermute(to_left, "lon", ring("lon", -1))
    total, add_left, add_right = lax.optimization_barrier(
        (jnp.sum(pieces, axis=0), add_left, add_right)
    )

    copies = jnp.broadcast_to(total[None], pieces.shape)
    own = lax.all_to_all(copies, band, 0, 0).reshape(640, 128)
    feature_grad = add_border(part, cotangent, add_left, add_right)
    own, feature_grad = lax.optimization_barrier((own, feature_grad))
    other = lax.ppermute(own, "member", swap)
    mix_grad, hidden_grad, output_grad, bias, gain, hidden_bias = finish(me, own, other)
    return (
        feature_grad,
        mix_grad.reshape(128, 4, 128),
        bias.reshape(128),
        gain.reshape(128),
        hidden_grad,
        hidden_bias.reshape(256),
        output_grad,
    )


def solution(mesh):
    cells = P("member", "lat", None, "lon")
    return jax.shard_map(
        on_device,
        mesh=mesh,
        in_specs=(cells, cells) + (P(),) * 8,
        out_specs=(cells,) + (P(),) * 6,
        check_vma=False,
    )
```
